256 devices in a mesh: coarse: 16 (over z, core), fine: 16 (over y, x).
Axes of the slice: x: 4, y: 4, z: 8, core: 2. Of those that a mesh axis runs over, the one named last changes fastest.
Arguments:
- source_term: float32 [256, 256, 256], P('coarse', 'fine'), may hold values from -4 to 10
- conduct_x: float32 [256, 256, 256], P('coarse', 'fine'), may hold values from 0.5 to 4
- conduct_y: float32 [256, 256, 256], P('coarse', 'fine'), may hold values from 0.5 to 4
- conduct_z: float32 [256, 256, 256], P('coarse', 'fine'), may hold values from 0.5 to 4
- absorption: float32 [256, 256, 256], P('coarse', 'fine'), may hold values from 0.05 to 1
- block_active: int32 [16, 16, 16], P('coarse', 'fine'), may hold values 0 or 1
Outputs:
- solution_field: float32 [256, 256, 256], P('coarse', 'fine')
- coarse_correction: float32 [64, 64, 64], P('coarse', 'fine')
The draws below stay inside these ranges and needn't reach their ends.
All inputs are finite; a program needn't handle non-finite values. No bound on the sum of `block_active` on one device may be relied on, other than what follows from the above.
Results may differ from the reference program's by a relative error of at most 0.0003.
Values sent between devices are 32-bit elements; how exact they have to be, the bound alone decides.
No kernel may reach another device: no remote copies, remote signals or barrier semaphores. Data moves between devices by JAX's collectives and lax.ppermute only.
A program may use at most 64 MiB of HBM per device.

```python
import math
import jax
import jax.numpy as jnp
from jax import lax

DEGREE = 3
KRYLOV = 2
NX = 256
NY = 256
NZ = 256


def wave(count, phase):
    steps = jnp.arange(count, dtype=jnp.float32)
    return jnp.cos(2.0 * math.pi / count * steps + phase)


def draw_source_term(key, part):
    key = jax.random.fold_in(key, 11)
    phase_key, level_key, noise_key = jax.random.split(key, 3)
    phases = jax.random.uniform(phase_key, (3,), jnp.float32, -math.pi, math.pi)
    level = jax.random.uniform(level_key, (), jnp.float32, 1.5, 2.5)
    noise = jnp.clip(jax.random.normal(noise_key, (NX, NY, NZ), jnp.float32), -4.0, 4.0)
    first = wave(NX, phases[0])
    second = wave(NY, phases[1])
    third = wave(NZ, phases[2])
    smooth = level * (1.0 + 0.5 * first[:, None, None] * second[None, :, None] * third[None, None, :])
    return (smooth + noise).astype(jnp.float32)


def set_ends(entries, stream_key, low, high):
    shape = entries.shape
    spot = [jax.random.randint(jax.random.fold_in(stream_key, axis), (), 0, shape[axis]) for axis in range(len(shape))]
    entries = entries.at[tuple(spot)].set(low)
    longest = shape.index(max(shape))
    spot[longest] = (spot[longest] + 1) % shape[longest]
    return entries.at[tuple(spot)].set(high)


def levels(stream_key, dims, cuts, least, high):
    factor_of = 1.0
    for dim, shards_of in cuts:
        heights = jax.random.uniform(jax.random.fold_in(jax.random.fold_in(stream_key, 6), dim), (shards_of,), jnp.float32, least / len(cuts), high / len(cuts))
        factor_of = factor_of * jnp.repeat(jnp.exp(heights), dims[dim] // shards_of).reshape((-1,) + (1,) * (len(dims) - 1 - dim))
    return factor_of


def setup_inputs(seed: int = 0) -> dict:
    key_of = jax.random.split(jax.random.key(seed), 7)
    return {
        "source_term": draw_source_term(jax.random.fold_in(key_of[6], 71), 0),
        "conduct_x": jnp.clip(jnp.exp(math.log(4.0) - 2.0794415 * jax.random.uniform(key_of[1], (NX, NY, NZ), jnp.float32) ** levels(key_of[1], (NX, NY, NZ), ((0, 16), (1, 16)), -0.2, 0.2)), 0.5, 4.0),
        "conduct_y": jnp.clip(jnp.exp(math.log(4.0) - 2.0794415 * jax.random.uniform(key_of[2], (NX, NY, NZ), jnp.float32) ** levels(key_of[2], (NX, NY, NZ), ((0, 16), (1, 16)), -0.2, 0.2)), 0.5, 4.0),
        "conduct_z": jnp.clip(jnp.exp(math.log(4.0) - 2.0794415 * jax.random.uniform(key_of[3], (NX, NY, NZ), jnp.float32) ** levels(key_of[3], (NX, NY, NZ), ((0, 16), (1, 16)), -0.2, 0.2)), 0.5, 4.0),
        "absorption": jnp.clip(jnp.exp(math.log(1.0) - 2.9957323 * jax.random.uniform(key_of[4], (NX, NY, NZ), jnp.float32) ** levels(key_of[4], (NX, NY, NZ), ((0, 16), (1, 16)), -0.2, 0.2)), 0.05, 1.0),
        "block_active": set_ends((jax.random.randint(key_of[5], (NX // 16, NY // 16, NZ // 16), 0, 4) < 3).astype(jnp.int32), jax.random.fold_in(key_of[5], 1), 0, 1),
    }


fine_low = 0.25
fine_high = 2.0
coarse_share = 0.125

def extend_plain(values):
    return jnp.pad(values, ((1, 1), (1, 1), (0, 0)))

def total_plain(parts):
    return jnp.sum(parts)

def build_faces(conduct_x, conduct_y, conduct_z, absorption, extend):
    lower_x = extend(conduct_x)[:-2, 1:-1]
    lower_y = extend(conduct_y)[1:-1, :-2]
    lower_z = jnp.pad(conduct_z, ((0, 0), (0, 0), (1, 0)))[:, :, :-1]
    diagonal = conduct_x + lower_x + conduct_y + lower_y + conduct_z + lower_z + absorption
    return (conduct_x, lower_x, conduct_y, lower_y, conduct_z, lower_z, diagonal)

def stencil(padded, values, faces):
    conduct_x, lower_x, conduct_y, lower_y, conduct_z, lower_z, diagonal = faces
    column = jnp.pad(padded, ((0, 0), (0, 0), (1, 1)))
    near = conduct_x * column[2:, 1:-1, 1:-1] + lower_x * column[:-2, 1:-1, 1:-1]
    near = near + conduct_y * column[1:-1, 2:, 1:-1] + lower_y * column[1:-1, :-2, 1:-1]
    near = near + conduct_z * column[1:-1, 1:-1, 2:] + lower_z * column[1:-1, 1:-1, :-2]
    return diagonal * values - near

def chebyshev(iterate, residual, apply, inverse, lower, upper, last_residual):
    center = 0.5 * (upper + lower)
    radius = 0.5 * (upper - lower)
    aspect = center / radius
    factor = 1.0 / aspect
    update = inverse * residual / center
    for step in range(DEGREE):
        if step > 0:
            new_factor = 1.0 / (2.0 * aspect - factor)
            update = new_factor * factor * update + 2.0 * new_factor / radius * inverse * residual
            factor = new_factor
        iterate = iterate + update
        if step < DEGREE - 1 or last_residual:
            residual = residual - apply(update)
    return (iterate, residual)

def blocks(values):
    first, second, third = values.shape
    return values.reshape(first // 4, 4, second // 4, 4, third // 4, 4)

def coarsen(conduct_x, conduct_y, conduct_z, absorption):
    coarse_x = lax.optimization_barrier(jnp.sum(blocks(conduct_x)[:, 3], axis=(2, 4)))
    coarse_y = lax.optimization_barrier(jnp.sum(blocks(conduct_y)[:, :, :, 3], axis=(1, 4)))
    coarse_z = lax.optimization_barrier(jnp.sum(blocks(conduct_z)[:, :, :, :, :, 3], axis=(1, 3)))
    coarse_a = lax.optimization_barrier(jnp.sum(blocks(absorption), axis=(1, 3, 5)))
    return (coarse_x, coarse_y, coarse_z, coarse_a)

def expand(block_active):
    field = block_active.astype(jnp.float32)
    field = jnp.repeat(field, 4, axis=0)
    field = jnp.repeat(field, 4, axis=1)
    return jnp.repeat(field, 4, axis=2)

def prolong(correction):
    first, second, third = correction.shape
    spread = jnp.broadcast_to(correction[:, None, :, None, :, None], (first, 4, second, 4, third, 4))
    return spread.reshape(first * 4, second * 4, third * 4)

def lanczos_bound(start, scale, apply, total):
    basis = start / jnp.sqrt(total(jnp.sum(start * start)))
    basis_prev = jnp.zeros_like(start)
    off_prev = jnp.float32(0.0)
    diag_terms = []
    off_terms = []
    for step in range(KRYLOV):
        image = scale * apply(scale * basis)
        diag_term = total(jnp.sum(basis * image))
        diag_terms.append(diag_term)
        if step < KRYLOV - 1:
            image = image - diag_term * basis - off_prev * basis_prev
            off_term = jnp.sqrt(total(jnp.sum(image * image)))
            off_terms.append(off_term)
            basis_prev = basis
            basis = image / off_term
            off_prev = off_term
    bound = diag_terms[0]
    for step in range(KRYLOV):
        row = diag_terms[step]
        if step > 0:
            row = row + off_terms[step - 1]
        if step < KRYLOV - 1:
            row = row + off_terms[step]
        bound = row if step == 0 else jnp.maximum(bound, row)
    return bound

def coarse_solve(coarse_rhs, coarse_x, coarse_y, coarse_z, coarse_a, mask_field, extend, total):
    faces = build_faces(coarse_x, coarse_y, coarse_z, coarse_a, extend)
    diagonal = faces[6]

    def masked_apply(values):
        return mask_field * stencil(extend(values), values, faces)
    start_rhs = mask_field * coarse_rhs
    scale = 1.0 / jnp.sqrt(diagonal)
    bound = lanczos_bound(scale * start_rhs, scale, masked_apply, total)
    correction, unused = chebyshev(jnp.zeros_like(start_rhs), start_rhs, masked_apply, 1.0 / diagonal, coarse_share * bound, bound, False)
    return correction

def reference(source_term, conduct_x, conduct_y, conduct_z, absorption, block_active):
    faces = build_faces(conduct_x, conduct_y, conduct_z, absorption, extend_plain)
    inverse = 1.0 / faces[6]

    def fine_apply(values):
        return stencil(extend_plain(values), values, faces)
    iterate, residual = chebyshev(jnp.zeros_like(source_term), source_term, fine_apply, inverse, fine_low, fine_high, True)
    coarse_rhs = lax.optimization_barrier(jnp.sum(blocks(residual), axis=(1, 3, 5)))
    coarse_x, coarse_y, coarse_z, coarse_a = coarsen(conduct_x, conduct_y, conduct_z, absorption)
    mask_field = expand(block_active)
    correction = coarse_solve(coarse_rhs, coarse_x, coarse_y, coarse_z, coarse_a, mask_field, extend_plain, total_plain)
    lifted = prolong(correction)
    iterate = iterate + lifted
    residual = residual - fine_apply(lifted)
    iterate, residual = chebyshev(iterate, residual, fine_apply, inverse, fine_low, fine_high, False)
    return (iterate, correction)
```

```python
import functools

import jax
import jax.numpy as jnp
from jax import lax
from jax.experimental import pallas as pl
from jax.experimental.pallas import tpu as pltpu
from jax.sharding import PartitionSpec as P

f32 = jnp.float32
fine_low = 0.25
fine_high = 2.0
coarse_share = 0.125
SIDE = 16
LONG = 256
ROWS = SIDE + 6
RING = 24
HIGH = lax.Precision.HIGHEST
VMEM = pl.BlockSpec(memory_space=pltpu.VMEM)
SMEM = pl.BlockSpec(memory_space=pltpu.SMEM)
LIMIT = 48 * 1024 * 1024


def factors(lower, upper):
    center = 0.5 * (upper + lower)
    radius = 0.5 * (upper - lower)
    aspect = center / radius
    p0 = 1.0 / aspect
    p1 = 1.0 / (2.0 * aspect - p0)
    p2 = 1.0 / (2.0 * aspect - p1)
    return center, p1 * p0, 2.0 * p1 / radius, p2 * p1, 2.0 * p2 / radius


FINE = factors(fine_low, fine_high)


def iota(shape, axis):
    return lax.broadcasted_iota(jnp.int32, shape, axis)


def back(values, axis):
    return pltpu.roll(values, 1, axis)


def ahead(values, axis):
    return pltpu.roll(values, values.shape[axis] - 1, axis)


def call(kernel, outs, scratch=(), ins=None):
    return pl.pallas_call(
        kernel,
        out_shape=[jax.ShapeDtypeStruct(s, f32) for s in outs],
        in_specs=ins,
        out_specs=[VMEM] * len(outs),
        scratch_shapes=list(scratch),
        compiler_params=pltpu.CompilerParams(vmem_limit_bytes=LIMIT),
    )


def pack_first(*refs):
    lows, highs, (up, down) = refs[:5], refs[5:10], refs[10:]
    at = 0
    for field in range(5):
        first = 0 if field == 1 else 1
        up[at : at + 4 - first] = highs[field][first:]
        at += 4 - first
        down[3 * field : 3 * field + 3] = lows[field][:3]


def pack_first_call(fields):
    low = pl.BlockSpec((4, SIDE, LONG), lambda i: (0, 0, 0))
    high = pl.BlockSpec((4, SIDE, LONG), lambda i: (3, 0, 0))
    return pl.pallas_call(
        pack_first,
        grid=(1,),
        out_shape=[jax.ShapeDtypeStruct((n, SIDE, LONG), f32) for n in (16, 15)],
        in_specs=[low] * 5 + [high] * 5,
        out_specs=[pl.BlockSpec((n, SIDE, LONG), lambda i: (0, 0, 0)) for n in (16, 15)],
    )(*fields, *fields)


UP_AT = (0, 4, 7, 10, 13)


def sum_lanes(last_only):
    cell, lane = iota((LONG, 128), 0), iota((LONG, 128), 1)
    hit = (cell // 4 == lane) & (cell >= 0)
    if last_only:
        hit = hit & (cell % 4 == 3)
    return hit.astype(f32)


def sum_rows(last_only, rows=SIDE):
    block, cell = iota((8, rows), 0), iota((8, rows), 1)
    hit = (cell // 4 == block) & (cell < SIDE)
    if last_only:
        hit = hit & (cell % 4 == 3)
    return hit.astype(f32)


def dot(a, b):
    return jnp.dot(a, b, precision=HIGH, preferred_element_type=f32)


def coarsen(cx, cy, cz, ab, out):
    lanes, last = sum_lanes(False), sum_lanes(True)
    rows, lastrow = sum_rows(False), sum_rows(True)
    for a in range(4):
        part = lambda ref: ref[4 * a] + ref[4 * a + 1] + ref[4 * a + 2] + ref[4 * a + 3]
        out[0, a] = dot(rows, dot(cx[4 * a + 3], lanes))
        out[1, a] = dot(lastrow, dot(part(cy), lanes))
        out[2, a] = dot(rows, dot(part(cz), last))
        out[3, a] = dot(rows, dot(part(ab), lanes))


def pack_second(flags, src, cx, cy, cz, ab, low, high, diag, top, bottom):
    center = FINE[0]
    row, lane = iota((SIDE, LONG), 0), iota((SIDE, LONG), 1)

    def build(i, src_i, cx_i, cxl_i, cy_i, cz_i, ab_i, inside, dst, at):
        g = cx_i + cxl_i + cy_i + cz_i + ab_i
        g = g + jnp.where(row == 0, 0.0, back(cy_i, 0))
        g = g + jnp.where(lane == 0, 0.0, back(cz_i, 1))
        diag[i] = g
        start = jnp.where(inside, src_i / (center * g), 0.0)
        pieces = (src_i, cx_i, cy_i, cz_i, g)
        top[dst, pl.ds(at, 12)] = jnp.concatenate(
            [p[14:16] for p in pieces] + [start[13:14], cy_i[13:14]], axis=0
        )
        bottom[dst, pl.ds(at, 12)] = jnp.concatenate(
            [p[0:2] for p in pieces] + [start[2:3], start[2:3]], axis=0
        )

    has_low, has_high = flags[0] > 0, flags[1] > 0
    keep_low, keep_high = has_low.astype(f32), has_high.astype(f32)
    for k in range(3):
        f = [low[UP_AT[n] + k] * keep_low for n in range(5)]
        before = low[3 + k] * keep_low
        build(k, f[0], f[1], before, f[2], f[3], f[4], has_low, k, 0)
    ins = (src, cx, cy, cz, ab)

    def own(x, before, at, shift):
        f = [ref[x] for ref in ins]
        build(x + 3, f[0], f[1], before, f[2], f[3], f[4], True, x + 3 - shift, at)

    own(0, low[6] * keep_low, 0, 0)

    @pl.loop(1, 8)
    def _(x):
        own(x, cx[x - 1], 0, 0)

    @pl.loop(8, SIDE)
    def _(x):
        own(x, cx[x - 1], 12, 11)

    for k in range(3):
        f = [high[3 * n + k] * keep_high for n in range(5)]
        before = cx[15] if k == 0 else high[3 + k - 1] * keep_high
        build(19 + k, f[0], f[1], before, f[2], f[3], f[4], has_high, 8 + k, 12)


def near(i, u, cx, cy, cz):
    here = u[i]
    cy_i, cz_i = cy[i], cz[i]
    total = cx[i] * u[i + 1] + cx[i - 1] * u[i - 1]
    total = total + (cy_i * ahead(here, 0) + back(cy_i * here, 0))
    return total + (cz_i * ahead(here, 1) + back(cz_i * here, 1))


def presmooth(
    flags, src, cx, cy, cz, low, high, diag, ylow, yhigh, coarse, active,
    cx_o, cy_o, cz_o, g_o, inv_o, resid, iterate, packed, weight, up, down,
    u0, u1, r0,
):
    center, m1, q1, m2, q2 = FINE
    row, lane = iota((RING, LONG), 0), iota((RING, LONG), 1)
    has_low, has_high = flags[0] > 0, flags[1] > 0
    keep_low, keep_high = has_low.astype(f32), has_high.astype(f32)
    has_left, has_right = flags[2] > 0, flags[3] > 0
    keep_left, keep_right = has_left.astype(f32), has_right.astype(f32)
    inside_y = (row < 16) | ((row < 18) & has_right) | ((row >= 22) & has_left)
    last = lane == LONG - 1
    edge = (row == 0) | (row == 16)
    none1 = jnp.zeros((1, LONG), f32)
    none4 = jnp.zeros((4, LONG), f32)

    def build(i, src_i, cx_i, cy_i, cz_i, at, shift, inside):
        lo = ylow[i - shift, pl.ds(at, 12)] * keep_left
        hi = yhigh[i - shift, pl.ds(at, 12)] * keep_right

        def ring(own, n):
            return jnp.concatenate([own, hi[2 * n : 2 * n + 2], none4, lo[2 * n : 2 * n + 2]], axis=0)

        src_r, cx_r, cz_r, g = ring(src_i, 0), ring(cx_i, 1), ring(cz_i, 3), ring(diag[i], 4)
        cy_r = jnp.concatenate([cy_i, hi[4:6], none1, none1, none1, lo[11:12], lo[4:6]], axis=0)
        g = g + jnp.where(edge, back(cy_r, 0), 0.0)
        inv = jnp.where(inside_y & inside, 1.0 / g, 0.0)
        cx_o[i] = cx_r
        cy_o[i] = cy_r
        cz_o[i] = jnp.where(last, 0.0, cz_r)
        g_o[i] = g
        inv_o[i] = inv
        r0[i] = src_r
        u = src_r * inv * (1.0 / center)
        u = jnp.where(row == 18, hi[10:11], u)
        u0[i] = jnp.where(row == 21, lo[10:11], u)

    for k in range(3):
        f = [low[UP_AT[n] + k] * keep_low for n in range(4)]
        build(k, *f, 0, 0, has_low)

    @pl.loop(0, 8)
    def _(x):
        build(x + 3, src[x], cx[x], cy[x], cz[x], 0, 0, True)

    @pl.loop(8, SIDE)
    def _(x):
        build(x + 3, src[x], cx[x], cy[x], cz[x], 12, 11, True)

    for k in range(3):
        f = [high[3 * n + k] * keep_high for n in range(4)]
        build(19 + k, *f, 12, 11, has_high)

    @pl.loop(1, ROWS - 1)
    def _(i):
        u = u0[i]
        r = r0[i] - (g_o[i] * u - near(i, u0, cx_o, cy_o, cz_o))
        r0[i] = r
        u1[i] = m1 * u + q1 * (inv_o[i] * r)

    u2 = iterate_scratch = u0

    @pl.loop(3, 19)
    def _(i):
        iterate[i - 3] = u0[i, pl.ds(0, SIDE)] + u1[i, pl.ds(0, SIDE)]

    @pl.loop(2, ROWS - 2)
    def _(i):
        u = u1[i]
        r = r0[i] - (g_o[i] * u - near(i, u1, cx_o, cy_o, cz_o))
        r0[i] = r
        u2[i] = m2 * u + q2 * (inv_o[i] * r)

    @pl.loop(3, 19)
    def _(i):
        u = u2[i]
        r = r0[i] - (g_o[i] * u - near(i, u2, cx_o, cy_o, cz_o))
        resid[i - 3] = r[:SIDE]
        iterate[i - 3] = iterate[i - 3] + u[:SIDE]

    lanes = sum_lanes(False)
    rows = sum_rows(False)
    crow, clane = iota((8, 128), 0), iota((8, 128), 1)
    own = (crow < 4) & (clane < 64)
    spread = ((iota((16, 128), 1) // 4) == iota((16, 128), 0)).astype(f32)
    mask = dot(jnp.broadcast_to(active[0].astype(f32), (8, 16)), spread)
    below_x = dot(rows, dot(cx_o[2, pl.ds(0, SIDE)], lanes))
    for a in range(4):
        at = 4 * a
        total = resid[at] + resid[at + 1] + resid[at + 2] + resid[at + 3]
        rhs = dot(rows, dot(total, lanes))
        tail = sum(cy_o[at + 3 + k, pl.ds(SIDE, 8)] for k in range(4))
        below_y = back(dot(tail, lanes), 0)
        cx_c, cy_c, cz_c, ab_c = (coarse[n, a] for n in range(4))
        g = cx_c + cy_c + cz_c + ab_c + back(cz_c, 1)
        g = g + (below_x if a == 0 else coarse[0, a - 1])
        g = g + jnp.where(crow == 0, below_y, back(cy_c, 0))
        g = jnp.where(own, g, 0.0)
        inv = jnp.where(own, mask / jnp.where(own, g, 1.0), 0.0)
        z = inv * rhs
        weight[a] = g
        cz_c = jnp.where(clane == 63, 0.0, cz_c)
        first = z + pltpu.roll(inv, 64, 1)
        second = cx_c + pltpu.roll(cy_c, 64, 1)
        packed[a, 0] = first + pltpu.roll(second, 4, 0)
        packed[a, 1] = cz_c

    for k in range(2):
        for n in range(4):
            ys, zs = pl.ds(8 * (n // 2), 8), pl.ds(128 * (n % 2), 128)
            up[4 * k + n] = resid[14 + k, ys, zs]
            down[4 * k + n] = resid[k, ys, zs]
    for k in range(3):
        for n in range(2):
            up[8 + 2 * k + n] = packed[1 + k, n]
            down[8 + 2 * k + n] = packed[k, n]


def pack_third(flags, resid, packed, low, high, top, bottom):
    keep_low, keep_high = (flags[0] > 0).astype(f32), (flags[1] > 0).astype(f32)

    def edges(x):
        if x < 0 or x >= SIDE:
            ref, keep, k = (low, keep_low, x + 2) if x < 0 else (high, keep_high, x - SIDE)
            halves = [[ref[4 * k + 2 * h + c] * keep for c in range(2)] for h in range(2)]
            return [half[0:2] for half in halves[0]], [half[6:8] for half in halves[1]]
        first = [resid[x, 0:2, 128 * c : 128 * c + 128] for c in range(2)]
        return first, [resid[x, 14:16, 128 * c : 128 * c + 128] for c in range(2)]

    for n in range(5):
        parts = [edges(4 * n - 2 + k) for k in range(4)]
        for c in range(2):
            bottom[2 * n + c] = jnp.concatenate([p[0][c] for p in parts], axis=0)
            top[2 * n + c] = jnp.concatenate([p[1][c] for p in parts], axis=0)
    for a in range(10):
        for n in range(2):
            if a < 3:
                tile = low[8 + 2 * a + n] * keep_low
            elif a < 7:
                tile = packed[a - 3, n]
            else:
                tile = high[8 + 2 * (a - 7) + n] * keep_high
            top[10 + 2 * a + n] = tile
            bottom[10 + 2 * a + n] = tile


def krylov(flags, packed, weight, low, high, left, right, basis, message, ext, t1s):
    keep_low, keep_high = (flags[0] > 0).astype(f32), (flags[1] > 0).astype(f32)
    keep_left, keep_right = (flags[2] > 0).astype(f32), (flags[3] > 0).astype(f32)
    crow, clane = iota((8, 128), 0), iota((8, 128), 1)
    own = (crow < 4) & (clane < 64)

    def unpack(tiles):
        first, second = tiles
        turned = pltpu.roll(first, 4, 0)
        five = (first, pltpu.roll(first, 64, 1), turned, pltpu.roll(turned, 64, 1), second)
        return [jnp.where(own, v, 0.0) for v in five]

    for a in range(10):
        if a < 3:
            here = [low[8 + 2 * a + n] * keep_low for n in range(2)]
        elif a < 7:
            here = [packed[a - 3, n] for n in range(2)]
        else:
            here = [high[8 + 2 * (a - 7) + n] * keep_high for n in range(2)]
        here = unpack(here)
        before = unpack([left[10 + 2 * a + n] * keep_left for n in range(2)])
        after = unpack([right[10 + 2 * a + n] * keep_right for n in range(2)])
        for n in range(5):
            ext[n, a, 0:8] = here[n] + pltpu.roll(after[n], 4, 0)
            ext[n, a, 8:16] = pltpu.roll(before[n], 4, 0)

    z, inv, cx, cy, cz = (ext.at[n] for n in range(5))
    for a in range(1, 9):
        t1s[a] = z[a] - inv[a] * near(a, z, cx, cy, cz)
    for a in range(2, 8):
        t1 = t1s[a]
        basis[0, a - 2] = z[a]
        basis[1, a - 2] = t1
        basis[2, a - 2] = t1 - inv[a] * near(a, t1s, cx, cy, cz)

    def total(parts):
        return jnp.sum(sum(parts), keepdims=True)

    g = [weight[a] for a in range(4)]
    v0, v1, v2 = ([basis[n, a + 1, 0:8] for a in range(4)] for n in range(3))
    s00 = total([w * p * p for w, p in zip(g, v0)])
    s01 = total([w * p * q for w, p, q in zip(g, v0, v1)])
    alpha = jnp.where(s00 > 0, s01 / jnp.where(s00 > 0, s00, 1.0), 0.0)
    e = [q - alpha * p for p, q in zip(v0, v1)]
    te = [q - alpha * p for p, q in zip(v1, v2)]
    terms = [
        s00,
        s01,
        alpha,
        total([w * p * p for w, p in zip(g, e)]),
        total([w * p * q for w, p, q in zip(g, e, v0)]),
        total([w * p * q for w, p, q in zip(g, e, te)]),
        total([w * p * q for w, p, q in zip(g, v0, te)]),
        total([w * p * q for w, p, q in zip(g, e, v1)]),
    ]
    lane = iota((256, 128), 1)
    line = jnp.zeros((256, 128), f32)
    for n, term in enumerate(terms):
        line = jnp.where(lane == n, term, line)
    message[...] = line


def finish(
    flags, gathered, basis, cx, cy, cz, g, inv, resid, iterate, low, high, left, right,
    out, correction, lift, u0, u1, r0,
):
    center, m1, q1, m2, q2 = FINE
    keep_low, keep_high = (flags[0] > 0).astype(f32), (flags[1] > 0).astype(f32)
    keep_left, keep_right = (flags[2] > 0).astype(f32), (flags[3] > 0).astype(f32)
    col = [gathered[:, n : n + 1] for n in range(8)]
    s00, s01, alpha, ee, ez, ete, zte, et1 = col

    def total(v):
        return jnp.sum(v, axis=0, keepdims=True)

    norm = total(s00)
    a1 = total(s01) / norm
    shift = alpha - a1
    square = total(ee + shift * (2.0 * ez + shift * s00))
    energy = total(ete + shift * (zte + et1 + shift * s01))
    b1 = jnp.sqrt(square / norm)
    a2 = energy / square
    bound = jnp.maximum(a1 + b1, a2 + b1)
    middle, k1, h1, k2, h2 = factors(coarse_share * bound, bound)
    v0 = 1.0 / middle
    v1 = (k1 * v0 + h1, -h1 * v0)
    v2 = (k2 * v1[0] + h2, k2 * v1[1] - h2 * (v0 + v1[0]), -h2 * v1[1])
    weights = (v0 + v1[0] + v2[0], v1[1] + v2[1], v2[2])

    fine_row, coarse_row = iota((RING, 16), 0), iota((RING, 16), 1)
    source = jnp.where(fine_row < 20, fine_row // 4, 15)
    rows = (source == coarse_row).astype(f32)
    lanes = (iota((128, LONG), 1) // 4 == iota((128, LONG), 0)).astype(f32)
    for a in range(6):
        field = weights[0] * basis[0, a] + weights[1] * basis[1, a] + weights[2] * basis[2, a]
        if 1 <= a <= 4:
            correction[a - 1] = field[0:4, 0:64]
        fine = dot(rows, dot(field, lanes))
        for k in range(4):
            x = 4 * a - 4 + k + 3
            if 0 <= x < ROWS:
                lift[x] = fine

    none4 = jnp.zeros((4, LONG), f32)

    def strip(ref, x, keep):
        n, k = x // 4, x % 4
        return jnp.concatenate([ref[2 * n + c, 2 * k : 2 * k + 2] for c in range(2)], axis=1) * keep

    for x in range(20):
        if x < 2 or x >= 18:
            ref, keep, k = (low, keep_low, x) if x < 2 else (high, keep_high, x - 18)
            halves = [
                jnp.concatenate([ref[4 * k + 2 * h + c] for c in range(2)], axis=1) for h in range(2)
            ]
            mine = jnp.concatenate(halves, axis=0) * keep
        else:
            mine = resid[x - 2]
        after, before = strip(right, x, keep_right), strip(left, x, keep_left)
        r0[x + 1] = jnp.concatenate([mine, after, none4, before], axis=0)

    @pl.loop(1, ROWS - 1)
    def _(i):
        r = r0[i] - (g[i] * lift[i] - near(i, lift, cx, cy, cz))
        r0[i] = r
        u0[i] = inv[i] * r * (1.0 / center)

    @pl.loop(2, ROWS - 2)
    def _(i):
        u = u0[i]
        r = r0[i] - (g[i] * u - near(i, u0, cx, cy, cz))
        r0[i] = r
        u1[i] = m1 * u + q1 * (inv[i] * r)

    @pl.loop(3, 19)
    def _(i):
        u = u1[i]
        r = r0[i] - (g[i] * u - near(i, u1, cx, cy, cz))
        step = (u0[i] + u) + (m2 * u + q2 * (inv[i] * r)) + lift[i]
        out[i - 3] = iterate[i - 3] + step[:SIDE]


def shift(values, axis, by):
    count = lax.axis_size(axis)
    return lax.ppermute(values, axis, [(i, (i + by) % count) for i in range(count)])


def body(src, cx, cy, cz, ab, active):
    ix, iy = lax.axis_index("coarse"), lax.axis_index("fine")
    nx, ny = lax.axis_size("coarse"), lax.axis_size("fine")
    flags = jnp.stack([ix > 0, ix < nx - 1, iy > 0, iy < ny - 1]).astype(jnp.int32)
    block, ring = (SIDE, SIDE, LONG), pltpu.VMEM((ROWS, RING, LONG), f32)
    rings = (ROWS, RING, LONG)

    up, down = pack_first_call((src, cx, cy, cz, ab))
    low, high = shift(up, "coarse", 1), shift(down, "coarse", -1)
    (coarse,) = call(coarsen, [(4, 4, 8, 128)], ins=[VMEM] * 4)(cx, cy, cz, ab)
    diag, top, bottom = call(
        pack_second,
        [(ROWS, SIDE, LONG), (11, 24, LONG), (11, 24, LONG)],
        ins=[SMEM] + [VMEM] * 7,
    )(flags, src, cx, cy, cz, ab, low, high)
    left, right = shift(top, "fine", 1), shift(bottom, "fine", -1)
    cx_r, cy_r, cz_r, g, inv, resid, iterate, packed, weight, up, down = call(
        presmooth,
        [rings] * 5 + [block, block, (4, 2, 8, 128), (4, 8, 128), (14, 8, 128), (14, 8, 128)],
        [ring] * 3,
        ins=[SMEM] + [VMEM] * 11,
    )(flags, src, cx, cy, cz, low, high, diag, left, right, coarse, active)
    low, high = shift(up, "coarse", 1), shift(down, "coarse", -1)
    top, bottom = call(pack_third, [(30, 8, 128)] * 2, ins=[SMEM] + [VMEM] * 4)(
        flags, resid, packed, low, high
    )
    left, right = shift(top, "fine", 1), shift(bottom, "fine", -1)
    count = nx * ny
    basis, message = call(
        functools.partial(krylov),
        [(3, 6, 16, 128), (256, 128)],
        [pltpu.VMEM((5, 10, 16, 128), f32), pltpu.VMEM((10, 16, 128), f32)],
        ins=[SMEM] + [VMEM] * 6,
    )(flags, packed, weight, low, high, left, right)
    gathered = lax.all_to_all(message[:count], ("coarse", "fine"), 0, 0, tiled=True)
    out, correction = call(
        finish,
        [block, (4, 4, 64)],
        [ring] * 4,
        ins=[SMEM] + [VMEM] * 13,
    )(flags, gathered, basis, cx_r, cy_r, cz_r, g, inv, resid, iterate, low, high, left, right)
    return (out, correction)


def solution(mesh):
    spec = P("coarse", "fine", None)
    return jax.shard_map(
        body, mesh=mesh, in_specs=(spec,) * 6, out_specs=(spec,) * 2, check_vma=False
    )
```

```python
import functools

import jax
import jax.numpy as jnp
from jax import lax
from jax.experimental import pallas as pl
from jax.experimental.pallas import tpu as pltpu
from jax.sharding import PartitionSpec as P

f32 = jnp.float32
fine_low = 0.25
fine_high = 2.0
coarse_share = 0.125
SIDE = 16
LONG = 256
ROWS = SIDE + 6
RING = 24
HIGH = lax.Precision.HIGHEST
VMEM = pl.BlockSpec(memory_space=pltpu.VMEM)
SMEM = pl.BlockSpec(memory_space=pltpu.SMEM)
LIMIT = 48 * 1024 * 1024


def factors(lower, upper):
    center = 0.5 * (upper + lower)
    radius = 0.5 * (upper - lower)
    aspect = center / radius
    p0 = 1.0 / aspect
    p1 = 1.0 / (2.0 * aspect - p0)
    p2 = 1.0 / (2.0 * aspect - p1)
    return center, p1 * p0, 2.0 * p1 / radius, p2 * p1, 2.0 * p2 / radius


FINE = factors(fine_low, fine_high)


def iota(shape, axis):
    return lax.broadcasted_iota(jnp.int32, shape, axis)


def back(values, axis):
    return pltpu.roll(values, 1, axis)


def ahead(values, axis):
    return pltpu.roll(values, values.shape[axis] - 1, axis)


def call(kernel, outs, scratch=(), ins=None):
    return pl.pallas_call(
        kernel,
        out_shape=[jax.ShapeDtypeStruct(s, f32) for s in outs],
        in_specs=ins,
        out_specs=[VMEM] * len(outs),
        scratch_shapes=list(scratch),
        compiler_params=pltpu.CompilerParams(vmem_limit_bytes=LIMIT),
    )


def pack_first(*refs):
    fields, (up, down), sems = refs[:5], refs[5:7], refs[7]
    copies = []
    for n, field in enumerate(fields):
        first = 12 if n == 1 else 13
        at = UP_AT[n] + first - 13
        copies.append((field.at[first:16], up.at[at : at + 16 - first]))
        copies.append((field.at[0:3], down.at[3 * n : 3 * n + 3]))
    copies = [pltpu.make_async_copy(a, b, sems.at[k]) for k, (a, b) in enumerate(copies)]
    for copy in copies:
        copy.start()
    for copy in copies:
        copy.wait()


UP_AT = (0, 4, 7, 10, 13)


def sum_lanes(last_only):
    cell, lane = iota((LONG, 128), 0), iota((LONG, 128), 1)
    hit = (cell // 4 == lane) & (cell >= 0)
    if last_only:
        hit = hit & (cell % 4 == 3)
    return hit.astype(f32)


def sum_rows(last_only, rows=SIDE):
    block, cell = iota((8, rows), 0), iota((8, rows), 1)
    hit = (cell // 4 == block) & (cell < SIDE)
    if last_only:
        hit = hit & (cell % 4 == 3)
    return hit.astype(f32)


def dot(a, b):
    return jnp.dot(a, b, precision=HIGH, preferred_element_type=f32)


def coarsen(cx, cy, cz, ab, out):
    lanes, last = sum_lanes(False), sum_lanes(True)
    rows, lastrow = sum_rows(False), sum_rows(True)
    for a in range(4):
        part = lambda ref: ref[4 * a] + ref[4 * a + 1] + ref[4 * a + 2] + ref[4 * a + 3]
        out[0, a] = dot(rows, dot(cx[4 * a + 3], lanes))
        out[1, a] = dot(lastrow, dot(part(cy), lanes))
        out[2, a] = dot(rows, dot(part(cz), last))
        out[3, a] = dot(rows, dot(part(ab), lanes))


def pack_second(flags, src, cx, cy, cz, ab, low, high, diag, first, second):
    even = flags[4] > 0
    center = FINE[0]
    row, lane = iota((SIDE, LONG), 0), iota((SIDE, LONG), 1)

    def build(i, src_i, cx_i, cxl_i, cy_i, cz_i, ab_i, inside, dst, at):
        g = cx_i + cxl_i + cy_i + cz_i + ab_i
        g = g + jnp.where(row == 0, 0.0, back(cy_i, 0))
        g = g + jnp.where(lane == 0, 0.0, back(cz_i, 1))
        diag[i] = g
        start = jnp.where(inside, src_i / (center * g), 0.0)
        pieces = (src_i, cx_i, cy_i, cz_i, g)
        top = jnp.concatenate(
            [p[14:16] for p in pieces] + [start[13:14], cy_i[13:14]], axis=0
        )
        bottom = jnp.concatenate(
            [p[0:2] for p in pieces] + [start[2:3], start[2:3]], axis=0
        )
        first[dst, pl.ds(at, 12)] = jnp.where(even, top, bottom)
        second[dst, pl.ds(at, 12)] = jnp.where(even, bottom, top)

    has_low, has_high = flags[0] > 0, flags[1] > 0
    keep_low, keep_high = has_low.astype(f32), has_high.astype(f32)
    for k in range(3):
        f = [low[UP_AT[n] + k] * keep_low for n in range(5)]
        before = low[3 + k] * keep_low
        build(k, f[0], f[1], before, f[2], f[3], f[4], has_low, k, 0)
    ins = (src, cx, cy, cz, ab)

    def own(x, before, at, shift):
        f = [ref[x] for ref in ins]
        build(x + 3, f[0], f[1], before, f[2], f[3], f[4], True, x + 3 - shift, at)

    own(0, low[6] * keep_low, 0, 0)

    @pl.loop(1, 8, unroll=True)
    def _(x):
        own(x, cx[x - 1], 0, 0)

    @pl.loop(8, SIDE, unroll=True)
    def _(x):
        own(x, cx[x - 1], 12, 11)

    for k in range(3):
        f = [high[3 * n + k] * keep_high for n in range(5)]
        before = cx[15] if k == 0 else high[3 + k - 1] * keep_high
        build(19 + k, f[0], f[1], before, f[2], f[3], f[4], has_high, 8 + k, 12)


def near(i, u, cx, cy, cz):
    here = u[i]
    cy_i, cz_i = cy[i], cz[i]
    total = cx[i] * u[i + 1] + cx[i - 1] * u[i - 1]
    total = total + (cy_i * ahead(here, 0) + back(cy_i * here, 0))
    return total + (cz_i * ahead(here, 1) + back(cz_i * here, 1))


def presmooth(
    flags, src, cx, cy, cz, low, high, diag, first, second, coarse, active,
    cx_o, cy_o, cz_o, g_o, inv_o, resid, iterate, packed, weight, up, down,
    u0, u1, r0,
):
    center, m1, q1, m2, q2 = FINE
    row, lane = iota((RING, LONG), 0), iota((RING, LONG), 1)
    has_low, has_high = flags[0] > 0, flags[1] > 0
    keep_low, keep_high = has_low.astype(f32), has_high.astype(f32)
    has_left, has_right, even = flags[2] > 0, flags[3] > 0, flags[4] > 0
    keep_left, keep_right = has_left.astype(f32), has_right.astype(f32)
    inside_y = (row < 16) | ((row < 18) & has_right) | ((row >= 22) & has_left)
    last = lane == LONG - 1
    edge = (row == 0) | (row == 16)
    none1 = jnp.zeros((1, LONG), f32)
    none4 = jnp.zeros((4, LONG), f32)

    def build(i, src_i, cx_i, cy_i, cz_i, at, shift, inside):
        one, two = first[i - shift, pl.ds(at, 12)], second[i - shift, pl.ds(at, 12)]
        lo = jnp.where(even, two, one) * keep_left
        hi = jnp.where(even, one, two) * keep_right

        def ring(own, n):
            return jnp.concatenate([own, hi[2 * n : 2 * n + 2], none4, lo[2 * n : 2 * n + 2]], axis=0)

        src_r, cx_r, cz_r, g = ring(src_i, 0), ring(cx_i, 1), ring(cz_i, 3), ring(diag[i], 4)
        cy_r = jnp.concatenate([cy_i, hi[4:6], none1, none1, none1, lo[11:12], lo[4:6]], axis=0)
        g = g + jnp.where(edge, back(cy_r, 0), 0.0)
        inv = jnp.where(inside_y & inside, 1.0 / g, 0.0)
        cx_o[i] = cx_r
        cy_o[i] = cy_r
        cz_o[i] = jnp.where(last, 0.0, cz_r)
        g_o[i] = g
        inv_o[i] = inv
        r0[i] = src_r
        u = src_r * inv * (1.0 / center)
        u = jnp.where(row == 18, hi[10:11], u)
        u0[i] = jnp.where(row == 21, lo[10:11], u)

    for k in range(3):
        f = [low[UP_AT[n] + k] * keep_low for n in range(4)]
        build(k, *f, 0, 0, has_low)

    @pl.loop(0, 8, unroll=True)
    def _(x):
        build(x + 3, src[x], cx[x], cy[x], cz[x], 0, 0, True)

    @pl.loop(8, SIDE, unroll=True)
    def _(x):
        build(x + 3, src[x], cx[x], cy[x], cz[x], 12, 11, True)

    for k in range(3):
        f = [high[3 * n + k] * keep_high for n in range(4)]
        build(19 + k, *f, 12, 11, has_high)

    @pl.loop(1, ROWS - 1, unroll=True)
    def _(i):
        u = u0[i]
        r = r0[i] - (g_o[i] * u - near(i, u0, cx_o, cy_o, cz_o))
        r0[i] = r
        u1[i] = m1 * u + q1 * (inv_o[i] * r)

    u2 = u0

    @pl.loop(3, 19, unroll=True)
    def _(i):
        iterate[i - 3] = u0[i, pl.ds(0, SIDE)] + u1[i, pl.ds(0, SIDE)]

    @pl.loop(2, ROWS - 2, unroll=True)
    def _(i):
        u = u1[i]
        r = r0[i] - (g_o[i] * u - near(i, u1, cx_o, cy_o, cz_o))
        r0[i] = r
        u2[i] = m2 * u + q2 * (inv_o[i] * r)

    @pl.loop(3, 19, unroll=True)
    def _(i):
        u = u2[i]
        r = r0[i] - (g_o[i] * u - near(i, u2, cx_o, cy_o, cz_o))
        resid[i - 3] = r[:SIDE]
        iterate[i - 3] = iterate[i - 3] + u[:SIDE]

    lanes = sum_lanes(False)
    rows = sum_rows(False)
    crow, clane = iota((8, 128), 0), iota((8, 128), 1)
    own = (crow < 4) & (clane < 64)
    spread = ((iota((16, 128), 1) // 4) == iota((16, 128), 0)).astype(f32)
    mask = dot(jnp.broadcast_to(active[0].astype(f32), (8, 16)), spread)
    below_x = dot(rows, dot(cx_o[2, pl.ds(0, SIDE)], lanes))
    for a in range(4):
        at = 4 * a
        total = resid[at] + resid[at + 1] + resid[at + 2] + resid[at + 3]
        rhs = dot(rows, dot(total, lanes))
        tail = sum(cy_o[at + 3 + k, pl.ds(SIDE, 8)] for k in range(4))
        below_y = back(dot(tail, lanes), 0)
        cx_c, cy_c, cz_c, ab_c = (coarse[n, a] for n in range(4))
        g = cx_c + cy_c + cz_c + ab_c + back(cz_c, 1)
        g = g + (below_x if a == 0 else coarse[0, a - 1])
        g = g + jnp.where(crow == 0, below_y, back(cy_c, 0))
        g = jnp.where(own, g, 0.0)
        inv = jnp.where(own, mask / jnp.where(own, g, 1.0), 0.0)
        z = inv * rhs
        weight[a] = g
        cz_c = jnp.where(clane == 63, 0.0, cz_c)
        upper = z + pltpu.roll(inv, 64, 1)
        lower = cx_c + pltpu.roll(cy_c, 64, 1)
        packed[a, 0] = upper + pltpu.roll(lower, 4, 0)
        packed[a, 1] = cz_c

    for k in range(2):
        for n in range(4):
            ys, zs = pl.ds(8 * (n // 2), 8), pl.ds(128 * (n % 2), 128)
            up[4 * k + n] = resid[14 + k, ys, zs]
            down[4 * k + n] = resid[k, ys, zs]
    for k in range(3):
        for n in range(2):
            up[8 + 2 * k + n] = packed[1 + k, n]
            down[8 + 2 * k + n] = packed[k, n]


def pack_third(flags, resid, packed, low, high, first, second):
    even = flags[4] > 0
    keep_low, keep_high = (flags[0] > 0).astype(f32), (flags[1] > 0).astype(f32)

    def edges(x):
        if x < 0 or x >= SIDE:
            ref, keep, k = (low, keep_low, x + 2) if x < 0 else (high, keep_high, x - SIDE)
            halves = [[ref[4 * k + 2 * h + c] * keep for c in range(2)] for h in range(2)]
            return [half[0:2] for half in halves[0]], [half[6:8] for half in halves[1]]
        head = [resid[x, 0:2, 128 * c : 128 * c + 128] for c in range(2)]
        return head, [resid[x, 14:16, 128 * c : 128 * c + 128] for c in range(2)]

    for n in range(5):
        parts = [edges(4 * n - 2 + k) for k in range(4)]
        for c in range(2):
            bottom = jnp.concatenate([p[0][c] for p in parts], axis=0)
            top = jnp.concatenate([p[1][c] for p in parts], axis=0)
            first[2 * n + c] = jnp.where(even, top, bottom)
            second[2 * n + c] = jnp.where(even, bottom, top)
    for a in range(10):
        for n in range(2):
            if a < 3:
                tile = low[8 + 2 * a + n] * keep_low
            elif a < 7:
                tile = packed[a - 3, n]
            else:
                tile = high[8 + 2 * (a - 7) + n] * keep_high
            first[10 + 2 * a + n] = tile
            second[10 + 2 * a + n] = tile


def krylov(flags, packed, weight, low, high, one, two, basis, message, ext, t1s):
    even = flags[4] > 0
    keep_low, keep_high = (flags[0] > 0).astype(f32), (flags[1] > 0).astype(f32)
    keep_left, keep_right = (flags[2] > 0).astype(f32), (flags[3] > 0).astype(f32)
    crow, clane = iota((8, 128), 0), iota((8, 128), 1)
    own = (crow < 4) & (clane < 64)

    def unpack(tiles):
        first, second = tiles
        turned = pltpu.roll(first, 4, 0)
        five = (first, pltpu.roll(first, 64, 1), turned, pltpu.roll(turned, 64, 1), second)
        return [jnp.where(own, v, 0.0) for v in five]

    for a in range(10):
        if a < 3:
            here = [low[8 + 2 * a + n] * keep_low for n in range(2)]
        elif a < 7:
            here = [packed[a - 3, n] for n in range(2)]
        else:
            here = [high[8 + 2 * (a - 7) + n] * keep_high for n in range(2)]
        here = unpack(here)
        sides = [(one[10 + 2 * a + n], two[10 + 2 * a + n]) for n in range(2)]
        before = unpack([jnp.where(even, q, p) * keep_left for p, q in sides])
        after = unpack([jnp.where(even, p, q) * keep_right for p, q in sides])
        for n in range(5):
            ext[n, a, 0:8] = here[n] + pltpu.roll(after[n], 4, 0)
            ext[n, a, 8:16] = pltpu.roll(before[n], 4, 0)

    z, inv, cx, cy, cz = (ext.at[n] for n in range(5))
    for a in range(1, 9):
        t1s[a] = z[a] - inv[a] * near(a, z, cx, cy, cz)
    for a in range(2, 8):
        t1 = t1s[a]
        basis[0, a - 2] = z[a]
        basis[1, a - 2] = t1
        basis[2, a - 2] = t1 - inv[a] * near(a, t1s, cx, cy, cz)

    def total(parts):
        return jnp.sum(sum(parts), keepdims=True)

    g = [weight[a] for a in range(4)]
    v0, v1, v2 = ([basis[n, a + 1, 0:8] for a in range(4)] for n in range(3))
    s00 = total([w * p * p for w, p in zip(g, v0)])
    s01 = total([w * p * q for w, p, q in zip(g, v0, v1)])
    alpha = jnp.where(s00 > 0, s01 / jnp.where(s00 > 0, s00, 1.0), 0.0)
    e = [q - alpha * p for p, q in zip(v0, v1)]
    te = [q - alpha * p for p, q in zip(v1, v2)]
    terms = [
        s00,
        s01,
        alpha,
        total([w * p * p for w, p in zip(g, e)]),
        total([w * p * q for w, p, q in zip(g, e, v0)]),
        total([w * p * q for w, p, q in zip(g, e, te)]),
        total([w * p * q for w, p, q in zip(g, v0, te)]),
        total([w * p * q for w, p, q in zip(g, e, v1)]),
    ]
    lane = iota((256, 128), 1)
    line = jnp.zeros((256, 128), f32)
    for n, term in enumerate(terms):
        line = jnp.where(lane == n, term, line)
    message[...] = line


def finish(
    flags, gathered, basis, cx, cy, cz, g, inv, resid, iterate, low, high, one, two,
    out, correction, lift, u0, u1, r0,
):
    center, m1, q1, m2, q2 = FINE
    keep_low, keep_high = (flags[0] > 0).astype(f32), (flags[1] > 0).astype(f32)
    keep_left, keep_right = (flags[2] > 0).astype(f32), (flags[3] > 0).astype(f32)
    even = flags[4] > 0
    col = [gathered[:, n : n + 1] for n in range(8)]
    s00, s01, alpha, ee, ez, ete, zte, et1 = col

    def total(v):
        return jnp.sum(v, axis=0, keepdims=True)

    norm = total(s00)
    a1 = total(s01) / norm
    shift = alpha - a1
    square = total(ee + shift * (2.0 * ez + shift * s00))
    energy = total(ete + shift * (zte + et1 + shift * s01))
    b1 = jnp.sqrt(square / norm)
    a2 = energy / square
    bound = jnp.maximum(a1 + b1, a2 + b1)
    middle, k1, h1, k2, h2 = factors(coarse_share * bound, bound)
    v0 = 1.0 / middle
    v1 = (k1 * v0 + h1, -h1 * v0)
    v2 = (k2 * v1[0] + h2, k2 * v1[1] - h2 * (v0 + v1[0]), -h2 * v1[1])
    weights = (v0 + v1[0] + v2[0], v1[1] + v2[1], v2[2])

    fine_row, coarse_row = iota((RING, 16), 0), iota((RING, 16), 1)
    source = jnp.where(fine_row < 20, fine_row // 4, 15)
    rows = (source == coarse_row).astype(f32)
    lanes = (iota((128, LONG), 1) // 4 == iota((128, LONG), 0)).astype(f32)
    for a in range(6):
        field = weights[0] * basis[0, a] + weights[1] * basis[1, a] + weights[2] * basis[2, a]
        if 1 <= a <= 4:
            correction[a - 1] = field[0:4, 0:64]
        fine = dot(rows, dot(field, lanes))
        for k in range(4):
            x = 4 * a - 4 + k + 3
            if 0 <= x < ROWS:
                lift[x] = fine

    none4 = jnp.zeros((4, LONG), f32)

    def strip(ref, x):
        n, k = x // 4, x % 4
        return jnp.concatenate([ref[2 * n + c, 2 * k : 2 * k + 2] for c in range(2)], axis=1)

    for x in range(20):
        if x < 2 or x >= 18:
            ref, keep, k = (low, keep_low, x) if x < 2 else (high, keep_high, x - 18)
            halves = [
                jnp.concatenate([ref[4 * k + 2 * h + c] for c in range(2)], axis=1) for h in range(2)
            ]
            mine = jnp.concatenate(halves, axis=0) * keep
        else:
            mine = resid[x - 2]
        p, q = strip(one, x), strip(two, x)
        after = jnp.where(even, p, q) * keep_right
        before = jnp.where(even, q, p) * keep_left
        r0[x + 1] = jnp.concatenate([mine, after, none4, before], axis=0)

    @pl.loop(1, ROWS - 1, unroll=True)
    def _(i):
        r = r0[i] - (g[i] * lift[i] - near(i, lift, cx, cy, cz))
        r0[i] = r
        u0[i] = inv[i] * r * (1.0 / center)

    @pl.loop(2, ROWS - 2, unroll=True)
    def _(i):
        u = u0[i]
        r = r0[i] - (g[i] * u - near(i, u0, cx, cy, cz))
        r0[i] = r
        u1[i] = m1 * u + q1 * (inv[i] * r)

    @pl.loop(3, 19, unroll=True)
    def _(i):
        u = u1[i]
        r = r0[i] - (g[i] * u - near(i, u1, cx, cy, cz))
        step = (u0[i] + u) + (m2 * u + q2 * (inv[i] * r)) + lift[i]
        out[i - 3] = iterate[i - 3] + step[:SIDE]


def swap(values, axis, odd):
    count = lax.axis_size(axis)
    other = [(i ^ 1) if not odd else (((i + 1) ^ 1) - 1) % count for i in range(count)]
    return lax.ppermute(values, axis, list(enumerate(other)))


def shift(values, axis, by):
    count = lax.axis_size(axis)
    return lax.ppermute(values, axis, [(i, (i + by) % count) for i in range(count)])


def body(src, cx, cy, cz, ab, active):
    ix, iy = lax.axis_index("coarse"), lax.axis_index("fine")
    nx, ny = lax.axis_size("coarse"), lax.axis_size("fine")
    flags = jnp.stack([ix > 0, ix < nx - 1, iy > 0, iy < ny - 1, iy % 2 == 0]).astype(jnp.int32)
    block, ring = (SIDE, SIDE, LONG), pltpu.VMEM((ROWS, RING, LONG), f32)
    rings = (ROWS, RING, LONG)

    up, down = call(
        pack_first,
        [(16, SIDE, LONG), (15, SIDE, LONG)],
        [pltpu.SemaphoreType.DMA((10,))],
        ins=[pl.BlockSpec(memory_space=pl.ANY)] * 5,
    )(src, cx, cy, cz, ab)
    low, high = shift(up, "coarse", 1), shift(down, "coarse", -1)
    (coarse,) = call(coarsen, [(4, 4, 8, 128)], ins=[VMEM] * 4)(cx, cy, cz, ab)
    diag, top, bottom = call(
        pack_second,
        [(ROWS, SIDE, LONG), (11, 24, LONG), (11, 24, LONG)],
        ins=[SMEM] + [VMEM] * 7,
    )(flags, src, cx, cy, cz, ab, low, high)
    left, right = swap(top, "fine", False), swap(bottom, "fine", True)
    cx_r, cy_r, cz_r, g, inv, resid, iterate, packed, weight, up, down = call(
        presmooth,
        [rings] * 5 + [block, block, (4, 2, 8, 128), (4, 8, 128), (14, 8, 128), (14, 8, 128)],
        [ring] * 3,
        ins=[SMEM] + [VMEM] * 11,
    )(flags, src, cx, cy, cz, low, high, diag, left, right, coarse, active)
    low, high = shift(up, "coarse", 1), shift(down, "coarse", -1)
    top, bottom = call(pack_third, [(30, 8, 128)] * 2, ins=[SMEM] + [VMEM] * 4)(
        flags, resid, packed, low, high
    )
    left, right = swap(top, "fine", False), swap(bottom, "fine", True)
    count = nx * ny
    basis, message = call(
        functools.partial(krylov),
        [(3, 6, 16, 128), (256, 128)],
        [pltpu.VMEM((5, 10, 16, 128), f32), pltpu.VMEM((10, 16, 128), f32)],
        ins=[SMEM] + [VMEM] * 6,
    )(flags, packed, weight, low, high, left, right)
    gathered = lax.all_to_all(message[:count], ("coarse", "fine"), 0, 0, tiled=True)
    out, correction = call(
        finish,
        [block, (4, 4, 64)],
        [ring] * 4,
        ins=[SMEM] + [VMEM] * 13,
    )(flags, gathered, basis, cx_r, cy_r, cz_r, g, inv, resid, iterate, low, high, left, right)
    return (out, correction)


def solution(mesh):
    spec = P("coarse", "fine", None)
    return jax.shard_map(
        body, mesh=mesh, in_specs=(spec,) * 6, out_specs=(spec,) * 2, check_vma=False
    )
```

```python
import jax
import jax.numpy as jnp
from jax import lax
from jax.experimental import pallas as pl
from jax.experimental.pallas import tpu as pltpu
from jax.sharding import PartitionSpec as P

f32 = jnp.float32
bf16 = jnp.bfloat16
fine_low = 0.25
fine_high = 2.0
coarse_share = 0.125
SIDE = 16
LONG = 256
ROWS = SIDE + 6
RING = 24
VMEM = pl.BlockSpec(memory_space=pltpu.VMEM)
SMEM = pl.BlockSpec(memory_space=pltpu.SMEM)
LIMIT = 48 * 1024 * 1024


def factors(lower, upper):
    center = 0.5 * (upper + lower)
    radius = 0.5 * (upper - lower)
    aspect = center / radius
    p0 = 1.0 / aspect
    p1 = 1.0 / (2.0 * aspect - p0)
    p2 = 1.0 / (2.0 * aspect - p1)
    return center, p1 * p0, 2.0 * p1 / radius, p2 * p1, 2.0 * p2 / radius


FINE = factors(fine_low, fine_high)


def iota(shape, axis):
    return lax.broadcasted_iota(jnp.int32, shape, axis)


def back(values, axis):
    return pltpu.roll(values, 1, axis)


def ahead(values, axis):
    return pltpu.roll(values, values.shape[axis] - 1, axis)


def call(kernel, outs, scratch=(), ins=None):
    return pl.pallas_call(
        kernel,
        out_shape=[jax.ShapeDtypeStruct(s, f32) for s in outs],
        in_specs=ins,
        out_specs=[VMEM] * len(outs),
        scratch_shapes=list(scratch),
        compiler_params=pltpu.CompilerParams(vmem_limit_bytes=LIMIT),
    )


def pack_first(*refs):
    lows, highs, pair = refs[:5], refs[5:10], refs[10:]
    even = lax.axis_index("coarse") % 2 == 0

    def fill(up, down):
        for n in range(5):
            extra = 1 if n == 1 else 0
            at = UP_AT[n] - extra
            up[at : at + 3 + extra] = highs[n][1 - extra :]
            down[3 * n : 3 * n + 3] = lows[n][:3]

    @pl.when(even)
    def _():
        fill(*pair)

    @pl.when(jnp.logical_not(even))
    def _():
        fill(*pair[::-1])


def pack_first_call(fields):
    low = pl.BlockSpec((4, SIDE, LONG), lambda i: (0, 0, 0))
    high = pl.BlockSpec((4, SIDE, LONG), lambda i: (3, 0, 0))
    return pl.pallas_call(
        pack_first,
        grid=(1,),
        out_shape=[jax.ShapeDtypeStruct((16, SIDE, LONG), f32)] * 2,
        in_specs=[low] * 5 + [high] * 5,
        out_specs=[VMEM] * 2,
    )(*fields, *fields)


UP_AT = (0, 4, 7, 10, 13)


def sum_lanes(last_only):
    cell, lane = iota((LONG, 128), 0), iota((LONG, 128), 1)
    hit = cell // 4 == lane
    if last_only:
        hit = hit & (cell % 4 == 3)
    return hit.astype(bf16)


def sum_rows(last_only):
    block, cell = iota((8, SIDE), 0), iota((8, SIDE), 1)
    hit = cell // 4 == block
    if last_only:
        hit = hit & (cell % 4 == 3)
    return hit.astype(bf16)


def parts_of(values):
    first = values.astype(bf16)
    rest = values - first.astype(f32)
    second = rest.astype(bf16)
    return first, second, (rest - second.astype(f32)).astype(bf16)


def by_right(values, choose):
    return sum(jnp.dot(p, choose, preferred_element_type=f32) for p in parts_of(values))


def by_left(choose, values):
    return sum(jnp.dot(choose, p, preferred_element_type=f32) for p in parts_of(values))


def coarsen(cx, cy, cz, ab, out):
    lanes, last = sum_lanes(False), sum_lanes(True)
    rows, lastrow = sum_rows(False), sum_rows(True)

    def coarse(n, part, left, right):
        total = by_right(jnp.concatenate([part(4 * a) for a in range(4)], axis=0), right)
        for a in range(4):
            out[n, a] = by_left(left, total[SIDE * a : SIDE * a + SIDE])

    def layers(ref):
        return lambda x: (ref[x] + ref[x + 1]) + (ref[x + 2] + ref[x + 3])

    coarse(0, lambda x: cx[x + 3], rows, lanes)
    coarse(1, layers(cy), lastrow, lanes)
    coarse(2, layers(cz), rows, last)
    coarse(3, layers(ab), rows, lanes)


def pack_second(flags, src, cx, cy, cz, ab, one, two, diag, first, second):
    even = flags[4] > 0
    center = FINE[0]
    row, lane = iota((SIDE, LONG), 0), iota((SIDE, LONG), 1)

    def build(i, src_i, cx_i, cxl_i, cy_i, cz_i, ab_i, inside, dst, at):
        g = cx_i + cxl_i + cy_i + cz_i + ab_i
        g = g + jnp.where(row == 0, 0.0, back(cy_i, 0))
        g = g + jnp.where(lane == 0, 0.0, back(cz_i, 1))
        diag[i] = g
        start = jnp.where(inside, src_i / (center * g), 0.0)
        pieces = (src_i, cx_i, cy_i, cz_i, g)
        top = jnp.concatenate(
            [p[14:16] for p in pieces] + [start[13:14], cy_i[13:14]], axis=0
        )
        bottom = jnp.concatenate(
            [p[0:2] for p in pieces] + [start[2:3], start[2:3]], axis=0
        )
        first[dst, pl.ds(at, 12)] = jnp.where(even, top, bottom)
        second[dst, pl.ds(at, 12)] = jnp.where(even, bottom, top)

    has_low, has_high = flags[0] > 0, flags[1] > 0
    low, high = sides(one, two, flags[5] > 0, has_low, has_high)
    for k in range(3):
        f = [low(UP_AT[n] + k) for n in range(5)]
        before = low(3 + k)
        build(k, f[0], f[1], before, f[2], f[3], f[4], has_low, k, 0)
    ins = (src, cx, cy, cz, ab)

    def own(x, before, at, shift):
        f = [ref[x] for ref in ins]
        build(x + 3, f[0], f[1], before, f[2], f[3], f[4], True, x + 3 - shift, at)

    own(0, low(6), 0, 0)

    @pl.loop(1, 8, unroll=True)
    def _(x):
        own(x, cx[x - 1], 0, 0)

    @pl.loop(8, SIDE, unroll=True)
    def _(x):
        own(x, cx[x - 1], 12, 11)

    for k in range(3):
        f = [high(3 * n + k) for n in range(5)]
        before = cx[15] if k == 0 else high(3 + k - 1)
        build(19 + k, f[0], f[1], before, f[2], f[3], f[4], has_high, 8 + k, 12)


def sides(one, two, even, has_low, has_high):
    keep_low, keep_high = has_low.astype(f32), has_high.astype(f32)

    def low(*at):
        return jnp.where(even, two[at], one[at]) * keep_low

    def high(*at):
        return jnp.where(even, one[at], two[at]) * keep_high

    return low, high


def near(i, u, cx, cy, cz):
    here = u[i]
    cy_i, cz_i = cy[i], cz[i]
    total = cx[i] * u[i + 1] + cx[i - 1] * u[i - 1]
    total = total + (cy_i * ahead(here, 0) + back(cy_i * here, 0))
    return total + (cz_i * ahead(here, 1) + back(cz_i * here, 1))


def presmooth(
    flags, src, cx, cy, cz, one_x, two_x, diag, one, two, coarse, active,
    cx_o, cy_o, cz_o, g_o, inv_o, resid, iterate, packed, weight, first, second,
    u0, u1, r0,
):
    center, m1, q1, m2, q2 = FINE
    row, lane = iota((RING, LONG), 0), iota((RING, LONG), 1)
    has_low, has_high = flags[0] > 0, flags[1] > 0
    has_left, has_right = flags[2] > 0, flags[3] > 0
    low, high = sides(one_x, two_x, flags[5] > 0, has_low, has_high)
    left, right = sides(one, two, flags[4] > 0, has_left, has_right)
    inside_y = (row < 16) | ((row < 18) & has_right) | ((row >= 22) & has_left)
    last = lane == LONG - 1
    edge = (row == 0) | (row == 16)
    none1 = jnp.zeros((1, LONG), f32)
    none4 = jnp.zeros((4, LONG), f32)

    def build(i, src_i, cx_i, cy_i, cz_i, at, shift, inside):
        lo = left(i - shift, pl.ds(at, 12))
        hi = right(i - shift, pl.ds(at, 12))

        def ring(own, n):
            return jnp.concatenate([own, hi[2 * n : 2 * n + 2], none4, lo[2 * n : 2 * n + 2]], axis=0)

        src_r, cx_r, cz_r, g = ring(src_i, 0), ring(cx_i, 1), ring(cz_i, 3), ring(diag[i], 4)
        cy_r = jnp.concatenate([cy_i, hi[4:6], none1, none1, none1, lo[11:12], lo[4:6]], axis=0)
        g = g + jnp.where(edge, back(cy_r, 0), 0.0)
        inv = jnp.where(inside_y & inside, 1.0 / g, 0.0)
        cx_o[i] = cx_r
        cy_o[i] = cy_r
        cz_o[i] = jnp.where(last, 0.0, cz_r)
        g_o[i] = g
        inv_o[i] = inv
        r0[i] = src_r
        u = src_r * inv * (1.0 / center)
        u = jnp.where(row == 18, hi[10:11], u)
        u0[i] = jnp.where(row == 21, lo[10:11], u)

    for k in range(3):
        f = [low(UP_AT[n] + k) for n in range(4)]
        build(k, *f, 0, 0, has_low)
    for x in range(SIDE):
        at, shift = (0, 0) if x < 8 else (12, 11)
        build(x + 3, src[x], cx[x], cy[x], cz[x], at, shift, True)
    for k in range(3):
        f = [high(3 * n + k) for n in range(4)]
        build(19 + k, *f, 12, 11, has_high)

    lanes, rows = sum_lanes(False), sum_rows(False)
    crow, clane = iota((8, 128), 0), iota((8, 128), 1)
    own = (crow < 4) & (clane < 64)
    spread = ((iota((16, 128), 1) // 4) == iota((16, 128), 0)).astype(bf16)
    mask = jnp.broadcast_to(active[0].astype(f32), (8, 16)).astype(bf16)
    mask = jnp.dot(mask, spread, preferred_element_type=f32)
    tails = [sum(cy_o[4 * a + 3 + k, pl.ds(SIDE, 8)] for k in range(4)) for a in range(4)]
    below = by_right(jnp.concatenate([cx_o[2, pl.ds(0, SIDE)]] + tails, axis=0), lanes)
    below_x = by_left(rows, below[:SIDE])
    inverse = []
    for a in range(4):
        below_y = back(below[SIDE + 8 * a : SIDE + 8 * a + 8], 0)
        cx_c, cy_c, cz_c, ab_c = (coarse[n, a] for n in range(4))
        g = cx_c + cy_c + cz_c + ab_c + back(cz_c, 1)
        g = g + (below_x if a == 0 else coarse[0, a - 1])
        g = g + jnp.where(crow == 0, below_y, back(cy_c, 0))
        weight[a] = jnp.where(own, g, 0.0)
        inverse.append(jnp.where(own, mask / jnp.where(own, g, 1.0), 0.0))
        lower = cx_c + pltpu.roll(cy_c, 64, 1)
        packed[a, 0] = pltpu.roll(inverse[a], 64, 1) + pltpu.roll(lower, 4, 0)
        packed[a, 1] = jnp.where(clane == 63, 0.0, cz_c)

    for i in range(1, ROWS - 1):
        u = u0[i]
        r = r0[i] - (g_o[i] * u - near(i, u0, cx_o, cy_o, cz_o))
        r0[i] = r
        v = m1 * u + q1 * (inv_o[i] * r)
        u1[i] = v
        if 3 <= i < 19:
            iterate[i - 3] = u[:SIDE] + v[:SIDE]

    u2 = u0
    for i in range(2, ROWS - 2):
        u = u1[i]
        r = r0[i] - (g_o[i] * u - near(i, u1, cx_o, cy_o, cz_o))
        r0[i] = r
        v = m2 * u + q2 * (inv_o[i] * r)
        u2[i] = v
        if 3 <= i < 19:
            iterate[i - 3] = iterate[i - 3] + v[:SIDE]

    even = flags[5] > 0
    totals, edges = [], {}
    for i in range(3, 19):
        r = r0[i] - (g_o[i] * u2[i] - near(i, u2, cx_o, cy_o, cz_o))
        r = r[:SIDE]
        resid[i - 3] = r
        if i % 4 == 3:
            totals.append(r)
        else:
            totals[-1] = totals[-1] + r
        if i - 3 in (0, 1, 14, 15):
            edges[i - 3] = r

    for k in range(2):
        up, down = edges[14 + k], edges[k]
        for n in range(4):
            ys, zs = 8 * (n // 2), 128 * (n % 2)
            p, q = up[ys : ys + 8, zs : zs + 128], down[ys : ys + 8, zs : zs + 128]
            first[4 * k + n] = jnp.where(even, p, q)
            second[4 * k + n] = jnp.where(even, q, p)
    rhs = by_right(jnp.concatenate(totals, axis=0), lanes)
    tiles = []
    for a in range(4):
        z = inverse[a] * by_left(rows, rhs[SIDE * a : SIDE * a + SIDE])
        tiles.append((packed[a, 0] + z, packed[a, 1]))
        packed[a, 0] = tiles[a][0]
    for k in range(3):
        for n in range(2):
            p, q = tiles[1 + k][n], tiles[k][n]
            first[8 + 2 * k + n] = jnp.where(even, p, q)
            second[8 + 2 * k + n] = jnp.where(even, q, p)


def pack_third(flags, resid, packed, one_x, two_x, first, second):
    even = flags[4] > 0
    low, high = sides(one_x, two_x, flags[5] > 0, flags[0] > 0, flags[1] > 0)

    def edges(x):
        if x < 0 or x >= SIDE:
            get, k = (low, x + 2) if x < 0 else (high, x - SIDE)
            halves = [[get(4 * k + 2 * h + c) for c in range(2)] for h in range(2)]
            return [half[0:2] for half in halves[0]], [half[6:8] for half in halves[1]]
        head = [resid[x, 0:2, 128 * c : 128 * c + 128] for c in range(2)]
        return head, [resid[x, 14:16, 128 * c : 128 * c + 128] for c in range(2)]

    for n in range(5):
        parts = [edges(4 * n - 2 + k) for k in range(4)]
        for c in range(2):
            bottom = jnp.concatenate([p[0][c] for p in parts], axis=0)
            top = jnp.concatenate([p[1][c] for p in parts], axis=0)
            first[2 * n + c] = jnp.where(even, top, bottom)
            second[2 * n + c] = jnp.where(even, bottom, top)
    for a in range(10):
        for n in range(2):
            if a < 3:
                tile = low(8 + 2 * a + n)
            elif a < 7:
                tile = packed[a - 3, n]
            else:
                tile = high(8 + 2 * (a - 7) + n)
            first[10 + 2 * a + n] = tile
            second[10 + 2 * a + n] = tile


def krylov(flags, packed, weight, one_x, two_x, one, two, basis, message, ext, t1s):
    low, high = sides(one_x, two_x, flags[5] > 0, flags[0] > 0, flags[1] > 0)
    left, right = sides(one, two, flags[4] > 0, flags[2] > 0, flags[3] > 0)
    crow, clane = iota((8, 128), 0), iota((8, 128), 1)
    own = (crow < 4) & (clane < 64)

    def unpack(tiles):
        first, second = tiles
        turned = pltpu.roll(first, 4, 0)
        five = (first, pltpu.roll(first, 64, 1), turned, pltpu.roll(turned, 64, 1), second)
        return [jnp.where(own, v, 0.0) for v in five]

    for a in range(10):
        if a < 3:
            here = [low(8 + 2 * a + n) for n in range(2)]
        elif a < 7:
            here = [packed[a - 3, n] for n in range(2)]
        else:
            here = [high(8 + 2 * (a - 7) + n) for n in range(2)]
        here = unpack(here)
        before = unpack([left(10 + 2 * a + n) for n in range(2)])
        after = unpack([right(10 + 2 * a + n) for n in range(2)])
        for n in range(5):
            ext[n, a, 0:8] = here[n] + pltpu.roll(after[n], 4, 0)
            ext[n, a, 8:16] = pltpu.roll(before[n], 4, 0)

    z, inv, cx, cy, cz = (ext.at[n] for n in range(5))
    for a in range(1, 9):
        t1s[a] = z[a] - inv[a] * near(a, z, cx, cy, cz)
    for a in range(2, 8):
        t1 = t1s[a]
        basis[0, a - 2] = z[a]
        basis[1, a - 2] = t1
        basis[2, a - 2] = t1 - inv[a] * near(a, t1s, cx, cy, cz)

    def total(parts):
        return jnp.sum(sum(parts), keepdims=True)

    g = [weight[a] for a in range(4)]
    v0, v1, v2 = ([basis[n, a + 1, 0:8] for a in range(4)] for n in range(3))
    s00 = total([w * p * p for w, p in zip(g, v0)])
    s01 = total([w * p * q for w, p, q in zip(g, v0, v1)])
    alpha = jnp.where(s00 > 0, s01 / jnp.where(s00 > 0, s00, 1.0), 0.0)
    e = [q - alpha * p for p, q in zip(v0, v1)]
    te = [q - alpha * p for p, q in zip(v1, v2)]
    terms = [
        total([w * p * p for w, p in zip(g, e)]),
        2.0 * total([w * p * q for w, p, q in zip(g, e, v0)]),
        s00,
        total([w * p * q for w, p, q in zip(g, e, te)]),
        total([w * (p * q + r * t) for w, p, q, r, t in zip(g, v0, te, e, v1)]),
        s01,
    ]
    lane = iota((8, 128), 1)
    line = jnp.where(lane < 64, 0.0, alpha)
    for n, term in enumerate(terms):
        line = jnp.where(lane == n, term, line)
    message[...] = jnp.broadcast_to(line[0:1], (256, 128))


def finish(
    flags, gathered, basis, cx, cy, cz, g, inv, resid, iterate, one_x, two_x, one, two,
    out, correction, lift, u0, u1, r0,
):
    center, m1, q1, m2, q2 = FINE
    low, high = sides(one_x, two_x, flags[5] > 0, flags[0] > 0, flags[1] > 0)
    left, right = sides(one, two, flags[4] > 0, flags[2] > 0, flags[3] > 0)

    lines = gathered[...]
    lane1 = iota((1, 128), 1)
    sums = jnp.sum(lines, axis=0, keepdims=True)

    def pick(values, first, count):
        hit = (lane1 >= first) & (lane1 < first + count)
        return jnp.sum(jnp.where(hit, values, 0.0), axis=1, keepdims=True)

    norm = pick(sums, 2, 1)
    a1 = pick(sums, 5, 1) / norm
    shift = pltpu.roll(lines, 64, 1) - a1
    plain, linear, quadratic = (((lane1 == k) | (lane1 == k + 3)).astype(f32) for k in range(3))
    power = plain + shift * (linear + shift * quadratic)
    sums = jnp.sum(lines * power, axis=0, keepdims=True)
    square, energy = pick(sums, 0, 3), pick(sums, 3, 3)
    bound = jnp.maximum(a1, energy / square) + jnp.sqrt(square / norm)
    middle, k1, h1, k2, h2 = factors(coarse_share, 1.0)
    scale = 1.0 / bound
    v0, h1, h2 = scale * (1.0 / middle), scale * h1, scale * h2
    v1 = (k1 * v0 + h1, -h1 * v0)
    v2 = (k2 * v1[0] + h2, k2 * v1[1] - h2 * (v0 + v1[0]), -h2 * v1[1])
    weights = (v0 + v1[0] + v2[0], v1[1] + v2[1], v2[2])

    upper = iota((8, 128), 0) < 4
    tall = []
    for a in range(6):
        field = weights[0] * basis[0, a] + weights[1] * basis[1, a] + weights[2] * basis[2, a]
        if 1 <= a <= 4:
            correction[a - 1] = field[0:4, 0:64]
        for p, q in ((0, 1), (2, 3), (4, 15)):
            p, q = (jnp.broadcast_to(field[k : k + 1], (8, 128)) for k in (p, q))
            tall.append(jnp.where(upper, p, q))
    lanes = (iota((128, LONG), 1) // 4 == iota((128, LONG), 0)).astype(bf16)
    fine = by_right(jnp.concatenate(tall, axis=0), lanes)
    lifted = [fine[RING * a : RING * a + RING] for a in range(6)]
    for i in range(ROWS):
        lift[i] = lifted[(i + 1) // 4]

    none4 = jnp.zeros((4, LONG), f32)

    def strip(get, x):
        n, k = x // 4, x % 4
        return jnp.concatenate([get(2 * n + c, pl.ds(2 * k, 2)) for c in range(2)], axis=1)

    for i in range(1, ROWS - 1):
        x = i - 1
        if x < 2 or x >= 18:
            get, k = (low, x) if x < 2 else (high, x - 18)
            halves = [
                jnp.concatenate([get(4 * k + 2 * h + c) for c in range(2)], axis=1) for h in range(2)
            ]
            mine = jnp.concatenate(halves, axis=0)
        else:
            mine = resid[x - 2]
        r0[i] = jnp.concatenate([mine, strip(right, x), none4, strip(left, x)], axis=0)

    for i in range(1, ROWS - 1):
        r = r0[i] - (g[i] * lift[i] - near(i, lift, cx, cy, cz))
        r0[i] = r
        u0[i] = inv[i] * r * (1.0 / center)

    for i in range(2, ROWS - 2):
        u = u0[i]
        r = r0[i] - (g[i] * u - near(i, u0, cx, cy, cz))
        r0[i] = r
        u1[i] = m1 * u + q1 * (inv[i] * r)

    for i in range(3, 19):
        u = u1[i]
        r = r0[i] - (g[i] * u - near(i, u1, cx, cy, cz))
        step = (u0[i] + u) + (m2 * u + q2 * (inv[i] * r)) + lift[i]
        out[i - 3] = iterate[i - 3] + step[:SIDE]


def swap(values, axis, odd):
    count = lax.axis_size(axis)
    other = [(i ^ 1) if not odd else (((i + 1) ^ 1) - 1) % count for i in range(count)]
    return lax.ppermute(values, axis, list(enumerate(other)))


def body(src, cx, cy, cz, ab, active):
    ix, iy = lax.axis_index("coarse"), lax.axis_index("fine")
    nx, ny = lax.axis_size("coarse"), lax.axis_size("fine")
    flags = jnp.stack([ix > 0, ix < nx - 1, iy > 0, iy < ny - 1, iy % 2 == 0, ix % 2 == 0]).astype(jnp.int32)
    block, ring = (SIDE, SIDE, LONG), pltpu.VMEM((ROWS, RING, LONG), f32)
    rings = (ROWS, RING, LONG)

    first, second = pack_first_call((src, cx, cy, cz, ab))
    one_x, two_x = swap(first, "coarse", False), swap(second, "coarse", True)
    (coarse,) = call(coarsen, [(4, 4, 8, 128)], ins=[VMEM] * 4)(cx, cy, cz, ab)
    diag, first, second = call(
        pack_second,
        [(ROWS, SIDE, LONG), (11, 24, LONG), (11, 24, LONG)],
        ins=[SMEM] + [VMEM] * 7,
    )(flags, src, cx, cy, cz, ab, one_x, two_x)
    one, two = swap(first, "fine", False), swap(second, "fine", True)
    cx_r, cy_r, cz_r, g, inv, resid, iterate, packed, weight, first, second = call(
        presmooth,
        [rings] * 5 + [block, block, (4, 2, 8, 128), (4, 8, 128), (14, 8, 128), (14, 8, 128)],
        [ring] * 3,
        ins=[SMEM] + [VMEM] * 11,
    )(flags, src, cx, cy, cz, one_x, two_x, diag, one, two, coarse, active)
    one_x, two_x = swap(first, "coarse", False), swap(second, "coarse", True)
    first, second = call(pack_third, [(30, 8, 128)] * 2, ins=[SMEM] + [VMEM] * 4)(
        flags, resid, packed, one_x, two_x
    )
    one, two = swap(first, "fine", False), swap(second, "fine", True)
    count = nx * ny
    basis, message = call(
        krylov,
        [(3, 6, 16, 128), (256, 128)],
        [pltpu.VMEM((5, 10, 16, 128), f32), pltpu.VMEM((10, 16, 128), f32)],
        ins=[SMEM] + [VMEM] * 6,
    )(flags, packed, weight, one_x, two_x, one, two)
    gathered = lax.all_to_all(message[:count], ("coarse", "fine"), 0, 0, tiled=True)
    out, correction = call(
        finish,
        [block, (4, 4, 64)],
        [ring] * 4,
        ins=[SMEM] + [VMEM] * 13,
    )(flags, gathered, basis, cx_r, cy_r, cz_r, g, inv, resid, iterate, one_x, two_x, one, two)
    return (out, correction)


def solution(mesh):
    spec = P("coarse", "fine", None)
    return jax.shard_map(
        body, mesh=mesh, in_specs=(spec,) * 6, out_specs=(spec,) * 2, check_vma=False
    )
```

```python
import jax
import jax.numpy as jnp
from jax import lax
from jax.experimental import pallas as pl
from jax.experimental.pallas import tpu as pltpu
from jax.sharding import PartitionSpec as P

f32 = jnp.float32
bf16 = jnp.bfloat16
fine_low = 0.25
fine_high = 2.0
coarse_share = 0.125
SIDE = 16
LONG = 256
ROWS = SIDE + 6
RING = 24
VMEM = pl.BlockSpec(memory_space=pltpu.VMEM)
SMEM = pl.BlockSpec(memory_space=pltpu.SMEM)
LIMIT = 48 * 1024 * 1024


def factors(lower, upper):
    center = 0.5 * (upper + lower)
    radius = 0.5 * (upper - lower)
    aspect = center / radius
    p0 = 1.0 / aspect
    p1 = 1.0 / (2.0 * aspect - p0)
    p2 = 1.0 / (2.0 * aspect - p1)
    return center, p1 * p0, 2.0 * p1 / radius, p2 * p1, 2.0 * p2 / radius


FINE = factors(fine_low, fine_high)


def iota(shape, axis):
    return lax.broadcasted_iota(jnp.int32, shape, axis)


def back(values, axis):
    return pltpu.roll(values, 1, axis)


def ahead(values, axis):
    return pltpu.roll(values, values.shape[axis] - 1, axis)


def call(kernel, outs, scratch=(), ins=None):
    return pl.pallas_call(
        kernel,
        out_shape=[jax.ShapeDtypeStruct(s, f32) for s in outs],
        in_specs=ins,
        out_specs=[VMEM] * len(outs),
        scratch_shapes=list(scratch),
        compiler_params=pltpu.CompilerParams(vmem_limit_bytes=LIMIT),
    )


def pack_first(*refs):
    fields, pair, sems = refs[:5], refs[5:7], refs[7]
    even = lax.axis_index("coarse") % 2 == 0

    def fill(up, down):
        copies = []
        for n, field in enumerate(fields):
            first = 12 if n == 1 else 13
            at = UP_AT[n] + first - 13
            copies.append((field.at[first:16], up.at[at : at + 16 - first]))
            copies.append((field.at[0:3], down.at[3 * n : 3 * n + 3]))
        copies = [pltpu.make_async_copy(a, b, sems.at[k]) for k, (a, b) in enumerate(copies)]
        for copy in copies:
            copy.start()
        for copy in copies:
            copy.wait()

    @pl.when(even)
    def _():
        fill(*pair)

    @pl.when(jnp.logical_not(even))
    def _():
        fill(*pair[::-1])


def pack_first_call(fields):
    return pl.pallas_call(
        pack_first,
        out_shape=[jax.ShapeDtypeStruct((16, SIDE, LONG), f32)] * 2,
        in_specs=[pl.BlockSpec(memory_space=pltpu.HBM)] * 5,
        out_specs=[VMEM] * 2,
        scratch_shapes=[pltpu.SemaphoreType.DMA((10,))],
    )(*fields)


UP_AT = (0, 4, 7, 10, 13)


def sum_lanes(last_only):
    cell, lane = iota((LONG, 128), 0), iota((LONG, 128), 1)
    hit = cell // 4 == lane
    if last_only:
        hit = hit & (cell % 4 == 3)
    return hit.astype(bf16)


def sum_rows(last_only):
    block, cell = iota((8, SIDE), 0), iota((8, SIDE), 1)
    hit = cell // 4 == block
    if last_only:
        hit = hit & (cell % 4 == 3)
    return hit.astype(bf16)


def parts_of(values):
    first = values.astype(bf16)
    rest = values - first.astype(f32)
    second = rest.astype(bf16)
    return first, second, (rest - second.astype(f32)).astype(bf16)


def by_right(values, choose):
    return sum(jnp.dot(p, choose, preferred_element_type=f32) for p in parts_of(values))


def by_left(choose, values):
    return sum(jnp.dot(choose, p, preferred_element_type=f32) for p in parts_of(values))


def coarsen(cx, cy, cz, ab, active, out, mask):
    lanes, last = sum_lanes(False), sum_lanes(True)
    rows, lastrow = sum_rows(False), sum_rows(True)

    def coarse(n, part, left, right):
        total = by_right(jnp.concatenate([part(4 * a) for a in range(4)], axis=0), right)
        for a in range(4):
            out[n, a] = by_left(left, total[SIDE * a : SIDE * a + SIDE])

    def layers(ref):
        return lambda x: (ref[x] + ref[x + 1]) + (ref[x + 2] + ref[x + 3])

    coarse(0, lambda x: cx[x + 3], rows, lanes)
    coarse(1, layers(cy), lastrow, lanes)
    coarse(2, layers(cz), rows, last)
    coarse(3, layers(ab), rows, lanes)
    spread = ((iota((16, 128), 1) // 4) == iota((16, 128), 0)).astype(bf16)
    line = jnp.broadcast_to(active[0].astype(f32), (8, 16)).astype(bf16)
    mask[...] = jnp.dot(line, spread, preferred_element_type=f32)


def diagonal(cx_i, cxl_i, cy_i, cz_i, ab_i):
    row, lane = iota((SIDE, LONG), 0), iota((SIDE, LONG), 1)
    g = cx_i + cxl_i + cy_i + cz_i + ab_i
    g = g + jnp.where(row == 0, 0.0, back(cy_i, 0))
    return g + jnp.where(lane == 0, 0.0, back(cz_i, 1))


def strips(src_i, cx_i, cy_i, cz_i, g, inside, beyond=None):
    start = jnp.where(inside, src_i / (FINE[0] * g), 0.0)
    pieces = (src_i, cx_i, cy_i, cz_i, g)
    third = cy_i[13:14] if beyond is None else beyond[15:16]
    top = jnp.concatenate([p[14:16] for p in pieces] + [start[13:14], third], axis=0)
    bottom = jnp.concatenate([p[0:2] for p in pieces] + [start[2:3], start[2:3]], axis=0)
    return top, bottom


def pack_inner(flags, src, cx, cy, cz, ab, diag, first, second):
    even = flags[4] > 0
    for x in range(1, SIDE):
        g = diagonal(cx[x], cx[x - 1], cy[x], cz[x], ab[x])
        diag[x] = g
        top, bottom = strips(src[x], cx[x], cy[x], cz[x], g, True)
        at = (x - 1) % 8, pl.ds(12 * ((x - 1) // 8), 12)
        first[at] = jnp.where(even, top, bottom)
        second[at] = jnp.where(even, bottom, top)


def pack_outer(flags, src, cx, cy, cz, ab, one, two, diag, first, second):
    even = flags[4] > 0
    has_low, has_high = flags[0] > 0, flags[1] > 0
    low, high = sides(one, two, flags[5] > 0, has_low, has_high)
    layers = []
    for k in range(3):
        f = [low(UP_AT[n] + k) for n in range(5)]
        layers.append((f, low(3 + k), has_low, low(UP_AT[2]) if k == 1 else None))
    layers.append(([ref[0] for ref in (src, cx, cy, cz, ab)], low(6), True, None))
    for k in range(3):
        f = [high(3 * n + k) for n in range(5)]
        before = cx[15] if k == 0 else high(3 + k - 1)
        layers.append((f, before, has_high, high(8) if k == 1 else None))
    for k, (f, before, inside, beyond) in enumerate(layers):
        g = diagonal(f[1], before, *f[2:])
        diag[k] = g
        if 1 <= k < 6:
            top, bottom = strips(*f[:4], g, inside, beyond)
            at = (k - 1) % 3, pl.ds(12 * ((k - 1) // 3), 12)
            first[at] = jnp.where(even, top, bottom)
            second[at] = jnp.where(even, bottom, top)


def sides(one, two, even, has_low, has_high):
    keep_low, keep_high = has_low.astype(f32), has_high.astype(f32)

    def low(*at):
        return jnp.where(even, two[at], one[at]) * keep_low

    def high(*at):
        return jnp.where(even, one[at], two[at]) * keep_high

    return low, high


def near(i, u, cx, cy, cz):
    here = u[i]
    cy_i, cz_i = cy[i], cz[i]
    total = cx[i] * u[i + 1] + cx[i - 1] * u[i - 1]
    total = total + (cy_i * ahead(here, 0) + back(cy_i * here, 0))
    return total + (cz_i * ahead(here, 1) + back(cz_i * here, 1))


def join(layers):
    total = layers[0]
    for k, v in enumerate(layers[1:], 1):
        v = pltpu.roll(v, 64, 1) if k >= 2 else v
        total = total + (pltpu.roll(v, 4, 0) if k % 2 else v)
    return total


def presmooth(
    flags, src, cx, cy, cz, one_x, two_x, diag, diag_out, one, two, one_out, two_out, coarse, active,
    cx_o, cy_o, cz_o, g_o, inv_o, resid, iterate, packed, weight, first, second,
    u0, u1, r0,
):
    center, m1, q1, m2, q2 = FINE
    row, lane = iota((RING, LONG), 0), iota((RING, LONG), 1)
    has_low, has_high = flags[0] > 0, flags[1] > 0
    has_left, has_right = flags[2] > 0, flags[3] > 0
    low, high = sides(one_x, two_x, flags[5] > 0, has_low, has_high)
    left, right = sides(one, two, flags[4] > 0, has_left, has_right)
    left_out, right_out = sides(one_out, two_out, flags[4] > 0, has_left, has_right)
    inside_y = (row < 16) | ((row < 18) & has_right) | ((row >= 22) & has_left)
    last = lane == LONG - 1
    edge = (row == 0) | (row == 16)
    none1 = jnp.zeros((1, LONG), f32)
    none4 = jnp.zeros((4, LONG), f32)

    none12 = jnp.zeros((12, LONG), f32)

    def build(i, src_i, cx_i, cy_i, cz_i, inside):
        lo = hi = none12
        hit = inside_y & inside
        if 4 <= i < 19:
            at, g = ((i - 4) % 8, pl.ds(12 * ((i - 4) // 8), 12)), diag[i - 3]
            lo, hi = left(*at), right(*at)
        else:
            k = i if i < 4 else i - 15
            g = diag_out[k]
            if 1 <= k < 6:
                at = (k - 1) % 3, pl.ds(12 * ((k - 1) // 3), 12)
                lo, hi = left_out(*at), right_out(*at)
            else:
                hit = hit & (row < SIDE)

        def ring(own, n):
            return jnp.concatenate([own, hi[2 * n : 2 * n + 2], none4, lo[2 * n : 2 * n + 2]], axis=0)

        src_r, cx_r, cz_r, g = ring(src_i, 0), ring(cx_i, 1), ring(cz_i, 3), ring(g, 4)
        cy_r = jnp.concatenate([cy_i, hi[4:6], none1, none1, none1, lo[11:12], lo[4:6]], axis=0)
        if i in (0, ROWS - 1):
            dst, at = (0, 0) if i == 0 else (1, 12)
            cy_r = jnp.where(row == 23, left_out(dst, pl.ds(at, 12))[11:12], cy_r)
        g = g + jnp.where(edge, back(cy_r, 0), 0.0)
        inv = jnp.where(hit, 1.0 / g, 0.0)
        cx_o[i] = cx_r
        cy_o[i] = cy_r
        cz_o[i] = jnp.where(last, 0.0, cz_r)
        g_o[i] = g
        inv_o[i] = inv
        r0[i] = src_r
        u = src_r * inv * (1.0 / center)
        u = jnp.where(row == 18, hi[10:11], u)
        u0[i] = jnp.where(row == 21, lo[10:11], u)

    for k in range(3):
        build(k, *[low(UP_AT[n] + k) for n in range(4)], has_low)
    for x in range(SIDE):
        build(x + 3, src[x], cx[x], cy[x], cz[x], True)
    for k in range(3):
        build(19 + k, *[high(3 * n + k) for n in range(4)], has_high)

    lanes, rows = sum_lanes(False), sum_rows(False)
    crow, clane = iota((8, 128), 0), iota((8, 128), 1)
    own = (crow < 4) & (clane < 64)
    mask = active[...]
    tails = [sum(cy_o[4 * a + 3 + k, pl.ds(SIDE, 8)] for k in range(4)) for a in range(4)]
    below = by_right(jnp.concatenate([cx_o[2, pl.ds(0, SIDE)]] + tails, axis=0), lanes)
    below_x = by_left(rows, below[:SIDE])
    inverse, uppers = [], []
    for a in range(4):
        below_y = back(below[SIDE + 8 * a : SIDE + 8 * a + 8], 0)
        cx_c, cy_c, cz_c, ab_c = (coarse[n, a] for n in range(4))
        g = cx_c + cy_c + cz_c + ab_c + back(cz_c, 1)
        g = g + (below_x if a == 0 else coarse[0, a - 1])
        g = g + jnp.where(crow == 0, below_y, back(cy_c, 0))
        weight[a] = jnp.where(own, g, 0.0)
        inverse.append(jnp.where(own, mask / jnp.where(own, g, 1.0), 0.0))
        lower = cx_c + pltpu.roll(cy_c, 64, 1)
        packed[a] = pltpu.roll(inverse[a], 64, 1) + pltpu.roll(lower, 4, 0)
        uppers.append(jnp.where(clane == 63, 0.0, cz_c))
    packed[4] = join(uppers)

    for i in range(1, ROWS - 1):
        u = u0[i]
        r = r0[i] - (g_o[i] * u - near(i, u0, cx_o, cy_o, cz_o))
        r0[i] = r
        v = m1 * u + q1 * (inv_o[i] * r)
        u1[i] = v
        if 3 <= i < 19:
            iterate[i - 3] = u[:SIDE] + v[:SIDE]

    u2 = u0
    for i in range(2, ROWS - 2):
        u = u1[i]
        r = r0[i] - (g_o[i] * u - near(i, u1, cx_o, cy_o, cz_o))
        r0[i] = r
        v = m2 * u + q2 * (inv_o[i] * r)
        u2[i] = v
        if 3 <= i < 19:
            iterate[i - 3] = iterate[i - 3] + v[:SIDE]

    even = flags[5] > 0
    totals, edges = [], {}
    for i in range(3, 19):
        r = r0[i] - (g_o[i] * u2[i] - near(i, u2, cx_o, cy_o, cz_o))
        r = r[:SIDE]
        resid[i - 3] = r
        if i % 4 == 3:
            totals.append(r)
        else:
            totals[-1] = totals[-1] + r
        if i - 3 in (0, 1, 14, 15):
            edges[i - 3] = r

    for k in range(2):
        up, down = edges[14 + k], edges[k]
        for n in range(4):
            ys, zs = 8 * (n // 2), 128 * (n % 2)
            p, q = up[ys : ys + 8, zs : zs + 128], down[ys : ys + 8, zs : zs + 128]
            first[4 * k + n] = jnp.where(even, p, q)
            second[4 * k + n] = jnp.where(even, q, p)
    rhs = by_right(jnp.concatenate(totals, axis=0), lanes)
    tiles = []
    for a in range(4):
        z = inverse[a] * by_left(rows, rhs[SIDE * a : SIDE * a + SIDE])
        tiles.append(packed[a] + z)
        packed[a] = tiles[a]
    ups, downs = tiles[1:4] + [join(uppers[1:4])], tiles[0:3] + [join(uppers[0:3])]
    for k, (p, q) in enumerate(zip(ups, downs)):
        first[8 + k] = jnp.where(even, p, q)
        second[8 + k] = jnp.where(even, q, p)


def pack_third(flags, resid, packed, one_x, two_x, first, second):
    even = flags[4] > 0
    low, high = sides(one_x, two_x, flags[5] > 0, flags[0] > 0, flags[1] > 0)

    def edges(x):
        if x < 0 or x >= SIDE:
            get, k = (low, x + 2) if x < 0 else (high, x - SIDE)
            halves = [[get(4 * k + 2 * h + c) for c in range(2)] for h in range(2)]
            return [half[0:2] for half in halves[0]], [half[6:8] for half in halves[1]]
        head = [resid[x, 0:2, 128 * c : 128 * c + 128] for c in range(2)]
        return head, [resid[x, 14:16, 128 * c : 128 * c + 128] for c in range(2)]

    for n in range(5):
        parts = [edges(4 * n - 2 + k) for k in range(4)]
        for c in range(2):
            bottom = jnp.concatenate([p[0][c] for p in parts], axis=0)
            top = jnp.concatenate([p[1][c] for p in parts], axis=0)
            first[2 * n + c] = jnp.where(even, top, bottom)
            second[2 * n + c] = jnp.where(even, bottom, top)
    tiles = [low(8 + a) for a in range(3)] + [packed[a] for a in range(4)] + [high(8 + a) for a in range(3)]
    for a, tile in enumerate(tiles + [low(11), packed[4], high(11)]):
        first[10 + a] = tile
        second[10 + a] = tile


def krylov(flags, packed, weight, one_x, two_x, one, two, basis, message, ext, t1s):
    low, high = sides(one_x, two_x, flags[5] > 0, flags[0] > 0, flags[1] > 0)
    left, right = sides(one, two, flags[4] > 0, flags[2] > 0, flags[3] > 0)
    crow, clane = iota((8, 128), 0), iota((8, 128), 1)
    own = (crow < 4) & (clane < 64)

    def unpack(tiles, a):
        turned = pltpu.roll(tiles[a], 4, 0)
        five = [tiles[a], pltpu.roll(tiles[a], 64, 1), turned, pltpu.roll(turned, 64, 1)]
        group, k = (0, a) if a < 3 else (1, a - 3) if a < 7 else (2, a - 7)
        upper = tiles[10 + group]
        upper = pltpu.roll(upper, 4, 0) if k % 2 else upper
        five.append(pltpu.roll(upper, 64, 1) if k >= 2 else upper)
        return [jnp.where(own, v, 0.0) for v in five]

    mine = [low(8 + a) for a in range(3)] + [packed[a] for a in range(4)] + [high(8 + a) for a in range(3)]
    mine = mine + [low(11), packed[4], high(11)]
    previous, following = [left(10 + a) for a in range(13)], [right(10 + a) for a in range(13)]
    for a in range(10):
        here, before, after = unpack(mine, a), unpack(previous, a), unpack(following, a)
        for n in range(5):
            ext[n, a, 0:8] = here[n] + pltpu.roll(after[n], 4, 0)
            ext[n, a, 8:16] = pltpu.roll(before[n], 4, 0)

    z, inv, cx, cy, cz = (ext.at[n] for n in range(5))
    for a in range(1, 9):
        t1s[a] = z[a] - inv[a] * near(a, z, cx, cy, cz)
    for a in range(2, 8):
        t1 = t1s[a]
        basis[0, a - 2] = z[a]
        basis[1, a - 2] = t1
        basis[2, a - 2] = t1 - inv[a] * near(a, t1s, cx, cy, cz)

    def total(parts):
        return jnp.sum(sum(parts), keepdims=True)

    g = [weight[a] for a in range(4)]
    v0, v1, v2 = ([basis[n, a + 1, 0:8] for a in range(4)] for n in range(3))
    s00 = total([w * p * p for w, p in zip(g, v0)])
    s01 = total([w * p * q for w, p, q in zip(g, v0, v1)])
    alpha = jnp.where(s00 > 0, s01 / jnp.where(s00 > 0, s00, 1.0), 0.0)
    e = [q - alpha * p for p, q in zip(v0, v1)]
    te = [q - alpha * p for p, q in zip(v1, v2)]
    terms = [
        total([w * p * p for w, p in zip(g, e)]),
        2.0 * total([w * p * q for w, p, q in zip(g, e, v0)]),
        s00,
        total([w * p * q for w, p, q in zip(g, e, te)]),
        total([w * (p * q + r * t) for w, p, q, r, t in zip(g, v0, te, e, v1)]),
        s01,
    ]
    lane = iota((8, 128), 1)
    line = jnp.where(lane < 64, 0.0, alpha)
    for n, term in enumerate(terms):
        line = jnp.where(lane == n, term, line)
    message[...] = jnp.broadcast_to(line[0:1], (256, 128))


def finish(
    flags, gathered, basis, cx, cy, cz, g, inv, resid, iterate, one_x, two_x, one, two,
    out, correction, lift, u0, u1, r0,
):
    center, m1, q1, m2, q2 = FINE
    low, high = sides(one_x, two_x, flags[5] > 0, flags[0] > 0, flags[1] > 0)
    left, right = sides(one, two, flags[4] > 0, flags[2] > 0, flags[3] > 0)

    lines = gathered[...]
    lane1 = iota((1, 128), 1)
    sums = jnp.sum(lines, axis=0, keepdims=True)

    def pick(values, first, count):
        hit = (lane1 >= first) & (lane1 < first + count)
        return jnp.sum(jnp.where(hit, values, 0.0), axis=1, keepdims=True)

    norm = pick(sums, 2, 1)
    a1 = pick(sums, 5, 1) / norm
    shift = pltpu.roll(lines, 64, 1) - a1
    plain, linear, quadratic = (((lane1 == k) | (lane1 == k + 3)).astype(f32) for k in range(3))
    power = plain + shift * (linear + shift * quadratic)
    sums = jnp.sum(lines * power, axis=0, keepdims=True)
    square, energy = pick(sums, 0, 3), pick(sums, 3, 3)
    bound = jnp.maximum(a1, energy / square) + jnp.sqrt(square / norm)
    middle, k1, h1, k2, h2 = factors(coarse_share, 1.0)
    scale = 1.0 / bound
    v0, h1, h2 = scale * (1.0 / middle), scale * h1, scale * h2
    v1 = (k1 * v0 + h1, -h1 * v0)
    v2 = (k2 * v1[0] + h2, k2 * v1[1] - h2 * (v0 + v1[0]), -h2 * v1[1])
    weights = (v0 + v1[0] + v2[0], v1[1] + v2[1], v2[2])

    upper = iota((8, 128), 0) < 4
    tall = []
    for a in range(6):
        field = weights[0] * basis[0, a] + weights[1] * basis[1, a] + weights[2] * basis[2, a]
        if 1 <= a <= 4:
            correction[a - 1] = field[0:4, 0:64]
        for p, q in ((0, 1), (2, 3), (4, 15)):
            p, q = (jnp.broadcast_to(field[k : k + 1], (8, 128)) for k in (p, q))
            tall.append(jnp.where(upper, p, q))
    lanes = (iota((128, LONG), 1) // 4 == iota((128, LONG), 0)).astype(bf16)
    fine = by_right(jnp.concatenate(tall, axis=0), lanes)
    lifted = [fine[RING * a : RING * a + RING] for a in range(6)]
    for i in range(ROWS):
        lift[i] = lifted[(i + 1) // 4]

    none4 = jnp.zeros((4, LONG), f32)

    def strip(get, x):
        n, k = x // 4, x % 4
        return jnp.concatenate([get(2 * n + c, pl.ds(2 * k, 2)) for c in range(2)], axis=1)

    for i in range(1, ROWS - 1):
        x = i - 1
        if x < 2 or x >= 18:
            get, k = (low, x) if x < 2 else (high, x - 18)
            halves = [
                jnp.concatenate([get(4 * k + 2 * h + c) for c in range(2)], axis=1) for h in range(2)
            ]
            mine = jnp.concatenate(halves, axis=0)
        else:
            mine = resid[x - 2]
        r0[i] = jnp.concatenate([mine, strip(right, x), none4, strip(left, x)], axis=0)

    for i in range(1, ROWS - 1):
        r = r0[i] - (g[i] * lift[i] - near(i, lift, cx, cy, cz))
        r0[i] = r
        u0[i] = inv[i] * r * (1.0 / center)

    for i in range(2, ROWS - 2):
        u = u0[i]
        r = r0[i] - (g[i] * u - near(i, u0, cx, cy, cz))
        r0[i] = r
        u1[i] = m1 * u + q1 * (inv[i] * r)

    for i in range(3, 19):
        u = u1[i]
        r = r0[i] - (g[i] * u - near(i, u1, cx, cy, cz))
        step = (u0[i] + u) + (m2 * u + q2 * (inv[i] * r)) + lift[i]
        out[i - 3] = iterate[i - 3] + step[:SIDE]


def swap(values, axis, odd):
    count = lax.axis_size(axis)
    other = [(i ^ 1) if not odd else (((i + 1) ^ 1) - 1) % count for i in range(count)]
    return lax.ppermute(values, axis, list(enumerate(other)))


def body(src, cx, cy, cz, ab, active):
    ix, iy = lax.axis_index("coarse"), lax.axis_index("fine")
    nx, ny = lax.axis_size("coarse"), lax.axis_size("fine")
    flags = jnp.stack([ix > 0, ix < nx - 1, iy > 0, iy < ny - 1, iy % 2 == 0, ix % 2 == 0]).astype(jnp.int32)
    block, ring = (SIDE, SIDE, LONG), pltpu.VMEM((ROWS, RING, LONG), f32)
    rings = (ROWS, RING, LONG)

    first, second = pack_first_call((src, cx, cy, cz, ab))
    one_x, two_x = swap(first, "coarse", False), swap(second, "coarse", True)
    coarse, mask = call(coarsen, [(4, 4, 8, 128), (8, 128)], ins=[VMEM] * 5)(cx, cy, cz, ab, active)
    diag, first, second = call(
        pack_inner, [block, (8, 24, LONG), (8, 24, LONG)], ins=[SMEM] + [VMEM] * 5
    )(flags, src, cx, cy, cz, ab)
    one, two = swap(first, "fine", False), swap(second, "fine", True)
    diag_out, first, second = call(
        pack_outer, [(7, SIDE, LONG), (3, 24, LONG), (3, 24, LONG)], ins=[SMEM] + [VMEM] * 7
    )(flags, src, cx, cy, cz, ab, one_x, two_x)
    one_out, two_out = swap(first, "fine", False), swap(second, "fine", True)
    cx_r, cy_r, cz_r, g, inv, resid, iterate, packed, weight, first, second = call(
        presmooth,
        [rings] * 5 + [block, block, (5, 8, 128), (4, 8, 128), (12, 8, 128), (12, 8, 128)],
        [ring] * 3,
        ins=[SMEM] + [VMEM] * 14,
    )(flags, src, cx, cy, cz, one_x, two_x, diag, diag_out, one, two, one_out, two_out, coarse, mask)
    one_x, two_x = swap(first, "coarse", False), swap(second, "coarse", True)
    first, second = call(pack_third, [(23, 8, 128)] * 2, ins=[SMEM] + [VMEM] * 4)(
        flags, resid, packed, one_x, two_x
    )
    one, two = swap(first, "fine", False), swap(second, "fine", True)
    count = nx * ny
    basis, message = call(
        krylov,
        [(3, 6, 16, 128), (256, 128)],
        [pltpu.VMEM((5, 10, 16, 128), f32), pltpu.VMEM((10, 16, 128), f32)],
        ins=[SMEM] + [VMEM] * 6,
    )(flags, packed, weight, one_x, two_x, one, two)
    gathered = lax.all_to_all(message[:count], ("coarse", "fine"), 0, 0, tiled=True)
    out, correction = call(
        finish,
        [block, (4, 4, 64)],
        [ring] * 4,
        ins=[SMEM] + [VMEM] * 13,
    )(flags, gathered, basis, cx_r, cy_r, cz_r, g, inv, resid, iterate, one_x, two_x, one, two)
    return (out, correction)


def solution(mesh):
    spec = P("coarse", "fine", None)
    return jax.shard_map(
        body, mesh=mesh, in_specs=(spec,) * 6, out_specs=(spec,) * 2, check_vma=False
    )
```

```python
import jax
import jax.numpy as jnp
from jax import lax
from jax.experimental import pallas as pl
from jax.experimental.pallas import tpu as pltpu
from jax.sharding import PartitionSpec as P

f32 = jnp.float32
bf16 = jnp.bfloat16
fine_low = 0.25
fine_high = 2.0
coarse_share = 0.125
SIDE = 16
LONG = 256
ROWS = SIDE + 6
RING = 24
VMEM = pl.BlockSpec(memory_space=pltpu.VMEM)
SMEM = pl.BlockSpec(memory_space=pltpu.SMEM)
LIMIT = 24 * 1024 * 1024


def factors(lower, upper):
    center = 0.5 * (upper + lower)
    radius = 0.5 * (upper - lower)
    aspect = center / radius
    p0 = 1.0 / aspect
    p1 = 1.0 / (2.0 * aspect - p0)
    p2 = 1.0 / (2.0 * aspect - p1)
    return center, p1 * p0, 2.0 * p1 / radius, p2 * p1, 2.0 * p2 / radius


FINE = factors(fine_low, fine_high)


def iota(shape, axis):
    return lax.broadcasted_iota(jnp.int32, shape, axis)


def back(values, axis):
    return pltpu.roll(values, 1, axis)


def ahead(values, axis):
    return pltpu.roll(values, values.shape[axis] - 1, axis)


def call(kernel, outs, scratch=(), ins=None):
    return pl.pallas_call(
        kernel,
        out_shape=[jax.ShapeDtypeStruct(s, f32) for s in outs],
        in_specs=ins,
        out_specs=[VMEM] * len(outs),
        scratch_shapes=list(scratch),
        compiler_params=pltpu.CompilerParams(vmem_limit_bytes=LIMIT),
    )


def pack_first(*refs):
    fields, pair, sems = refs[:5], refs[5:7], refs[7]
    even = lax.axis_index("coarse") % 2 == 0

    def fill(up, down):
        copies = []
        for n, field in enumerate(fields):
            first = 12 if n == 1 else 13
            at = UP_AT[n] + first - 13
            copies.append((field.at[first:16], up.at[at : at + 16 - first]))
            copies.append((field.at[0:3], down.at[3 * n : 3 * n + 3]))
        copies = [pltpu.make_async_copy(a, b, sems.at[k]) for k, (a, b) in enumerate(copies)]
        for copy in copies:
            copy.start()
        for copy in copies:
            copy.wait()

    @pl.when(even)
    def _():
        fill(*pair)

    @pl.when(jnp.logical_not(even))
    def _():
        fill(*pair[::-1])


def pack_first_call(fields):
    return pl.pallas_call(
        pack_first,
        out_shape=[jax.ShapeDtypeStruct((16, SIDE, LONG), f32)] * 2,
        in_specs=[pl.BlockSpec(memory_space=pltpu.HBM)] * 5,
        out_specs=[VMEM] * 2,
        scratch_shapes=[pltpu.SemaphoreType.DMA((10,))],
    )(*fields)


UP_AT = (0, 4, 7, 10, 13)


def sum_lanes(last_only):
    cell, lane = iota((LONG, 128), 0), iota((LONG, 128), 1)
    hit = cell // 4 == lane
    if last_only:
        hit = hit & (cell % 4 == 3)
    return hit.astype(bf16)


def sum_rows(last_only):
    block, cell = iota((8, SIDE), 0), iota((8, SIDE), 1)
    hit = cell // 4 == block
    if last_only:
        hit = hit & (cell % 4 == 3)
    return hit.astype(bf16)


def parts_of(values):
    first = values.astype(bf16)
    rest = values - first.astype(f32)
    second = rest.astype(bf16)
    return first, second, (rest - second.astype(f32)).astype(bf16)


def by_right(values, choose):
    return sum(jnp.dot(p, choose, preferred_element_type=f32) for p in parts_of(values))


def by_left(choose, values):
    return sum(jnp.dot(choose, p, preferred_element_type=f32) for p in parts_of(values))


def coarsen(cx, cy, cz, ab, active, out, mask):
    lanes, last = sum_lanes(False), sum_lanes(True)
    rows, lastrow = sum_rows(False), sum_rows(True)

    def coarse(n, part, left, right):
        total = by_right(jnp.concatenate([part(4 * a) for a in range(4)], axis=0), right)
        for a in range(4):
            out[n, a] = by_left(left, total[SIDE * a : SIDE * a + SIDE])

    def layers(ref):
        return lambda x: (ref[x] + ref[x + 1]) + (ref[x + 2] + ref[x + 3])

    coarse(0, lambda x: cx[x + 3], rows, lanes)
    coarse(1, layers(cy), lastrow, lanes)
    coarse(2, layers(cz), rows, last)
    coarse(3, layers(ab), rows, lanes)
    spread = ((iota((16, 128), 1) // 4) == iota((16, 128), 0)).astype(bf16)
    line = jnp.broadcast_to(active[0].astype(f32), (8, 16)).astype(bf16)
    mask[...] = jnp.dot(line, spread, preferred_element_type=f32)


def diagonal(cx_i, cxl_i, cy_i, cz_i, ab_i):
    row, lane = iota((SIDE, LONG), 0), iota((SIDE, LONG), 1)
    g = cx_i + cxl_i + cy_i + cz_i + ab_i
    g = g + jnp.where(row == 0, 0.0, back(cy_i, 0))
    return g + jnp.where(lane == 0, 0.0, back(cz_i, 1))


def strips(src_i, cx_i, cy_i, cz_i, g, inside, beyond=None):
    start = jnp.where(inside, src_i / (FINE[0] * g), 0.0)
    pieces = (src_i, cx_i, cy_i, cz_i, g)
    third = cy_i[13:14] if beyond is None else beyond[15:16]
    top = jnp.concatenate([p[14:16] for p in pieces] + [start[13:14], third], axis=0)
    bottom = jnp.concatenate([p[0:2] for p in pieces] + [start[2:3], start[2:3]], axis=0)
    return top, bottom


def pack_inner(flags, src, cx, cy, cz, ab, diag, first, second):
    even = flags[4] > 0
    for x in range(1, SIDE):
        g = diagonal(cx[x], cx[x - 1], cy[x], cz[x], ab[x])
        diag[x] = g
        top, bottom = strips(src[x], cx[x], cy[x], cz[x], g, True)
        at = (x - 1) % 8, pl.ds(12 * ((x - 1) // 8), 12)
        first[at] = jnp.where(even, top, bottom)
        second[at] = jnp.where(even, bottom, top)


def pack_outer(flags, src, cx, cy, cz, ab, one, two, diag, first, second):
    even = flags[4] > 0
    has_low, has_high = flags[0] > 0, flags[1] > 0
    low, high = sides(one, two, flags[5] > 0, has_low, has_high)
    layers = []
    for k in range(3):
        f = [low(UP_AT[n] + k) for n in range(5)]
        layers.append((f, low(3 + k), has_low, low(UP_AT[2]) if k == 1 else None))
    layers.append(([ref[0] for ref in (src, cx, cy, cz, ab)], low(6), True, None))
    for k in range(3):
        f = [high(3 * n + k) for n in range(5)]
        before = cx[15] if k == 0 else high(3 + k - 1)
        layers.append((f, before, has_high, high(8) if k == 1 else None))
    for k, (f, before, inside, beyond) in enumerate(layers):
        g = diagonal(f[1], before, *f[2:])
        diag[k] = g
        if 1 <= k < 6:
            top, bottom = strips(*f[:4], g, inside, beyond)
            at = (k - 1) % 3, pl.ds(12 * ((k - 1) // 3), 12)
            first[at] = jnp.where(even, top, bottom)
            second[at] = jnp.where(even, bottom, top)


def sides(one, two, even, has_low, has_high):
    keep_low, keep_high = has_low.astype(f32), has_high.astype(f32)

    def low(*at):
        return jnp.where(even, two[at], one[at]) * keep_low

    def high(*at):
        return jnp.where(even, one[at], two[at]) * keep_high

    return low, high


def near(i, u, cx, cy, cz):
    here = u[i]
    cy_i, cz_i = cy[i], cz[i]
    total = cx[i] * u[i + 1] + cx[i - 1] * u[i - 1]
    total = total + (cy_i * ahead(here, 0) + back(cy_i * here, 0))
    return total + (cz_i * ahead(here, 1) + back(cz_i * here, 1))


def join(layers):
    total = layers[0]
    for k, v in enumerate(layers[1:], 1):
        v = pltpu.roll(v, 64, 1) if k >= 2 else v
        total = total + (pltpu.roll(v, 4, 0) if k % 2 else v)
    return total


class Layers:
    def __init__(self, inner, outer=None):
        self.inner, self.outer = inner, outer

    def __getitem__(self, i):
        if 4 <= i < 19:
            return self.inner[i - 4]
        return self.outer[i if i < 4 else i - 15]

    def __setitem__(self, i, value):
        self.inner[i - 4] = value


class Over(dict):
    def __init__(self, inner, rows=None):
        self.inner, self.rows = inner, rows

    def __missing__(self, i):
        return self.inner[i - 4 if self.rows is None else self.rows[i]]


def own_layer(x, inner, outer, first, last, skip):
    return inner[x - first] if first <= x <= last else outer[x if x < first else x - skip]


def ring_layer(fields, g, lo, hi, hit, face=None):
    src_i, cx_i, cy_i, cz_i = fields
    row, lane = iota((RING, LONG), 0), iota((RING, LONG), 1)
    none1, none4 = jnp.zeros((1, LONG), f32), jnp.zeros((4, LONG), f32)

    def ring(own, n):
        return jnp.concatenate([own, hi[2 * n : 2 * n + 2], none4, lo[2 * n : 2 * n + 2]], axis=0)

    src_r, cx_r, cz_r, g = ring(src_i, 0), ring(cx_i, 1), ring(cz_i, 3), ring(g, 4)
    cy_r = jnp.concatenate([cy_i, hi[4:6], none1, none1, none1, lo[11:12], lo[4:6]], axis=0)
    if face is not None:
        cy_r = jnp.where(row == 23, face, cy_r)
    g = g + jnp.where((row == 0) | (row == 16), back(cy_r, 0), 0.0)
    inv = jnp.where(hit, 1.0 / g, 0.0)
    u = src_r * inv * (1.0 / FINE[0])
    u = jnp.where(row == 18, hi[10:11], u)
    u = jnp.where(row == 21, lo[10:11], u)
    return cx_r, cy_r, jnp.where(lane == LONG - 1, 0.0, cz_r), g, inv, src_r, u


def inside_ring(flags):
    row = iota((RING, LONG), 0)
    return (row < 16) | ((row < 18) & (flags[3] > 0)) | ((row >= 22) & (flags[2] > 0))


EDGE_ROWS = ((4, 5, 6, 16, 17, 18), (4, 5, 17, 18), (5, 6, 16, 17), (6, 7, 15, 16))
EDGES = [{i: k + sum(map(len, EDGE_ROWS[:n])) for k, i in enumerate(v)} for n, v in enumerate(EDGE_ROWS)]


def smooth_inner(
    flags, src, cx, cy, cz, diag, one, two,
    cx_o, cy_o, cz_o, g_o, inv_o, edge, iterate, resid, u0, u1, u2, r,
):
    center, m1, q1, m2, q2 = FINE
    left, right = sides(one, two, flags[4] > 0, flags[2] > 0, flags[3] > 0)
    hit = inside_ring(flags)
    made = [Layers(ref) for ref in (cx_o, cy_o, cz_o, g_o, inv_o, r, u0)]
    u1, u2 = Layers(u1), Layers(u2)
    for i in range(4, 19):
        x, at = i - 3, ((i - 4) % 8, pl.ds(12 * ((i - 4) // 8), 12))
        fields = src[x], cx[x], cy[x], cz[x]
        for out, value in zip(made, ring_layer(fields, diag[x], left(*at), right(*at), hit)):
            out[i] = value
    cx, cy, cz, g, inv, r, u0 = made
    for i in range(5, 18):
        u = u0[i]
        v = r[i] - (g[i] * u - near(i, u0, cx, cy, cz))
        r[i] = v
        u1[i] = m1 * u + q1 * (inv[i] * v)
    for i in range(6, 17):
        u = u1[i]
        v = r[i] - (g[i] * u - near(i, u1, cx, cy, cz))
        r[i] = v
        v = m2 * u + q2 * (inv[i] * v)
        u2[i] = v
        iterate[i - 6] = (u0[i] + u + v)[:SIDE]
    for values, rows in zip((r, u0, u1, u2), EDGES):
        for i, at in rows.items():
            edge[at] = values[i]
    for i in range(7, 16):
        resid[i - 7] = (r[i] - (g[i] * u2[i] - near(i, u2, cx, cy, cz)))[:SIDE]


def smooth_outer(
    flags, src, cx, cy, cz, one_x, two_x, diag, one, two, coarse, active,
    cx_i, cy_i, cz_i, g_i, inv_i, edge, resid_i,
    cx_o, cy_o, cz_o, g_o, inv_o, iterate, resid, packed, weight, first, second,
):
    center, m1, q1, m2, q2 = FINE
    has_low, has_high = flags[0] > 0, flags[1] > 0
    low, high = sides(one_x, two_x, flags[5] > 0, has_low, has_high)
    left, right = sides(one, two, flags[4] > 0, flags[2] > 0, flags[3] > 0)
    hit = inside_ring(flags)
    own_row = iota((RING, LONG), 0) < SIDE
    none12 = jnp.zeros((12, LONG), f32)
    layers = [([low(UP_AT[n] + k) for n in range(4)], has_low) for k in range(3)]
    layers.append(([ref[0] for ref in (src, cx, cy, cz)], True))
    layers += [([high(3 * n + k) for n in range(4)], has_high) for k in range(3)]
    made = [Over(ref) for ref in (cx_i, cy_i, cz_i, g_i, inv_i)]
    made += [Over(edge, EDGES[0]), Over(edge, EDGES[1])]
    for k, (fields, inside) in enumerate(layers):
        lo, hi, face = none12, none12, None
        if 1 <= k < 6:
            at = (k - 1) % 3, pl.ds(12 * ((k - 1) // 3), 12)
            lo, hi, here = left(*at), right(*at), hit & inside
        else:
            dst, at = (0, 0) if k == 0 else (1, 12)
            face, here = left(dst, pl.ds(at, 12))[11:12], hit & inside & own_row
        values = ring_layer(fields, diag[k], lo, hi, here, face)
        for out, value in zip(made, values):
            out[k if k < 4 else k + 15] = value
        for out, value in zip((cx_o, cy_o, cz_o, g_o, inv_o), values):
            out[k] = value
    cx, cy, cz, g, inv, r, u0 = made
    u1, u2 = Over(edge, EDGES[2]), Over(edge, EDGES[3])

    lanes, rows = sum_lanes(False), sum_rows(False)
    crow, clane = iota((8, 128), 0), iota((8, 128), 1)
    own = (crow < 4) & (clane < 64)
    mask = active[...]
    tails = [sum(cy[4 * a + 3 + k][SIDE:] for k in range(4)) for a in range(4)]
    below = by_right(jnp.concatenate([cx[2][:SIDE]] + tails, axis=0), lanes)
    below_x = by_left(rows, below[:SIDE])
    inverse, uppers, tiles = [], [], []
    for a in range(4):
        below_y = back(below[SIDE + 8 * a : SIDE + 8 * a + 8], 0)
        cx_c, cy_c, cz_c, ab_c = (coarse[n, a] for n in range(4))
        total = cx_c + cy_c + cz_c + ab_c + back(cz_c, 1)
        total = total + (below_x if a == 0 else coarse[0, a - 1])
        total = total + jnp.where(crow == 0, below_y, back(cy_c, 0))
        weight[a] = jnp.where(own, total, 0.0)
        inverse.append(jnp.where(own, mask / jnp.where(own, total, 1.0), 0.0))
        lower = cx_c + pltpu.roll(cy_c, 64, 1)
        tiles.append(pltpu.roll(inverse[a], 64, 1) + pltpu.roll(lower, 4, 0))
        uppers.append(jnp.where(clane == 63, 0.0, cz_c))
    packed[4] = join(uppers)

    for i in (1, 2, 3, 4, 18, 19, 20):
        v = r[i] - (g[i] * u0[i] - near(i, u0, cx, cy, cz))
        r[i] = v
        u1[i] = m1 * u0[i] + q1 * (inv[i] * v)
    for i in (2, 3, 4, 5, 17, 18, 19):
        v = r[i] - (g[i] * u1[i] - near(i, u1, cx, cy, cz))
        r[i] = v
        u2[i] = m2 * u1[i] + q2 * (inv[i] * v)
    for k, i in enumerate((3, 4, 5, 17, 18)):
        iterate[k] = (u0[i] + u1[i] + u2[i])[:SIDE]
    edges = {}
    for k, i in enumerate((3, 4, 5, 6, 16, 17, 18)):
        edges[i - 3] = (r[i] - (g[i] * u2[i] - near(i, u2, cx, cy, cz)))[:SIDE]
        resid[k] = edges[i - 3]
    even = flags[5] > 0
    rest = [edges[x] if x in edges else resid_i[x - 4] for x in range(SIDE)]
    totals = [(rest[x] + rest[x + 1]) + (rest[x + 2] + rest[x + 3]) for x in range(0, SIDE, 4)]

    for k in range(2):
        up, down = edges[14 + k], edges[k]
        for n in range(4):
            ys, zs = 8 * (n // 2), 128 * (n % 2)
            p, q = up[ys : ys + 8, zs : zs + 128], down[ys : ys + 8, zs : zs + 128]
            first[4 * k + n] = jnp.where(even, p, q)
            second[4 * k + n] = jnp.where(even, q, p)
    rhs = by_right(jnp.concatenate(totals, axis=0), lanes)
    for a in range(4):
        tiles[a] = tiles[a] + inverse[a] * by_left(rows, rhs[SIDE * a : SIDE * a + SIDE])
        packed[a] = tiles[a]
    ups, downs = tiles[1:4] + [join(uppers[1:4])], tiles[0:3] + [join(uppers[0:3])]
    for k, (p, q) in enumerate(zip(ups, downs)):
        first[8 + k] = jnp.where(even, p, q)
        second[8 + k] = jnp.where(even, q, p)


def pack_third(flags, resid_i, resid_o, packed, one_x, two_x, first, second):
    even = flags[4] > 0
    low, high = sides(one_x, two_x, flags[5] > 0, flags[0] > 0, flags[1] > 0)

    def edges(x):
        if x < 0 or x >= SIDE:
            get, k = (low, x + 2) if x < 0 else (high, x - SIDE)
            halves = [[get(4 * k + 2 * h + c) for c in range(2)] for h in range(2)]
            return [half[0:2] for half in halves[0]], [half[6:8] for half in halves[1]]
        mine = own_layer(x, resid_i, resid_o, 4, 12, 9)
        halves = [mine[:, 128 * c : 128 * c + 128] for c in range(2)]
        return [half[0:2] for half in halves], [half[14:16] for half in halves]

    for n in range(5):
        parts = [edges(4 * n - 2 + k) for k in range(4)]
        for c in range(2):
            bottom = jnp.concatenate([p[0][c] for p in parts], axis=0)
            top = jnp.concatenate([p[1][c] for p in parts], axis=0)
            first[2 * n + c] = jnp.where(even, top, bottom)
            second[2 * n + c] = jnp.where(even, bottom, top)
    tiles = [low(8 + a) for a in range(3)] + [packed[a] for a in range(4)] + [high(8 + a) for a in range(3)]
    for a, tile in enumerate(tiles + [low(11), packed[4], high(11)]):
        first[10 + a] = tile
        second[10 + a] = tile


def krylov(flags, packed, weight, one_x, two_x, one, two, basis, message, ext, t1s):
    low, high = sides(one_x, two_x, flags[5] > 0, flags[0] > 0, flags[1] > 0)
    left, right = sides(one, two, flags[4] > 0, flags[2] > 0, flags[3] > 0)
    crow, clane = iota((8, 128), 0), iota((8, 128), 1)
    own = (crow < 4) & (clane < 64)

    def unpack(tiles, a):
        turned = pltpu.roll(tiles[a], 4, 0)
        five = [tiles[a], pltpu.roll(tiles[a], 64, 1), turned, pltpu.roll(turned, 64, 1)]
        group, k = (0, a) if a < 3 else (1, a - 3) if a < 7 else (2, a - 7)
        upper = tiles[10 + group]
        upper = pltpu.roll(upper, 4, 0) if k % 2 else upper
        five.append(pltpu.roll(upper, 64, 1) if k >= 2 else upper)
        return [jnp.where(own, v, 0.0) for v in five]

    mine = [low(8 + a) for a in range(3)] + [packed[a] for a in range(4)] + [high(8 + a) for a in range(3)]
    mine = mine + [low(11), packed[4], high(11)]
    previous, following = [left(10 + a) for a in range(13)], [right(10 + a) for a in range(13)]
    for a in range(10):
        here, before, after = unpack(mine, a), unpack(previous, a), unpack(following, a)
        for n in range(5):
            ext[n, a, 0:8] = here[n] + pltpu.roll(after[n], 4, 0)
            ext[n, a, 8:16] = pltpu.roll(before[n], 4, 0)

    z, inv, cx, cy, cz = (ext.at[n] for n in range(5))
    for a in range(1, 9):
        t1s[a] = z[a] - inv[a] * near(a, z, cx, cy, cz)
    for a in range(2, 8):
        t1 = t1s[a]
        basis[0, a - 2] = z[a]
        basis[1, a - 2] = t1
        basis[2, a - 2] = t1 - inv[a] * near(a, t1s, cx, cy, cz)

    def total(parts):
        return jnp.sum(sum(parts), keepdims=True)

    g = [weight[a] for a in range(4)]
    v0, v1, v2 = ([basis[n, a + 1, 0:8] for a in range(4)] for n in range(3))
    s00 = total([w * p * p for w, p in zip(g, v0)])
    s01 = total([w * p * q for w, p, q in zip(g, v0, v1)])
    alpha = jnp.where(s00 > 0, s01 / jnp.where(s00 > 0, s00, 1.0), 0.0)
    e = [q - alpha * p for p, q in zip(v0, v1)]
    te = [q - alpha * p for p, q in zip(v1, v2)]
    terms = [
        total([w * p * p for w, p in zip(g, e)]),
        2.0 * total([w * p * q for w, p, q in zip(g, e, v0)]),
        s00,
        total([w * p * q for w, p, q in zip(g, e, te)]),
        total([w * (p * q + r * t) for w, p, q, r, t in zip(g, v0, te, e, v1)]),
        s01,
    ]
    lane = iota((8, 128), 1)
    line = jnp.where(lane < 64, 0.0, alpha)
    for n, term in enumerate(terms):
        line = jnp.where(lane == n, term, line)
    message[...] = jnp.broadcast_to(line[0:1], (256, 128))


def finish(
    flags, gathered, basis, cx_i, cy_i, cz_i, g_i, inv_i, cx_o, cy_o, cz_o, g_o, inv_o,
    resid_i, resid_o, iterate_i, iterate_o, one_x, two_x, one, two,
    out, correction, lift, u0, u1, r0,
):
    center, m1, q1, m2, q2 = FINE
    low, high = sides(one_x, two_x, flags[5] > 0, flags[0] > 0, flags[1] > 0)
    left, right = sides(one, two, flags[4] > 0, flags[2] > 0, flags[3] > 0)

    pairs = (cx_i, cx_o), (cy_i, cy_o), (cz_i, cz_o), (g_i, g_o), (inv_i, inv_o)
    cx, cy, cz, g, inv = (Layers(*pair) for pair in pairs)

    lines = gathered[...]
    lane1 = iota((1, 128), 1)
    sums = jnp.sum(lines, axis=0, keepdims=True)

    def pick(values, first, count):
        hit = (lane1 >= first) & (lane1 < first + count)
        return jnp.sum(jnp.where(hit, values, 0.0), axis=1, keepdims=True)

    norm = pick(sums, 2, 1)
    a1 = pick(sums, 5, 1) / norm
    shift = pltpu.roll(lines, 64, 1) - a1
    plain, linear, quadratic = (((lane1 == k) | (lane1 == k + 3)).astype(f32) for k in range(3))
    power = plain + shift * (linear + shift * quadratic)
    sums = jnp.sum(lines * power, axis=0, keepdims=True)
    square, energy = pick(sums, 0, 3), pick(sums, 3, 3)
    bound = jnp.maximum(a1, energy / square) + jnp.sqrt(square / norm)
    middle, k1, h1, k2, h2 = factors(coarse_share, 1.0)
    scale = 1.0 / bound
    v0, h1, h2 = scale * (1.0 / middle), scale * h1, scale * h2
    v1 = (k1 * v0 + h1, -h1 * v0)
    v2 = (k2 * v1[0] + h2, k2 * v1[1] - h2 * (v0 + v1[0]), -h2 * v1[1])
    weights = (v0 + v1[0] + v2[0], v1[1] + v2[1], v2[2])

    upper = iota((8, 128), 0) < 4
    tall = []
    for a in range(6):
        field = weights[0] * basis[0, a] + weights[1] * basis[1, a] + weights[2] * basis[2, a]
        if 1 <= a <= 4:
            correction[a - 1] = field[0:4, 0:64]
        for p, q in ((0, 1), (2, 3), (4, 15)):
            p, q = (jnp.broadcast_to(field[k : k + 1], (8, 128)) for k in (p, q))
            tall.append(jnp.where(upper, p, q))
    lanes = (iota((128, LONG), 1) // 4 == iota((128, LONG), 0)).astype(bf16)
    fine = by_right(jnp.concatenate(tall, axis=0), lanes)
    lifted = [fine[RING * a : RING * a + RING] for a in range(6)]
    for i in range(ROWS):
        lift[i] = lifted[(i + 1) // 4]

    none4 = jnp.zeros((4, LONG), f32)

    def strip(get, x):
        n, k = x // 4, x % 4
        return jnp.concatenate([get(2 * n + c, pl.ds(2 * k, 2)) for c in range(2)], axis=1)

    for i in range(1, ROWS - 1):
        x = i - 1
        if x < 2 or x >= 18:
            get, k = (low, x) if x < 2 else (high, x - 18)
            halves = [
                jnp.concatenate([get(4 * k + 2 * h + c) for c in range(2)], axis=1) for h in range(2)
            ]
            mine = jnp.concatenate(halves, axis=0)
        else:
            mine = own_layer(x - 2, resid_i, resid_o, 4, 12, 9)
        r0[i] = jnp.concatenate([mine, strip(right, x), none4, strip(left, x)], axis=0)

    for i in range(1, ROWS - 1):
        r = r0[i] - (g[i] * lift[i] - near(i, lift, cx, cy, cz))
        r0[i] = r
        u0[i] = inv[i] * r * (1.0 / center)

    for i in range(2, ROWS - 2):
        u = u0[i]
        r = r0[i] - (g[i] * u - near(i, u0, cx, cy, cz))
        r0[i] = r
        u1[i] = m1 * u + q1 * (inv[i] * r)

    for i in range(3, 19):
        u = u1[i]
        r = r0[i] - (g[i] * u - near(i, u1, cx, cy, cz))
        step = (u0[i] + u) + (m2 * u + q2 * (inv[i] * r)) + lift[i]
        out[i - 3] = own_layer(i - 3, iterate_i, iterate_o, 3, 13, 11) + step[:SIDE]


def swap(values, axis, odd):
    count = lax.axis_size(axis)
    other = [(i ^ 1) if not odd else (((i + 1) ^ 1) - 1) % count for i in range(count)]
    return lax.ppermute(values, axis, list(enumerate(other)))


def body(src, cx, cy, cz, ab, active):
    ix, iy = lax.axis_index("coarse"), lax.axis_index("fine")
    nx, ny = lax.axis_size("coarse"), lax.axis_size("fine")
    flags = jnp.stack([ix > 0, ix < nx - 1, iy > 0, iy < ny - 1, iy % 2 == 0, ix % 2 == 0]).astype(jnp.int32)
    block, ring = (SIDE, SIDE, LONG), pltpu.VMEM((ROWS, RING, LONG), f32)

    first, second = pack_first_call((src, cx, cy, cz, ab))
    one_x, two_x = swap(first, "coarse", False), swap(second, "coarse", True)
    coarse, mask = call(coarsen, [(4, 4, 8, 128), (8, 128)], ins=[VMEM] * 5)(cx, cy, cz, ab, active)
    diag, first, second = call(
        pack_inner, [block, (8, 24, LONG), (8, 24, LONG)], ins=[SMEM] + [VMEM] * 5
    )(flags, src, cx, cy, cz, ab)
    one, two = swap(first, "fine", False), swap(second, "fine", True)
    diag_out, first, second = call(
        pack_outer, [(7, SIDE, LONG), (3, 24, LONG), (3, 24, LONG)], ins=[SMEM] + [VMEM] * 7
    )(flags, src, cx, cy, cz, ab, one_x, two_x)
    one_out, two_out = swap(first, "fine", False), swap(second, "fine", True)
    inner, outer = (15, RING, LONG), (7, RING, LONG)
    *fields_i, edge, iterate_i, resid_i = call(
        smooth_inner,
        [inner] * 5 + [(18, RING, LONG), (11, SIDE, LONG), (9, SIDE, LONG)],
        [pltpu.VMEM(inner, f32)] * 4,
        ins=[SMEM] + [VMEM] * 7,
    )(flags, src, cx, cy, cz, diag, one, two)
    *fields_o, iterate_o, resid_o, packed, weight, first, second = call(
        smooth_outer,
        [outer] * 5 + [(5, SIDE, LONG), (7, SIDE, LONG)]
        + [(5, 8, 128), (4, 8, 128), (12, 8, 128), (12, 8, 128)],
        ins=[SMEM] + [VMEM] * 18,
    )(
        flags, src, cx, cy, cz, one_x, two_x, diag_out, one_out, two_out, coarse, mask,
        *fields_i, edge, resid_i,
    )
    one_x, two_x = swap(first, "coarse", False), swap(second, "coarse", True)
    first, second = call(pack_third, [(23, 8, 128)] * 2, ins=[SMEM] + [VMEM] * 5)(
        flags, resid_i, resid_o, packed, one_x, two_x
    )
    one, two = swap(first, "fine", False), swap(second, "fine", True)
    count = nx * ny
    basis, message = call(
        krylov,
        [(3, 6, 16, 128), (256, 128)],
        [pltpu.VMEM((5, 10, 16, 128), f32), pltpu.VMEM((10, 16, 128), f32)],
        ins=[SMEM] + [VMEM] * 6,
    )(flags, packed, weight, one_x, two_x, one, two)
    gathered = lax.all_to_all(message[:count], ("coarse", "fine"), 0, 0, tiled=True)
    out, correction = call(
        finish,
        [block, (4, 4, 64)],
        [ring] * 4,
        ins=[SMEM] + [VMEM] * 20,
    )(
        flags, gathered, basis, *fields_i, *fields_o, resid_i, resid_o, iterate_i, iterate_o,
        one_x, two_x, one, two,
    )
    return (out, correction)


def solution(mesh):
    spec = P("coarse", "fine", None)
    return jax.shard_map(
        body, mesh=mesh, in_specs=(spec,) * 6, out_specs=(spec,) * 2, check_vma=False
    )
```

```python
import jax
import jax.numpy as jnp
from jax import lax
from jax.experimental import pallas as pl
from jax.experimental.pallas import tpu as pltpu
from jax.sharding import PartitionSpec as P

f32 = jnp.float32
bf16 = jnp.bfloat16
fine_low = 0.25
fine_high = 2.0
coarse_share = 0.125
SIDE = 16
LONG = 256
ROWS = SIDE + 6
RING = 24
VMEM = pl.BlockSpec(memory_space=pltpu.VMEM)
SMEM = pl.BlockSpec(memory_space=pltpu.SMEM)
LIMIT = 24 * 1024 * 1024


def factors(lower, upper):
    center = 0.5 * (upper + lower)
    radius = 0.5 * (upper - lower)
    aspect = center / radius
    p0 = 1.0 / aspect
    p1 = 1.0 / (2.0 * aspect - p0)
    p2 = 1.0 / (2.0 * aspect - p1)
    return center, p1 * p0, 2.0 * p1 / radius, p2 * p1, 2.0 * p2 / radius


FINE = factors(fine_low, fine_high)


def iota(shape, axis):
    return lax.broadcasted_iota(jnp.int32, shape, axis)


def back(values, axis):
    return pltpu.roll(values, 1, axis)


def ahead(values, axis):
    return pltpu.roll(values, values.shape[axis] - 1, axis)


def call(kernel, outs, scratch=(), ins=None):
    return pl.pallas_call(
        kernel,
        out_shape=[jax.ShapeDtypeStruct(s, f32) for s in outs],
        in_specs=ins,
        out_specs=[VMEM] * len(outs),
        scratch_shapes=list(scratch),
        compiler_params=pltpu.CompilerParams(vmem_limit_bytes=LIMIT),
    )


def pack_first(*refs):
    fields, pair, sems = refs[:5], refs[5:7], refs[7]
    even = lax.axis_index("coarse") % 2 == 0

    def fill(up, down):
        copies = []
        for n, field in enumerate(fields):
            first = 12 if n == 1 else 13
            at = UP_AT[n] + first - 13
            copies.append((field.at[first:16], up.at[at : at + 16 - first]))
            copies.append((field.at[0:3], down.at[3 * n : 3 * n + 3]))
        copies = [pltpu.make_async_copy(a, b, sems.at[k]) for k, (a, b) in enumerate(copies)]
        for copy in copies:
            copy.start()
        for copy in copies:
            copy.wait()

    @pl.when(even)
    def _():
        fill(*pair)

    @pl.when(jnp.logical_not(even))
    def _():
        fill(*pair[::-1])


def pack_first_call(fields):
    return pl.pallas_call(
        pack_first,
        out_shape=[jax.ShapeDtypeStruct((16, SIDE, LONG), f32)] * 2,
        in_specs=[pl.BlockSpec(memory_space=pltpu.HBM)] * 5,
        out_specs=[VMEM] * 2,
        scratch_shapes=[pltpu.SemaphoreType.DMA((10,))],
    )(*fields)


UP_AT = (0, 4, 7, 10, 13)


def sum_lanes(last_only):
    cell, lane = iota((LONG, 128), 0), iota((LONG, 128), 1)
    hit = cell // 4 == lane
    if last_only:
        hit = hit & (cell % 4 == 3)
    return hit.astype(bf16)


def sum_rows(last_only):
    block, cell = iota((8, SIDE), 0), iota((8, SIDE), 1)
    hit = cell // 4 == block
    if last_only:
        hit = hit & (cell % 4 == 3)
    return hit.astype(bf16)


def parts_of(values):
    first = values.astype(bf16)
    rest = values - first.astype(f32)
    second = rest.astype(bf16)
    return first, second, (rest - second.astype(f32)).astype(bf16)


def by_right(values, choose):
    return sum(jnp.dot(p, choose, preferred_element_type=f32) for p in parts_of(values))


def by_left(choose, values):
    return sum(jnp.dot(choose, p, preferred_element_type=f32) for p in parts_of(values))


def coarsen(cx, cy, cz, ab, active, out, mask):
    lanes, last = sum_lanes(False), sum_lanes(True)
    rows, lastrow = sum_rows(False), sum_rows(True)

    def coarse(n, part, left, right):
        total = by_right(jnp.concatenate([part(4 * a) for a in range(4)], axis=0), right)
        for a in range(4):
            out[n, a] = by_left(left, total[SIDE * a : SIDE * a + SIDE])

    def layers(ref):
        return lambda x: (ref[x] + ref[x + 1]) + (ref[x + 2] + ref[x + 3])

    coarse(0, lambda x: cx[x + 3], rows, lanes)
    coarse(1, layers(cy), lastrow, lanes)
    coarse(2, layers(cz), rows, last)
    coarse(3, layers(ab), rows, lanes)
    spread = ((iota((16, 128), 1) // 4) == iota((16, 128), 0)).astype(bf16)
    line = jnp.broadcast_to(active[0].astype(f32), (8, 16)).astype(bf16)
    mask[...] = jnp.dot(line, spread, preferred_element_type=f32)


def diagonal(cx_i, cxl_i, cy_i, cz_i, ab_i):
    row, lane = iota((SIDE, LONG), 0), iota((SIDE, LONG), 1)
    g = cx_i + cxl_i + cy_i + cz_i + ab_i
    g = g + jnp.where(row == 0, 0.0, back(cy_i, 0))
    return g + jnp.where(lane == 0, 0.0, back(cz_i, 1))


def strips(src_i, cx_i, cy_i, cz_i, g, inside, beyond=None):
    start = jnp.where(inside, src_i / (FINE[0] * g), 0.0)
    pieces = (src_i, cx_i, cy_i, cz_i, g)
    third = cy_i[13:14] if beyond is None else beyond[15:16]
    top = jnp.concatenate([p[14:16] for p in pieces] + [start[13:14], third], axis=0)
    bottom = jnp.concatenate([p[0:2] for p in pieces] + [start[2:3], start[2:3]], axis=0)
    return top, bottom


def pack_inner(flags, src, cx, cy, cz, ab, diag, first, second):
    even = flags[4] > 0
    for x in range(1, SIDE):
        g = diagonal(cx[x], cx[x - 1], cy[x], cz[x], ab[x])
        diag[x] = g
        top, bottom = strips(src[x], cx[x], cy[x], cz[x], g, True)
        at = (x - 1) % 8, pl.ds(12 * ((x - 1) // 8), 12)
        first[at] = jnp.where(even, top, bottom)
        second[at] = jnp.where(even, bottom, top)


def pack_outer(flags, src, cx, cy, cz, ab, one, two, diag, first, second):
    even = flags[4] > 0
    has_low, has_high = flags[0] > 0, flags[1] > 0
    low, high = sides(one, two, flags[5] > 0, has_low, has_high)
    layers = []
    for k in range(3):
        f = [low(UP_AT[n] + k) for n in range(5)]
        layers.append((f, low(3 + k), has_low, low(UP_AT[2]) if k == 1 else None))
    layers.append(([ref[0] for ref in (src, cx, cy, cz, ab)], low(6), True, None))
    for k in range(3):
        f = [high(3 * n + k) for n in range(5)]
        before = cx[15] if k == 0 else high(3 + k - 1)
        layers.append((f, before, has_high, high(8) if k == 1 else None))
    for k, (f, before, inside, beyond) in enumerate(layers):
        g = diagonal(f[1], before, *f[2:])
        diag[k] = g
        if 1 <= k < 6:
            top, bottom = strips(*f[:4], g, inside, beyond)
            at = (k - 1) % 3, pl.ds(12 * ((k - 1) // 3), 12)
            first[at] = jnp.where(even, top, bottom)
            second[at] = jnp.where(even, bottom, top)


def sides(one, two, even, has_low, has_high):
    keep_low, keep_high = has_low.astype(f32), has_high.astype(f32)

    def low(*at):
        return jnp.where(even, two[at], one[at]) * keep_low

    def high(*at):
        return jnp.where(even, one[at], two[at]) * keep_high

    return low, high


def near(i, u, cx, cy, cz):
    here = u[i]
    cy_i, cz_i = cy[i], cz[i]
    total = cx[i] * u[i + 1] + cx[i - 1] * u[i - 1]
    total = total + (cy_i * ahead(here, 0) + back(cy_i * here, 0))
    return total + (cz_i * ahead(here, 1) + back(cz_i * here, 1))


def join(layers):
    total = layers[0]
    for k, v in enumerate(layers[1:], 1):
        v = pltpu.roll(v, 64, 1) if k >= 2 else v
        total = total + (pltpu.roll(v, 4, 0) if k % 2 else v)
    return total


class Layers:
    def __init__(self, inner, outer=None):
        self.inner, self.outer = inner, outer

    def __getitem__(self, i):
        if 4 <= i < 19:
            return self.inner[i - 4]
        return self.outer[i if i < 4 else i - 15]

    def __setitem__(self, i, value):
        self.inner[i - 4] = value


class Over(dict):
    def __init__(self, inner, rows=None):
        self.inner, self.rows = inner, rows

    def __missing__(self, i):
        return self.inner[i - 4 if self.rows is None else self.rows[i]]


def own_layer(x, inner, outer, first, last, skip):
    return inner[x - first] if first <= x <= last else outer[x if x < first else x - skip]


def ring_layer(fields, g, lo, hi, hit, face=None):
    src_i, cx_i, cy_i, cz_i = fields
    row, lane = iota((RING, LONG), 0), iota((RING, LONG), 1)
    none1, none4 = jnp.zeros((1, LONG), f32), jnp.zeros((4, LONG), f32)

    def ring(own, n):
        return jnp.concatenate([own, hi[2 * n : 2 * n + 2], none4, lo[2 * n : 2 * n + 2]], axis=0)

    src_r, cx_r, cz_r, g = ring(src_i, 0), ring(cx_i, 1), ring(cz_i, 3), ring(g, 4)
    cy_r = jnp.concatenate([cy_i, hi[4:6], none1, none1, none1, lo[11:12], lo[4:6]], axis=0)
    if face is not None:
        cy_r = jnp.where(row == 23, face, cy_r)
    g = g + jnp.where((row == 0) | (row == 16), back(cy_r, 0), 0.0)
    inv = jnp.where(hit, 1.0 / g, 0.0)
    u = src_r * inv * (1.0 / FINE[0])
    u = jnp.where(row == 18, hi[10:11], u)
    u = jnp.where(row == 21, lo[10:11], u)
    return cx_r, cy_r, jnp.where(lane == LONG - 1, 0.0, cz_r), g, inv, src_r, u


def inside_ring(flags):
    row = iota((RING, LONG), 0)
    return (row < 16) | ((row < 18) & (flags[3] > 0)) | ((row >= 22) & (flags[2] > 0))


EDGE_ROWS = ((4, 5, 6, 16, 17, 18), (4, 5, 17, 18), (5, 6, 16, 17), (6, 7, 15, 16))
EDGES = [{i: k + sum(map(len, EDGE_ROWS[:n])) for k, i in enumerate(v)} for n, v in enumerate(EDGE_ROWS)]


def smooth_inner(
    flags, src, cx, cy, cz, diag, one, two,
    cx_o, cy_o, cz_o, g_o, inv_o, edge, iterate, resid, u0, u1, u2, r,
):
    center, m1, q1, m2, q2 = FINE
    left, right = sides(one, two, flags[4] > 0, flags[2] > 0, flags[3] > 0)
    hit = inside_ring(flags)
    made = [Layers(ref) for ref in (cx_o, cy_o, cz_o, g_o, inv_o, r, u0)]
    u1, u2 = Layers(u1), Layers(u2)
    for i in range(4, 19):
        x, at = i - 3, ((i - 4) % 8, pl.ds(12 * ((i - 4) // 8), 12))
        fields = src[x], cx[x], cy[x], cz[x]
        for out, value in zip(made, ring_layer(fields, diag[x], left(*at), right(*at), hit)):
            out[i] = value
    cx, cy, cz, g, inv, r, u0 = made
    for i in range(5, 18):
        u = u0[i]
        v = r[i] - (g[i] * u - near(i, u0, cx, cy, cz))
        r[i] = v
        u1[i] = m1 * u + q1 * (inv[i] * v)
    for i in range(6, 17):
        u = u1[i]
        v = r[i] - (g[i] * u - near(i, u1, cx, cy, cz))
        r[i] = v
        v = m2 * u + q2 * (inv[i] * v)
        u2[i] = v
        iterate[i - 6] = (u0[i] + u + v)[:SIDE]
    for values, rows in zip((r, u0, u1, u2), EDGES):
        for i, at in rows.items():
            edge[at] = values[i]
    for i in range(7, 16):
        resid[i - 7] = (r[i] - (g[i] * u2[i] - near(i, u2, cx, cy, cz)))[:SIDE]


def smooth_outer(
    flags, src, cx, cy, cz, one_x, two_x, diag, one, two, coarse, active,
    cx_i, cy_i, cz_i, g_i, inv_i, edge, resid_i,
    cx_o, cy_o, cz_o, g_o, inv_o, iterate, resid, packed, weight, first, second,
):
    center, m1, q1, m2, q2 = FINE
    has_low, has_high = flags[0] > 0, flags[1] > 0
    low, high = sides(one_x, two_x, flags[5] > 0, has_low, has_high)
    left, right = sides(one, two, flags[4] > 0, flags[2] > 0, flags[3] > 0)
    hit = inside_ring(flags)
    own_row = iota((RING, LONG), 0) < SIDE
    none12 = jnp.zeros((12, LONG), f32)
    layers = [([low(UP_AT[n] + k) for n in range(4)], has_low) for k in range(3)]
    layers.append(([ref[0] for ref in (src, cx, cy, cz)], True))
    layers += [([high(3 * n + k) for n in range(4)], has_high) for k in range(3)]
    made = [Over(ref) for ref in (cx_i, cy_i, cz_i, g_i, inv_i)]
    made += [Over(edge, EDGES[0]), Over(edge, EDGES[1])]
    for k, (fields, inside) in enumerate(layers):
        lo, hi, face = none12, none12, None
        if 1 <= k < 6:
            at = (k - 1) % 3, pl.ds(12 * ((k - 1) // 3), 12)
            lo, hi, here = left(*at), right(*at), hit & inside
        else:
            dst, at = (0, 0) if k == 0 else (1, 12)
            face, here = left(dst, pl.ds(at, 12))[11:12], hit & inside & own_row
        values = ring_layer(fields, diag[k], lo, hi, here, face)
        for out, value in zip(made, values):
            out[k if k < 4 else k + 15] = value
        for out, value in zip((cx_o, cy_o, cz_o, g_o, inv_o), values):
            out[k] = value
    cx, cy, cz, g, inv, r, u0 = made
    u1, u2 = Over(edge, EDGES[2]), Over(edge, EDGES[3])

    lanes, rows = sum_lanes(False), sum_rows(False)
    crow, clane = iota((8, 128), 0), iota((8, 128), 1)
    own = (crow < 4) & (clane < 64)
    mask = active[...]
    tails = [sum(cy[4 * a + 3 + k][SIDE:] for k in range(4)) for a in range(4)]
    below = by_right(jnp.concatenate([cx[2][:SIDE]] + tails, axis=0), lanes)
    below_x = by_left(rows, below[:SIDE])
    inverse, uppers, tiles = [], [], []
    for a in range(4):
        below_y = back(below[SIDE + 8 * a : SIDE + 8 * a + 8], 0)
        cx_c, cy_c, cz_c, ab_c = (coarse[n, a] for n in range(4))
        total = cx_c + cy_c + cz_c + ab_c + back(cz_c, 1)
        total = total + (below_x if a == 0 else coarse[0, a - 1])
        total = total + jnp.where(crow == 0, below_y, back(cy_c, 0))
        weight[a] = jnp.where(own, total, 0.0)
        inverse.append(jnp.where(own, mask / jnp.where(own, total, 1.0), 0.0))
        lower = cx_c + pltpu.roll(cy_c, 64, 1)
        tiles.append(pltpu.roll(inverse[a], 64, 1) + pltpu.roll(lower, 4, 0))
        uppers.append(jnp.where(clane == 63, 0.0, cz_c))
    packed[4] = join(uppers)

    for i in (1, 2, 3, 4, 18, 19, 20):
        v = r[i] - (g[i] * u0[i] - near(i, u0, cx, cy, cz))
        r[i] = v
        u1[i] = m1 * u0[i] + q1 * (inv[i] * v)
    for i in (2, 3, 4, 5, 17, 18, 19):
        v = r[i] - (g[i] * u1[i] - near(i, u1, cx, cy, cz))
        r[i] = v
        u2[i] = m2 * u1[i] + q2 * (inv[i] * v)
    for k, i in enumerate((3, 4, 5, 17, 18)):
        iterate[k] = (u0[i] + u1[i] + u2[i])[:SIDE]
    edges = {}
    for k, i in enumerate((3, 4, 5, 6, 16, 17, 18)):
        edges[i - 3] = (r[i] - (g[i] * u2[i] - near(i, u2, cx, cy, cz)))[:SIDE]
        resid[k] = edges[i - 3]
    even = flags[5] > 0
    rest = [edges[x] if x in edges else resid_i[x - 4] for x in range(SIDE)]
    totals = [(rest[x] + rest[x + 1]) + (rest[x + 2] + rest[x + 3]) for x in range(0, SIDE, 4)]

    for k in range(2):
        up, down = edges[14 + k], edges[k]
        for n in range(4):
            ys, zs = 8 * (n // 2), 128 * (n % 2)
            p, q = up[ys : ys + 8, zs : zs + 128], down[ys : ys + 8, zs : zs + 128]
            first[4 * k + n] = jnp.where(even, p, q)
            second[4 * k + n] = jnp.where(even, q, p)
    rhs = by_right(jnp.concatenate(totals, axis=0), lanes)
    for a in range(4):
        tiles[a] = tiles[a] + inverse[a] * by_left(rows, rhs[SIDE * a : SIDE * a + SIDE])
        packed[a] = tiles[a]
    ups, downs = tiles[1:4] + [join(uppers[1:4])], tiles[0:3] + [join(uppers[0:3])]
    for k, (p, q) in enumerate(zip(ups, downs)):
        first[8 + k] = jnp.where(even, p, q)
        second[8 + k] = jnp.where(even, q, p)


def residual_strips(layers, even, first, second, at):
    for c in range(2):
        parts = [layer[c] for layer in layers]
        bottom = jnp.concatenate([head for head, _ in parts], axis=0)
        top = jnp.concatenate([tail for _, tail in parts], axis=0)
        first[at + c] = jnp.where(even, top, bottom)
        second[at + c] = jnp.where(even, bottom, top)


def pack_own(flags, resid_i, resid_o, packed, first, second):
    def halves(x):
        mine = own_layer(x, resid_i, resid_o, 4, 12, 9)
        return [(mine[0:2, at : at + 128], mine[14:16, at : at + 128]) for at in (0, 128)]

    for n in range(4):
        residual_strips([halves(4 * n + k) for k in range(4)], flags[4] > 0, first, second, 2 * n)
    for k in range(5):
        first[8 + k] = packed[k]
        second[8 + k] = packed[k]


def pack_halo(flags, one_x, two_x, first, second):
    low, high = sides(one_x, two_x, flags[5] > 0, flags[0] > 0, flags[1] > 0)

    def halves(get, k):
        return [(get(4 * k + c)[0:2], get(4 * k + 2 + c)[6:8]) for c in range(2)]

    layers = [halves(low, 0), halves(low, 1), halves(high, 0), halves(high, 1)]
    residual_strips(layers, flags[4] > 0, first, second, 0)
    for k, get in enumerate((low, high)):
        for a in range(4):
            at = 2 + 3 * k + a if a < 3 else 8 + k
            tile = get(8 + a)
            first[at] = tile
            second[at] = tile


def krylov(flags, packed, weight, one_x, two_x, one, two, one_out, two_out, basis, message, ext, t1s):
    low, high = sides(one_x, two_x, flags[5] > 0, flags[0] > 0, flags[1] > 0)
    left, right = sides(one, two, flags[4] > 0, flags[2] > 0, flags[3] > 0)
    left_out, right_out = sides(one_out, two_out, flags[4] > 0, flags[2] > 0, flags[3] > 0)
    crow, clane = iota((8, 128), 0), iota((8, 128), 1)
    top, thin = crow < 4, clane < 64

    def tiles(own, out):
        return [out(2 + a) for a in range(3)] + [own(8 + a) for a in range(4)] + [
            out(5 + a) for a in range(3)
        ] + [out(8), own(12), out(9)]

    mine = [low(8 + a) for a in range(3)] + [packed[a] for a in range(4)]
    mine += [high(8 + a) for a in range(3)] + [low(11), packed[4], high(11)]
    previous, following = tiles(left, left_out), tiles(right, right_out)

    def upper(field, a):
        group, k = (0, a) if a < 3 else (1, a - 3) if a < 7 else (2, a - 7)
        tile = field[10 + group]
        return (pltpu.roll(tile, 64, 1) if k >= 2 else tile), k % 2

    def turn(tile):
        return pltpu.roll(tile, 4, 0)

    for a in range(10):
        here, after, before = mine[a], following[a], previous[a]
        pairs = (
            (jnp.where(top, here, turn(after)), jnp.where(top, turn(here), after)),
            (jnp.where(top, 0.0, turn(before)), jnp.where(top, 0.0, before)),
        )
        (here, odd), (after, _), (before, _) = (upper(f, a) for f in (mine, following, previous))
        if odd:
            faces = jnp.where(top, turn(here), after), jnp.where(top, 0.0, before)
        else:
            faces = jnp.where(top, here, turn(after)), jnp.where(top, 0.0, turn(before))
        for n in range(2):
            at = pl.ds(8 * n, 8)
            for m in range(2):
                ext[2 * m, a, at] = jnp.where(thin, pairs[n][m], 0.0)
                ext[2 * m + 1, a, at] = jnp.where(thin, pltpu.roll(pairs[n][m], 64, 1), 0.0)
            ext[4, a, at] = jnp.where(thin, faces[n], 0.0)

    z, inv, cx, cy, cz = (ext.at[n] for n in range(5))
    for a in range(1, 9):
        t1s[a] = z[a] - inv[a] * near(a, z, cx, cy, cz)
    for a in range(2, 8):
        t1 = t1s[a]
        basis[0, a - 2] = z[a]
        basis[1, a - 2] = t1
        basis[2, a - 2] = t1 - inv[a] * near(a, t1s, cx, cy, cz)

    def total(parts):
        return jnp.sum(sum(parts), keepdims=True)

    g = [weight[a] for a in range(4)]
    v0, v1, v2 = ([basis[n, a + 1, 0:8] for a in range(4)] for n in range(3))
    s00 = total([w * p * p for w, p in zip(g, v0)])
    s01 = total([w * p * q for w, p, q in zip(g, v0, v1)])
    alpha = jnp.where(s00 > 0, s01 / jnp.where(s00 > 0, s00, 1.0), 0.0)
    e = [q - alpha * p for p, q in zip(v0, v1)]
    te = [q - alpha * p for p, q in zip(v1, v2)]
    terms = [
        total([w * p * p for w, p in zip(g, e)]),
        2.0 * total([w * p * q for w, p, q in zip(g, e, v0)]),
        s00,
        total([w * p * q for w, p, q in zip(g, e, te)]),
        total([w * (p * q + r * t) for w, p, q, r, t in zip(g, v0, te, e, v1)]),
        s01,
    ]
    lane = iota((8, 128), 1)
    line = jnp.where(lane < 64, 0.0, alpha)
    for n, term in enumerate(terms):
        line = jnp.where(lane == n, term, line)
    message[...] = jnp.broadcast_to(line[0:1], (256, 128))


def finish(
    flags, gathered, basis, cx_i, cy_i, cz_i, g_i, inv_i, cx_o, cy_o, cz_o, g_o, inv_o,
    resid_i, resid_o, iterate_i, iterate_o, one_x, two_x, one, two, one_out, two_out,
    out, correction, lift, u0, u1, r0,
):
    center, m1, q1, m2, q2 = FINE
    low, high = sides(one_x, two_x, flags[5] > 0, flags[0] > 0, flags[1] > 0)
    left, right = sides(one, two, flags[4] > 0, flags[2] > 0, flags[3] > 0)

    pairs = (cx_i, cx_o), (cy_i, cy_o), (cz_i, cz_o), (g_i, g_o), (inv_i, inv_o)
    cx, cy, cz, g, inv = (Layers(*pair) for pair in pairs)

    lines = gathered[...]
    lane1 = iota((1, 128), 1)
    sums = jnp.sum(lines, axis=0, keepdims=True)

    def pick(values, first, count):
        hit = (lane1 >= first) & (lane1 < first + count)
        return jnp.sum(jnp.where(hit, values, 0.0), axis=1, keepdims=True)

    norm = pick(sums, 2, 1)
    a1 = pick(sums, 5, 1) / norm
    shift = pltpu.roll(lines, 64, 1) - a1
    plain, linear, quadratic = (((lane1 == k) | (lane1 == k + 3)).astype(f32) for k in range(3))
    power = plain + shift * (linear + shift * quadratic)
    sums = jnp.sum(lines * power, axis=0, keepdims=True)
    square, energy = pick(sums, 0, 3), pick(sums, 3, 3)
    bound = jnp.maximum(a1, energy / square) + jnp.sqrt(square / norm)
    middle, k1, h1, k2, h2 = factors(coarse_share, 1.0)
    scale = 1.0 / bound
    v0, h1, h2 = scale * (1.0 / middle), scale * h1, scale * h2
    v1 = (k1 * v0 + h1, -h1 * v0)
    v2 = (k2 * v1[0] + h2, k2 * v1[1] - h2 * (v0 + v1[0]), -h2 * v1[1])
    weights = (v0 + v1[0] + v2[0], v1[1] + v2[1], v2[2])

    upper = iota((8, 128), 0) < 4
    tall = []
    for a in range(6):
        field = weights[0] * basis[0, a] + weights[1] * basis[1, a] + weights[2] * basis[2, a]
        if 1 <= a <= 4:
            correction[a - 1] = field[0:4, 0:64]
        for p, q in ((0, 1), (2, 3), (4, 15)):
            p, q = (jnp.broadcast_to(field[k : k + 1], (8, 128)) for k in (p, q))
            tall.append(jnp.where(upper, p, q))
    lanes = (iota((128, LONG), 1) // 4 == iota((128, LONG), 0)).astype(bf16)
    fine = by_right(jnp.concatenate(tall, axis=0), lanes)
    lifted = [fine[RING * a : RING * a + RING] for a in range(6)]
    for i in range(ROWS):
        lift[i] = lifted[(i + 1) // 4]

    none4 = jnp.zeros((4, LONG), f32)

    left_out, right_out = sides(one_out, two_out, flags[4] > 0, flags[2] > 0, flags[3] > 0)

    def strip(own, outer, x):
        get, n, k = (own, (x - 2) // 4, (x - 2) % 4) if 2 <= x < 18 else (outer, 0, x if x < 2 else x - 16)
        return jnp.concatenate([get(2 * n + c, pl.ds(2 * k, 2)) for c in range(2)], axis=1)

    for i in range(1, ROWS - 1):
        x = i - 1
        if x < 2 or x >= 18:
            get, k = (low, x) if x < 2 else (high, x - 18)
            halves = [
                jnp.concatenate([get(4 * k + 2 * h + c) for c in range(2)], axis=1) for h in range(2)
            ]
            mine = jnp.concatenate(halves, axis=0)
        else:
            mine = own_layer(x - 2, resid_i, resid_o, 4, 12, 9)
        after, before = strip(right, right_out, x), strip(left, left_out, x)
        r0[i] = jnp.concatenate([mine, after, none4, before], axis=0)

    for i in range(1, ROWS - 1):
        r = r0[i] - (g[i] * lift[i] - near(i, lift, cx, cy, cz))
        r0[i] = r
        u0[i] = inv[i] * r * (1.0 / center)

    for i in range(2, ROWS - 2):
        u = u0[i]
        r = r0[i] - (g[i] * u - near(i, u0, cx, cy, cz))
        r0[i] = r
        u1[i] = m1 * u + q1 * (inv[i] * r)

    for i in range(3, 19):
        u = u1[i]
        r = r0[i] - (g[i] * u - near(i, u1, cx, cy, cz))
        step = (u0[i] + u) + (m2 * u + q2 * (inv[i] * r)) + lift[i]
        out[i - 3] = own_layer(i - 3, iterate_i, iterate_o, 3, 13, 11) + step[:SIDE]


def swap(values, axis, odd):
    count = lax.axis_size(axis)
    other = [(i ^ 1) if not odd else (((i + 1) ^ 1) - 1) % count for i in range(count)]
    return lax.ppermute(values, axis, list(enumerate(other)))


def body(src, cx, cy, cz, ab, active):
    ix, iy = lax.axis_index("coarse"), lax.axis_index("fine")
    nx, ny = lax.axis_size("coarse"), lax.axis_size("fine")
    flags = jnp.stack([ix > 0, ix < nx - 1, iy > 0, iy < ny - 1, iy % 2 == 0, ix % 2 == 0]).astype(jnp.int32)
    block, ring = (SIDE, SIDE, LONG), pltpu.VMEM((ROWS, RING, LONG), f32)

    first, second = pack_first_call((src, cx, cy, cz, ab))
    one_x, two_x = swap(first, "coarse", False), swap(second, "coarse", True)
    coarse, mask = call(coarsen, [(4, 4, 8, 128), (8, 128)], ins=[VMEM] * 5)(cx, cy, cz, ab, active)
    diag, first, second = call(
        pack_inner, [block, (8, 24, LONG), (8, 24, LONG)], ins=[SMEM] + [VMEM] * 5
    )(flags, src, cx, cy, cz, ab)
    one, two = swap(first, "fine", False), swap(second, "fine", True)
    diag_out, first, second = call(
        pack_outer, [(7, SIDE, LONG), (3, 24, LONG), (3, 24, LONG)], ins=[SMEM] + [VMEM] * 7
    )(flags, src, cx, cy, cz, ab, one_x, two_x)
    one_out, two_out = swap(first, "fine", False), swap(second, "fine", True)
    inner, outer = (15, RING, LONG), (7, RING, LONG)
    *fields_i, edge, iterate_i, resid_i = call(
        smooth_inner,
        [inner] * 5 + [(18, RING, LONG), (11, SIDE, LONG), (9, SIDE, LONG)],
        [pltpu.VMEM(inner, f32)] * 4,
        ins=[SMEM] + [VMEM] * 7,
    )(flags, src, cx, cy, cz, diag, one, two)
    *fields_o, iterate_o, resid_o, packed, weight, first, second = call(
        smooth_outer,
        [outer] * 5 + [(5, SIDE, LONG), (7, SIDE, LONG)]
        + [(5, 8, 128), (4, 8, 128), (12, 8, 128), (12, 8, 128)],
        ins=[SMEM] + [VMEM] * 18,
    )(
        flags, src, cx, cy, cz, one_x, two_x, diag_out, one_out, two_out, coarse, mask,
        *fields_i, edge, resid_i,
    )
    one_x, two_x = swap(first, "coarse", False), swap(second, "coarse", True)
    first, second = call(pack_own, [(13, 8, 128)] * 2, ins=[SMEM] + [VMEM] * 3)(
        flags, resid_i, resid_o, packed
    )
    one, two = swap(first, "fine", False), swap(second, "fine", True)
    first, second = call(pack_halo, [(10, 8, 128)] * 2, ins=[SMEM] + [VMEM] * 2)(flags, one_x, two_x)
    one_out, two_out = swap(first, "fine", False), swap(second, "fine", True)
    count = nx * ny
    basis, message = call(
        krylov,
        [(3, 6, 16, 128), (256, 128)],
        [pltpu.VMEM((5, 10, 16, 128), f32), pltpu.VMEM((10, 16, 128), f32)],
        ins=[SMEM] + [VMEM] * 8,
    )(flags, packed, weight, one_x, two_x, one, two, one_out, two_out)
    gathered = lax.all_to_all(message[:count], ("coarse", "fine"), 0, 0, tiled=True)
    out, correction = call(
        finish,
        [block, (4, 4, 64)],
        [ring] * 4,
        ins=[SMEM] + [VMEM] * 22,
    )(
        flags, gathered, basis, *fields_i, *fields_o, resid_i, resid_o, iterate_i, iterate_o,
        one_x, two_x, one, two, one_out, two_out,
    )
    return (out, correction)


def solution(mesh):
    spec = P("coarse", "fine", None)
    return jax.shard_map(
        body, mesh=mesh, in_specs=(spec,) * 6, out_specs=(spec,) * 2, check_vma=False
    )
```

```python
import jax
import jax.numpy as jnp
from jax import lax
from jax.experimental import pallas as pl
from jax.experimental.pallas import tpu as pltpu
from jax.sharding import PartitionSpec as P

f32 = jnp.float32
bf16 = jnp.bfloat16
fine_low = 0.25
fine_high = 2.0
coarse_share = 0.125
SIDE = 16
LONG = 256
ROWS = SIDE + 6
RING = 24
VMEM = pl.BlockSpec(memory_space=pltpu.VMEM)
LIMIT = 24 * 1024 * 1024


def factors(lower, upper):
    center = 0.5 * (upper + lower)
    radius = 0.5 * (upper - lower)
    aspect = center / radius
    p0 = 1.0 / aspect
    p1 = 1.0 / (2.0 * aspect - p0)
    p2 = 1.0 / (2.0 * aspect - p1)
    return center, p1 * p0, 2.0 * p1 / radius, p2 * p1, 2.0 * p2 / radius


FINE = factors(fine_low, fine_high)


def iota(shape, axis):
    return lax.broadcasted_iota(jnp.int32, shape, axis)


def back(values, axis):
    return pltpu.roll(values, 1, axis)


def ahead(values, axis):
    return pltpu.roll(values, values.shape[axis] - 1, axis)


def call(kernel, outs, scratch=(), ins=None):
    return pl.pallas_call(
        kernel,
        out_shape=[jax.ShapeDtypeStruct(s, f32) for s in outs],
        in_specs=ins,
        out_specs=[VMEM] * len(outs),
        scratch_shapes=list(scratch),
        compiler_params=pltpu.CompilerParams(vmem_limit_bytes=LIMIT),
    )


def place():
    ix, iy = lax.axis_index("coarse"), lax.axis_index("fine")
    nx, ny = lax.axis_size("coarse"), lax.axis_size("fine")
    return ix, nx - 1 - ix, iy, ny - 1 - iy, 1 - iy % 2, 1 - ix % 2


def pack_first(*refs):
    fields, pair, sems = refs[:5], refs[5:7], refs[7]
    even = lax.axis_index("coarse") % 2 == 0

    def fill(up, down):
        copies = []
        for n, field in enumerate(fields):
            first = 12 if n == 1 else 13
            at = UP_AT[n] + first - 13
            copies.append((field.at[first:16], up.at[at : at + 16 - first]))
            copies.append((field.at[0:3], down.at[3 * n : 3 * n + 3]))
        copies = [pltpu.make_async_copy(a, b, sems.at[k]) for k, (a, b) in enumerate(copies)]
        for copy in copies:
            copy.start()
        for copy in copies:
            copy.wait()

    @pl.when(even)
    def _():
        fill(*pair)

    @pl.when(jnp.logical_not(even))
    def _():
        fill(*pair[::-1])


def pack_first_call(fields):
    return pl.pallas_call(
        pack_first,
        out_shape=[jax.ShapeDtypeStruct((16, SIDE, LONG), f32)] * 2,
        in_specs=[pl.BlockSpec(memory_space=pltpu.HBM)] * 5,
        out_specs=[VMEM] * 2,
        scratch_shapes=[pltpu.SemaphoreType.DMA((10,))],
    )(*fields)


UP_AT = (0, 4, 7, 10, 13)


def sum_lanes(last_only):
    cell, lane = iota((LONG, 128), 0), iota((LONG, 128), 1)
    hit = cell // 4 == lane
    if last_only:
        hit = hit & (cell % 4 == 3)
    return hit.astype(bf16)


def sum_rows(last_only):
    block, cell = iota((8, SIDE), 0), iota((8, SIDE), 1)
    hit = cell // 4 == block
    if last_only:
        hit = hit & (cell % 4 == 3)
    return hit.astype(bf16)


def parts_of(values):
    first = values.astype(bf16)
    rest = values - first.astype(f32)
    second = rest.astype(bf16)
    return first, second, (rest - second.astype(f32)).astype(bf16)


def by_right(values, choose):
    return sum(jnp.dot(p, choose, preferred_element_type=f32) for p in parts_of(values))


def by_left(choose, values):
    return sum(jnp.dot(choose, p, preferred_element_type=f32) for p in parts_of(values))


def coarsen(cx, cy, cz, ab, active, out, mask):
    lanes, last = sum_lanes(False), sum_lanes(True)
    rows, lastrow = sum_rows(False), sum_rows(True)

    def coarse(n, part, left, right):
        total = by_right(jnp.concatenate([part(4 * a) for a in range(4)], axis=0), right)
        for a in range(4):
            out[n, a] = by_left(left, total[SIDE * a : SIDE * a + SIDE])

    def layers(ref):
        return lambda x: (ref[x] + ref[x + 1]) + (ref[x + 2] + ref[x + 3])

    coarse(0, lambda x: cx[x + 3], rows, lanes)
    coarse(1, layers(cy), lastrow, lanes)
    coarse(2, layers(cz), rows, last)
    coarse(3, layers(ab), rows, lanes)
    spread = ((iota((16, 128), 1) // 4) == iota((16, 128), 0)).astype(bf16)
    line = jnp.broadcast_to(active[0].astype(f32), (8, 16)).astype(bf16)
    mask[...] = jnp.dot(line, spread, preferred_element_type=f32)


def diagonal(cx_i, cxl_i, cy_i, cz_i, ab_i):
    row, lane = iota((SIDE, LONG), 0), iota((SIDE, LONG), 1)
    g = cx_i + cxl_i + cy_i + cz_i + ab_i
    g = g + jnp.where(row == 0, 0.0, back(cy_i, 0))
    return g + jnp.where(lane == 0, 0.0, back(cz_i, 1))


def strips(src_i, cx_i, cy_i, cz_i, g, inside, beyond=None):
    start = jnp.where(inside, src_i / (FINE[0] * g), 0.0)
    pieces = (src_i, cx_i, cy_i, cz_i, g)
    third = cy_i[13:14] if beyond is None else beyond[15:16]
    top = jnp.concatenate([p[14:16] for p in pieces] + [start[13:14], third], axis=0)
    bottom = jnp.concatenate([p[0:2] for p in pieces] + [start[2:3], start[2:3]], axis=0)
    return top, bottom


def pack_inner(src, cx, cy, cz, ab, diag, first, second):
    flags = place()
    even = flags[4] > 0
    for x in range(1, SIDE):
        g = diagonal(cx[x], cx[x - 1], cy[x], cz[x], ab[x])
        diag[x] = g
        top, bottom = strips(src[x], cx[x], cy[x], cz[x], g, True)
        at = (x - 1) % 8, pl.ds(12 * ((x - 1) // 8), 12)
        first[at] = jnp.where(even, top, bottom)
        second[at] = jnp.where(even, bottom, top)


def pack_outer(src, cx, cy, cz, ab, one, two, diag, first, second):
    flags = place()
    even = flags[4] > 0
    has_low, has_high = flags[0] > 0, flags[1] > 0
    low, high = sides(one, two, flags[5] > 0, has_low, has_high)
    layers = []
    for k in range(3):
        f = [low(UP_AT[n] + k) for n in range(5)]
        layers.append((f, low(3 + k), has_low, low(UP_AT[2]) if k == 1 else None))
    layers.append(([ref[0] for ref in (src, cx, cy, cz, ab)], low(6), True, None))
    for k in range(3):
        f = [high(3 * n + k) for n in range(5)]
        before = cx[15] if k == 0 else high(3 + k - 1)
        layers.append((f, before, has_high, high(8) if k == 1 else None))
    for k, (f, before, inside, beyond) in enumerate(layers):
        g = diagonal(f[1], before, *f[2:])
        diag[k] = g
        if 1 <= k < 6:
            top, bottom = strips(*f[:4], g, inside, beyond)
            at = (k - 1) % 3, pl.ds(12 * ((k - 1) // 3), 12)
            first[at] = jnp.where(even, top, bottom)
            second[at] = jnp.where(even, bottom, top)


def sides(one, two, even, has_low, has_high):
    keep_low, keep_high = has_low.astype(f32), has_high.astype(f32)

    def low(*at):
        return jnp.where(even, two[at], one[at]) * keep_low

    def high(*at):
        return jnp.where(even, one[at], two[at]) * keep_high

    return low, high


def near(i, u, cx, cy, cz):
    here = u[i]
    cy_i, cz_i = cy[i], cz[i]
    total = cx[i] * u[i + 1] + cx[i - 1] * u[i - 1]
    total = total + (cy_i * ahead(here, 0) + back(cy_i * here, 0))
    return total + (cz_i * ahead(here, 1) + back(cz_i * here, 1))


def join(layers):
    total = layers[0]
    for k, v in enumerate(layers[1:], 1):
        v = pltpu.roll(v, 64, 1) if k >= 2 else v
        total = total + (pltpu.roll(v, 4, 0) if k % 2 else v)
    return total


class Layers:
    def __init__(self, inner, outer=None):
        self.inner, self.outer = inner, outer

    def __getitem__(self, i):
        if 4 <= i < 19:
            return self.inner[i - 4]
        return self.outer[i if i < 4 else i - 15]

    def __setitem__(self, i, value):
        self.inner[i - 4] = value


class Over(dict):
    def __init__(self, inner, rows=None):
        self.inner, self.rows = inner, rows

    def __missing__(self, i):
        return self.inner[i - 4 if self.rows is None else self.rows[i]]


def own_layer(x, inner, outer, first, last, skip):
    return inner[x - first] if first <= x <= last else outer[x if x < first else x - skip]


def ring_layer(fields, g, lo, hi, hit, face=None):
    src_i, cx_i, cy_i, cz_i = fields
    row, lane = iota((RING, LONG), 0), iota((RING, LONG), 1)
    none1, none4 = jnp.zeros((1, LONG), f32), jnp.zeros((4, LONG), f32)

    def ring(own, n):
        return jnp.concatenate([own, hi[2 * n : 2 * n + 2], none4, lo[2 * n : 2 * n + 2]], axis=0)

    src_r, cx_r, cz_r, g = ring(src_i, 0), ring(cx_i, 1), ring(cz_i, 3), ring(g, 4)
    cy_r = jnp.concatenate([cy_i, hi[4:6], none1, none1, none1, lo[11:12], lo[4:6]], axis=0)
    if face is not None:
        cy_r = jnp.where(row == 23, face, cy_r)
    g = g + jnp.where((row == 0) | (row == 16), back(cy_r, 0), 0.0)
    inv = jnp.where(hit, 1.0 / g, 0.0)
    u = src_r * inv * (1.0 / FINE[0])
    u = jnp.where(row == 18, hi[10:11], u)
    u = jnp.where(row == 21, lo[10:11], u)
    return cx_r, cy_r, jnp.where(lane == LONG - 1, 0.0, cz_r), g, inv, src_r, u


def inside_ring(flags):
    row = iota((RING, LONG), 0)
    return (row < 16) | ((row < 18) & (flags[3] > 0)) | ((row >= 22) & (flags[2] > 0))


EDGE_ROWS = ((4, 5, 6, 16, 17, 18), (4, 5, 17, 18), (5, 6, 16, 17), (6, 7, 15, 16))
EDGES = [{i: k + sum(map(len, EDGE_ROWS[:n])) for k, i in enumerate(v)} for n, v in enumerate(EDGE_ROWS)]


def smooth_inner(
    src, cx, cy, cz, diag, one, two,
    cx_o, cy_o, cz_o, g_o, inv_o, edge, iterate, resid, u0, u1, u2, r,
):
    flags = place()
    center, m1, q1, m2, q2 = FINE
    left, right = sides(one, two, flags[4] > 0, flags[2] > 0, flags[3] > 0)
    hit = inside_ring(flags)
    made = [Layers(ref) for ref in (cx_o, cy_o, cz_o, g_o, inv_o, r, u0)]
    u1, u2 = Layers(u1), Layers(u2)
    for i in range(4, 19):
        x, at = i - 3, ((i - 4) % 8, pl.ds(12 * ((i - 4) // 8), 12))
        fields = src[x], cx[x], cy[x], cz[x]
        for out, value in zip(made, ring_layer(fields, diag[x], left(*at), right(*at), hit)):
            out[i] = value
    cx, cy, cz, g, inv, r, u0 = made
    for i in range(5, 18):
        u = u0[i]
        v = r[i] - (g[i] * u - near(i, u0, cx, cy, cz))
        r[i] = v
        u1[i] = m1 * u + q1 * (inv[i] * v)
    for i in range(6, 17):
        u = u1[i]
        v = r[i] - (g[i] * u - near(i, u1, cx, cy, cz))
        r[i] = v
        v = m2 * u + q2 * (inv[i] * v)
        u2[i] = v
        iterate[i - 6] = (u0[i] + u + v)[:SIDE]
    for values, rows in zip((r, u0, u1, u2), EDGES):
        for i, at in rows.items():
            edge[at] = values[i]
    for i in range(7, 16):
        resid[i - 7] = (r[i] - (g[i] * u2[i] - near(i, u2, cx, cy, cz)))[:SIDE]


def smooth_outer(
    src, cx, cy, cz, one_x, two_x, diag, one, two, coarse, active,
    cx_i, cy_i, cz_i, g_i, inv_i, edge, resid_i,
    cx_o, cy_o, cz_o, g_o, inv_o, iterate, resid, packed, weight, first, second,
):
    flags = place()
    center, m1, q1, m2, q2 = FINE
    has_low, has_high = flags[0] > 0, flags[1] > 0
    low, high = sides(one_x, two_x, flags[5] > 0, has_low, has_high)
    left, right = sides(one, two, flags[4] > 0, flags[2] > 0, flags[3] > 0)
    hit = inside_ring(flags)
    own_row = iota((RING, LONG), 0) < SIDE
    none12 = jnp.zeros((12, LONG), f32)
    layers = [([low(UP_AT[n] + k) for n in range(4)], has_low) for k in range(3)]
    layers.append(([ref[0] for ref in (src, cx, cy, cz)], True))
    layers += [([high(3 * n + k) for n in range(4)], has_high) for k in range(3)]
    made = [Over(ref) for ref in (cx_i, cy_i, cz_i, g_i, inv_i)]
    made += [Over(edge, EDGES[0]), Over(edge, EDGES[1])]
    for k, (fields, inside) in enumerate(layers):
        lo, hi, face = none12, none12, None
        if 1 <= k < 6:
            at = (k - 1) % 3, pl.ds(12 * ((k - 1) // 3), 12)
            lo, hi, here = left(*at), right(*at), hit & inside
        else:
            dst, at = (0, 0) if k == 0 else (1, 12)
            face, here = left(dst, pl.ds(at, 12))[11:12], hit & inside & own_row
        values = ring_layer(fields, diag[k], lo, hi, here, face)
        for out, value in zip(made, values):
            out[k if k < 4 else k + 15] = value
        for out, value in zip((cx_o, cy_o, cz_o, g_o, inv_o), values):
            out[k] = value
    cx, cy, cz, g, inv, r, u0 = made
    u1, u2 = Over(edge, EDGES[2]), Over(edge, EDGES[3])

    lanes, rows = sum_lanes(False), sum_rows(False)
    crow, clane = iota((8, 128), 0), iota((8, 128), 1)
    own = (crow < 4) & (clane < 64)
    mask = active[...]
    tails = [sum(cy[4 * a + 3 + k][SIDE:] for k in range(4)) for a in range(4)]
    below = by_right(jnp.concatenate([cx[2][:SIDE]] + tails, axis=0), lanes)
    below_x = by_left(rows, below[:SIDE])
    inverse, uppers, tiles = [], [], []
    for a in range(4):
        below_y = back(below[SIDE + 8 * a : SIDE + 8 * a + 8], 0)
        cx_c, cy_c, cz_c, ab_c = (coarse[n, a] for n in range(4))
        total = cx_c + cy_c + cz_c + ab_c + back(cz_c, 1)
        total = total + (below_x if a == 0 else coarse[0, a - 1])
        total = total + jnp.where(crow == 0, below_y, back(cy_c, 0))
        weight[a] = jnp.where(own, total, 0.0)
        inverse.append(jnp.where(own, mask / jnp.where(own, total, 1.0), 0.0))
        lower = cx_c + pltpu.roll(cy_c, 64, 1)
        tiles.append(pltpu.roll(inverse[a], 64, 1) + pltpu.roll(lower, 4, 0))
        uppers.append(jnp.where(clane == 63, 0.0, cz_c))
    packed[4] = join(uppers)

    for i in (1, 2, 3, 4, 18, 19, 20):
        v = r[i] - (g[i] * u0[i] - near(i, u0, cx, cy, cz))
        r[i] = v
        u1[i] = m1 * u0[i] + q1 * (inv[i] * v)
    for i in (2, 3, 4, 5, 17, 18, 19):
        v = r[i] - (g[i] * u1[i] - near(i, u1, cx, cy, cz))
        r[i] = v
        u2[i] = m2 * u1[i] + q2 * (inv[i] * v)
    for k, i in enumerate((3, 4, 5, 17, 18)):
        iterate[k] = (u0[i] + u1[i] + u2[i])[:SIDE]
    edges = {}
    for k, i in enumerate((3, 4, 5, 6, 16, 17, 18)):
        edges[i - 3] = (r[i] - (g[i] * u2[i] - near(i, u2, cx, cy, cz)))[:SIDE]
        resid[k] = edges[i - 3]
    even = flags[5] > 0
    rest = [edges[x] if x in edges else resid_i[x - 4] for x in range(SIDE)]
    totals = [(rest[x] + rest[x + 1]) + (rest[x + 2] + rest[x + 3]) for x in range(0, SIDE, 4)]

    for k in range(2):
        up, down = edges[14 + k], edges[k]
        for n in range(4):
            ys, zs = 8 * (n // 2), 128 * (n % 2)
            p, q = up[ys : ys + 8, zs : zs + 128], down[ys : ys + 8, zs : zs + 128]
            first[4 * k + n] = jnp.where(even, p, q)
            second[4 * k + n] = jnp.where(even, q, p)
    rhs = by_right(jnp.concatenate(totals, axis=0), lanes)
    for a in range(4):
        tiles[a] = tiles[a] + inverse[a] * by_left(rows, rhs[SIDE * a : SIDE * a + SIDE])
        packed[a] = tiles[a]
    ups, downs = tiles[1:4] + [join(uppers[1:4])], tiles[0:3] + [join(uppers[0:3])]
    for k, (p, q) in enumerate(zip(ups, downs)):
        first[8 + k] = jnp.where(even, p, q)
        second[8 + k] = jnp.where(even, q, p)


def residual_strips(layers, even, first, second, at):
    for c in range(2):
        parts = [layer[c] for layer in layers]
        bottom = jnp.concatenate([head for head, _ in parts], axis=0)
        top = jnp.concatenate([tail for _, tail in parts], axis=0)
        first[at + c] = jnp.where(even, top, bottom)
        second[at + c] = jnp.where(even, bottom, top)


def pack_own(resid_i, resid_o, packed, first, second):
    flags = place()
    def halves(x):
        mine = own_layer(x, resid_i, resid_o, 4, 12, 9)
        return [(mine[0:2, at : at + 128], mine[14:16, at : at + 128]) for at in (0, 128)]

    for n in range(4):
        residual_strips([halves(4 * n + k) for k in range(4)], flags[4] > 0, first, second, 2 * n)
    for k in range(5):
        first[8 + k] = packed[k]
        second[8 + k] = packed[k]


def pack_halo(one_x, two_x, first, second):
    flags = place()
    low, high = sides(one_x, two_x, flags[5] > 0, flags[0] > 0, flags[1] > 0)

    def halves(get, k):
        return [(get(4 * k + c)[0:2], get(4 * k + 2 + c)[6:8]) for c in range(2)]

    layers = [halves(low, 0), halves(low, 1), halves(high, 0), halves(high, 1)]
    residual_strips(layers, flags[4] > 0, first, second, 0)
    for k, get in enumerate((low, high)):
        for a in range(4):
            at = 2 + 3 * k + a if a < 3 else 8 + k
            tile = get(8 + a)
            first[at] = tile
            second[at] = tile


def krylov(packed, weight, one_x, two_x, one, two, one_out, two_out, basis, message, ext, t1s):
    flags = place()
    low, high = sides(one_x, two_x, flags[5] > 0, flags[0] > 0, flags[1] > 0)
    left, right = sides(one, two, flags[4] > 0, flags[2] > 0, flags[3] > 0)
    left_out, right_out = sides(one_out, two_out, flags[4] > 0, flags[2] > 0, flags[3] > 0)
    crow, clane = iota((8, 128), 0), iota((8, 128), 1)
    top, thin = crow < 4, clane < 64

    def tiles(own, out):
        return [out(2 + a) for a in range(3)] + [own(8 + a) for a in range(4)] + [
            out(5 + a) for a in range(3)
        ] + [out(8), own(12), out(9)]

    mine = [low(8 + a) for a in range(3)] + [packed[a] for a in range(4)]
    mine += [high(8 + a) for a in range(3)] + [low(11), packed[4], high(11)]
    previous, following = tiles(left, left_out), tiles(right, right_out)

    def upper(field, a):
        group, k = (0, a) if a < 3 else (1, a - 3) if a < 7 else (2, a - 7)
        tile = field[10 + group]
        return (pltpu.roll(tile, 64, 1) if k >= 2 else tile), k % 2

    def turn(tile):
        return pltpu.roll(tile, 4, 0)

    for a in range(10):
        here, after, before = mine[a], following[a], previous[a]
        pairs = (
            (jnp.where(top, here, turn(after)), jnp.where(top, turn(here), after)),
            (jnp.where(top, 0.0, turn(before)), jnp.where(top, 0.0, before)),
        )
        (here, odd), (after, _), (before, _) = (upper(f, a) for f in (mine, following, previous))
        if odd:
            faces = jnp.where(top, turn(here), after), jnp.where(top, 0.0, before)
        else:
            faces = jnp.where(top, here, turn(after)), jnp.where(top, 0.0, turn(before))
        for n in range(2):
            at = pl.ds(8 * n, 8)
            for m in range(2):
                ext[2 * m, a, at] = jnp.where(thin, pairs[n][m], 0.0)
                ext[2 * m + 1, a, at] = jnp.where(thin, pltpu.roll(pairs[n][m], 64, 1), 0.0)
            ext[4, a, at] = jnp.where(thin, faces[n], 0.0)

    z, inv, cx, cy, cz = (ext.at[n] for n in range(5))
    for a in range(1, 9):
        t1s[a] = z[a] - inv[a] * near(a, z, cx, cy, cz)
    for a in range(2, 8):
        t1 = t1s[a]
        basis[0, a - 2] = z[a]
        basis[1, a - 2] = t1
        basis[2, a - 2] = t1 - inv[a] * near(a, t1s, cx, cy, cz)

    def total(parts):
        return jnp.sum(sum(parts), keepdims=True)

    g = [weight[a] for a in range(4)]
    v0, v1, v2 = ([basis[n, a + 1, 0:8] for a in range(4)] for n in range(3))
    s00 = total([w * p * p for w, p in zip(g, v0)])
    s01 = total([w * p * q for w, p, q in zip(g, v0, v1)])
    alpha = jnp.where(s00 > 0, s01 / jnp.where(s00 > 0, s00, 1.0), 0.0)
    e = [q - alpha * p for p, q in zip(v0, v1)]
    te = [q - alpha * p for p, q in zip(v1, v2)]
    terms = [
        total([w * p * p for w, p in zip(g, e)]),
        2.0 * total([w * p * q for w, p, q in zip(g, e, v0)]),
        s00,
        total([w * p * q for w, p, q in zip(g, e, te)]),
        total([w * (p * q + r * t) for w, p, q, r, t in zip(g, v0, te, e, v1)]),
        s01,
    ]
    lane = iota((8, 128), 1)
    line = jnp.where(lane < 64, 0.0, alpha)
    for n, term in enumerate(terms):
        line = jnp.where(lane == n, term, line)
    message[...] = jnp.broadcast_to(line[0:1], (256, 128))


def finish(
    gathered, basis, cx_i, cy_i, cz_i, g_i, inv_i, cx_o, cy_o, cz_o, g_o, inv_o,
    resid_i, resid_o, iterate_i, iterate_o, one_x, two_x, one, two, one_out, two_out,
    out, correction, lift, u0, u1, r0,
):
    flags = place()
    center, m1, q1, m2, q2 = FINE
    low, high = sides(one_x, two_x, flags[5] > 0, flags[0] > 0, flags[1] > 0)
    left, right = sides(one, two, flags[4] > 0, flags[2] > 0, flags[3] > 0)

    pairs = (cx_i, cx_o), (cy_i, cy_o), (cz_i, cz_o), (g_i, g_o), (inv_i, inv_o)
    cx, cy, cz, g, inv = (Layers(*pair) for pair in pairs)

    lines = gathered[...]
    lane1 = iota((1, 128), 1)
    sums = jnp.sum(lines, axis=0, keepdims=True)

    def pick(values, first, count):
        hit = (lane1 >= first) & (lane1 < first + count)
        return jnp.sum(jnp.where(hit, values, 0.0), axis=1, keepdims=True)

    norm = pick(sums, 2, 1)
    a1 = pick(sums, 5, 1) / norm
    shift = pltpu.roll(lines, 64, 1) - a1
    plain, linear, quadratic = (((lane1 == k) | (lane1 == k + 3)).astype(f32) for k in range(3))
    power = plain + shift * (linear + shift * quadratic)
    sums = jnp.sum(lines * power, axis=0, keepdims=True)
    square, energy = pick(sums, 0, 3), pick(sums, 3, 3)
    bound = jnp.maximum(a1, energy / square) + jnp.sqrt(square / norm)
    middle, k1, h1, k2, h2 = factors(coarse_share, 1.0)
    scale = 1.0 / bound
    v0, h1, h2 = scale * (1.0 / middle), scale * h1, scale * h2
    v1 = (k1 * v0 + h1, -h1 * v0)
    v2 = (k2 * v1[0] + h2, k2 * v1[1] - h2 * (v0 + v1[0]), -h2 * v1[1])
    weights = (v0 + v1[0] + v2[0], v1[1] + v2[1], v2[2])

    upper = iota((8, 128), 0) < 4
    tall = []
    for a in range(6):
        field = weights[0] * basis[0, a] + weights[1] * basis[1, a] + weights[2] * basis[2, a]
        if 1 <= a <= 4:
            correction[a - 1] = field[0:4, 0:64]
        for p, q in ((0, 1), (2, 3), (4, 15)):
            p, q = (jnp.broadcast_to(field[k : k + 1], (8, 128)) for k in (p, q))
            tall.append(jnp.where(upper, p, q))
    lanes = (iota((128, LONG), 1) // 4 == iota((128, LONG), 0)).astype(bf16)
    fine = by_right(jnp.concatenate(tall, axis=0), lanes)
    lifted = [fine[RING * a : RING * a + RING] for a in range(6)]
    for i in range(ROWS):
        lift[i] = lifted[(i + 1) // 4]

    none4 = jnp.zeros((4, LONG), f32)

    left_out, right_out = sides(one_out, two_out, flags[4] > 0, flags[2] > 0, flags[3] > 0)

    def strip(own, outer, x):
        get, n, k = (own, (x - 2) // 4, (x - 2) % 4) if 2 <= x < 18 else (outer, 0, x if x < 2 else x - 16)
        return jnp.concatenate([get(2 * n + c, pl.ds(2 * k, 2)) for c in range(2)], axis=1)

    for i in range(1, ROWS - 1):
        x = i - 1
        if x < 2 or x >= 18:
            get, k = (low, x) if x < 2 else (high, x - 18)
            halves = [
                jnp.concatenate([get(4 * k + 2 * h + c) for c in range(2)], axis=1) for h in range(2)
            ]
            mine = jnp.concatenate(halves, axis=0)
        else:
            mine = own_layer(x - 2, resid_i, resid_o, 4, 12, 9)
        after, before = strip(right, right_out, x), strip(left, left_out, x)
        r0[i] = jnp.concatenate([mine, after, none4, before], axis=0)

    for i in range(1, ROWS - 1):
        r = r0[i] - (g[i] * lift[i] - near(i, lift, cx, cy, cz))
        r0[i] = r
        u0[i] = inv[i] * r * (1.0 / center)

    for i in range(2, ROWS - 2):
        u = u0[i]
        r = r0[i] - (g[i] * u - near(i, u0, cx, cy, cz))
        r0[i] = r
        u1[i] = m1 * u + q1 * (inv[i] * r)

    for i in range(3, 19):
        u = u1[i]
        r = r0[i] - (g[i] * u - near(i, u1, cx, cy, cz))
        step = (u0[i] + u) + (m2 * u + q2 * (inv[i] * r)) + lift[i]
        out[i - 3] = own_layer(i - 3, iterate_i, iterate_o, 3, 13, 11) + step[:SIDE]


def swap(values, axis, odd):
    count = lax.axis_size(axis)
    other = [(i ^ 1) if not odd else (((i + 1) ^ 1) - 1) % count for i in range(count)]
    return lax.ppermute(values, axis, list(enumerate(other)))


def body(src, cx, cy, cz, ab, active):
    count = lax.axis_size("coarse") * lax.axis_size("fine")
    block, ring = (SIDE, SIDE, LONG), pltpu.VMEM((ROWS, RING, LONG), f32)

    first, second = pack_first_call((src, cx, cy, cz, ab))
    one_x, two_x = swap(first, "coarse", False), swap(second, "coarse", True)
    coarse, mask = call(coarsen, [(4, 4, 8, 128), (8, 128)], ins=[VMEM] * 5)(cx, cy, cz, ab, active)
    diag, first, second = call(
        pack_inner, [block, (8, 24, LONG), (8, 24, LONG)], ins=[VMEM] * 5
    )(src, cx, cy, cz, ab)
    one, two = swap(first, "fine", False), swap(second, "fine", True)
    diag_out, first, second = call(
        pack_outer, [(7, SIDE, LONG), (3, 24, LONG), (3, 24, LONG)], ins=[VMEM] * 7
    )(src, cx, cy, cz, ab, one_x, two_x)
    one_out, two_out = swap(first, "fine", False), swap(second, "fine", True)
    inner, outer = (15, RING, LONG), (7, RING, LONG)
    *fields_i, edge, iterate_i, resid_i = call(
        smooth_inner,
        [inner] * 5 + [(18, RING, LONG), (11, SIDE, LONG), (9, SIDE, LONG)],
        [pltpu.VMEM(inner, f32)] * 4,
        ins=[VMEM] * 7,
    )(src, cx, cy, cz, diag, one, two)
    *fields_o, iterate_o, resid_o, packed, weight, first, second = call(
        smooth_outer,
        [outer] * 5 + [(5, SIDE, LONG), (7, SIDE, LONG)]
        + [(5, 8, 128), (4, 8, 128), (12, 8, 128), (12, 8, 128)],
        ins=[VMEM] * 18,
    )(
        src, cx, cy, cz, one_x, two_x, diag_out, one_out, two_out, coarse, mask,
        *fields_i, edge, resid_i,
    )
    one_x, two_x = swap(first, "coarse", False), swap(second, "coarse", True)
    first, second = call(pack_own, [(13, 8, 128)] * 2, ins=[VMEM] * 3)(
        resid_i, resid_o, packed
    )
    one, two = swap(first, "fine", False), swap(second, "fine", True)
    first, second = call(pack_halo, [(10, 8, 128)] * 2, ins=[VMEM] * 2)(one_x, two_x)
    one_out, two_out = swap(first, "fine", False), swap(second, "fine", True)
    basis, message = call(
        krylov,
        [(3, 6, 16, 128), (256, 128)],
        [pltpu.VMEM((5, 10, 16, 128), f32), pltpu.VMEM((10, 16, 128), f32)],
        ins=[VMEM] * 8,
    )(packed, weight, one_x, two_x, one, two, one_out, two_out)
    gathered = lax.all_to_all(message[:count], ("coarse", "fine"), 0, 0, tiled=True)
    out, correction = call(
        finish,
        [block, (4, 4, 64)],
        [ring] * 4,
        ins=[VMEM] * 22,
    )(
        gathered, basis, *fields_i, *fields_o, resid_i, resid_o, iterate_i, iterate_o,
        one_x, two_x, one, two, one_out, two_out,
    )
    return (out, correction)


def solution(mesh):
    spec = P("coarse", "fine", None)
    return jax.shard_map(
        body, mesh=mesh, in_specs=(spec,) * 6, out_specs=(spec,) * 2, check_vma=False
    )
```

```python
import jax
import jax.numpy as jnp
from jax import lax
from jax.experimental import pallas as pl
from jax.experimental.pallas import tpu as pltpu
from jax.sharding import PartitionSpec as P

f32 = jnp.float32
bf16 = jnp.bfloat16
fine_low = 0.25
fine_high = 2.0
coarse_share = 0.125
SIDE = 16
LONG = 256
ROWS = SIDE + 6
RING = 24
VMEM = pl.BlockSpec(memory_space=pltpu.VMEM)
LIMIT = 24 * 1024 * 1024


def factors(lower, upper):
    center = 0.5 * (upper + lower)
    radius = 0.5 * (upper - lower)
    aspect = center / radius
    p0 = 1.0 / aspect
    p1 = 1.0 / (2.0 * aspect - p0)
    p2 = 1.0 / (2.0 * aspect - p1)
    return center, p1 * p0, 2.0 * p1 / radius, p2 * p1, 2.0 * p2 / radius


FINE = factors(fine_low, fine_high)


def iota(shape, axis):
    return lax.broadcasted_iota(jnp.int32, shape, axis)


def back(values, axis):
    return pltpu.roll(values, 1, axis)


def ahead(values, axis):
    return pltpu.roll(values, values.shape[axis] - 1, axis)


def call(kernel, outs, scratch=(), ins=None):
    return pl.pallas_call(
        kernel,
        out_shape=[jax.ShapeDtypeStruct(s, f32) for s in outs],
        in_specs=ins,
        out_specs=[VMEM] * len(outs),
        scratch_shapes=list(scratch),
        compiler_params=pltpu.CompilerParams(vmem_limit_bytes=LIMIT),
    )


def place():
    ix, iy = lax.axis_index("coarse"), lax.axis_index("fine")
    nx, ny = lax.axis_size("coarse"), lax.axis_size("fine")
    return ix, nx - 1 - ix, iy, ny - 1 - iy, 1 - iy % 2, 1 - ix % 2


def pack_first(*refs):
    fields, pair, sems = refs[:5], refs[5:7], refs[7]
    even = lax.axis_index("coarse") % 2 == 0

    def fill(up, down):
        copies = []
        for n, field in enumerate(fields):
            first = 12 if n == 1 else 13
            at = UP_AT[n] + first - 13
            copies.append((field.at[first:16], up.at[at : at + 16 - first]))
            copies.append((field.at[0:3], down.at[3 * n : 3 * n + 3]))
        copies = [pltpu.make_async_copy(a, b, sems.at[k]) for k, (a, b) in enumerate(copies)]
        for copy in copies:
            copy.start()
        for copy in copies:
            copy.wait()

    @pl.when(even)
    def _():
        fill(*pair)

    @pl.when(jnp.logical_not(even))
    def _():
        fill(*pair[::-1])


def pack_first_call(fields):
    return pl.pallas_call(
        pack_first,
        out_shape=[jax.ShapeDtypeStruct((16, SIDE, LONG), f32)] * 2,
        in_specs=[pl.BlockSpec(memory_space=pltpu.HBM)] * 5,
        out_specs=[VMEM] * 2,
        scratch_shapes=[pltpu.SemaphoreType.DMA((10,))],
    )(*fields)


UP_AT = (0, 4, 7, 10, 13)


def sum_lanes(last_only):
    cell, lane = iota((LONG, 128), 0), iota((LONG, 128), 1)
    hit = cell // 4 == lane
    if last_only:
        hit = hit & (cell % 4 == 3)
    return hit.astype(bf16)


def sum_rows(last_only):
    block, cell = iota((8, SIDE), 0), iota((8, SIDE), 1)
    hit = cell // 4 == block
    if last_only:
        hit = hit & (cell % 4 == 3)
    return hit.astype(bf16)


def parts_of(values):
    first = values.astype(bf16)
    rest = values - first.astype(f32)
    second = rest.astype(bf16)
    return first, second, (rest - second.astype(f32)).astype(bf16)


def by_right(values, choose):
    return sum(jnp.dot(p, choose, preferred_element_type=f32) for p in parts_of(values))


def by_left(choose, values):
    return sum(jnp.dot(choose, p, preferred_element_type=f32) for p in parts_of(values))


def coarsen(cx, cy, cz, ab, active, out, mask):
    lanes, last = sum_lanes(False), sum_lanes(True)
    rows, lastrow = sum_rows(False), sum_rows(True)

    def coarse(n, part, left, right):
        total = by_right(jnp.concatenate([part(4 * a) for a in range(4)], axis=0), right)
        for a in range(4):
            out[n, a] = by_left(left, total[SIDE * a : SIDE * a + SIDE])

    def layers(ref):
        return lambda x: (ref[x] + ref[x + 1]) + (ref[x + 2] + ref[x + 3])

    coarse(0, lambda x: cx[x + 3], rows, lanes)
    coarse(1, layers(cy), lastrow, lanes)
    coarse(2, layers(cz), rows, last)
    coarse(3, layers(ab), rows, lanes)
    spread = ((iota((16, 128), 1) // 4) == iota((16, 128), 0)).astype(bf16)
    line = jnp.broadcast_to(active[0].astype(f32), (8, 16)).astype(bf16)
    mask[...] = jnp.dot(line, spread, preferred_element_type=f32)


def diagonal(cx_i, cxl_i, cy_i, cz_i, ab_i):
    row, lane = iota((SIDE, LONG), 0), iota((SIDE, LONG), 1)
    g = cx_i + cxl_i + cy_i + cz_i + ab_i
    g = g + jnp.where(row == 0, 0.0, back(cy_i, 0))
    return g + jnp.where(lane == 0, 0.0, back(cz_i, 1))


def strips(src_i, cx_i, cy_i, cz_i, g, inside, beyond=None):
    start = jnp.where(inside, src_i / (FINE[0] * g), 0.0)
    pieces = (src_i, cx_i, cy_i, cz_i, g)
    third = cy_i[13:14] if beyond is None else beyond[15:16]
    top = jnp.concatenate([p[14:16] for p in pieces] + [start[13:14], third], axis=0)
    bottom = jnp.concatenate([p[0:2] for p in pieces] + [start[2:3], start[2:3]], axis=0)
    return top, bottom


def pack_inner(src, cx, cy, cz, ab, diag, first, second):
    flags = place()
    even = flags[4] > 0
    for x in range(1, SIDE):
        g = diagonal(cx[x], cx[x - 1], cy[x], cz[x], ab[x])
        diag[x] = g
        top, bottom = strips(src[x], cx[x], cy[x], cz[x], g, True)
        at = (x - 1) % 8, pl.ds(12 * ((x - 1) // 8), 12)
        first[at] = jnp.where(even, top, bottom)
        second[at] = jnp.where(even, bottom, top)


def pack_outer(src, cx, cy, cz, ab, one, two, diag, first, second):
    flags = place()
    even = flags[4] > 0
    has_low, has_high = flags[0] > 0, flags[1] > 0
    low, high = sides(one, two, flags[5] > 0, has_low, has_high)
    layers = []
    for k in range(3):
        f = [low(UP_AT[n] + k) for n in range(5)]
        layers.append((f, low(3 + k), has_low, low(UP_AT[2]) if k == 1 else None))
    layers.append(([ref[0] for ref in (src, cx, cy, cz, ab)], low(6), True, None))
    for k in range(3):
        f = [high(3 * n + k) for n in range(5)]
        before = cx[15] if k == 0 else high(3 + k - 1)
        layers.append((f, before, has_high, high(8) if k == 1 else None))
    for k, (f, before, inside, beyond) in enumerate(layers):
        g = diagonal(f[1], before, *f[2:])
        diag[k] = g
        if 1 <= k < 6:
            top, bottom = strips(*f[:4], g, inside, beyond)
            at = (k - 1) % 3, pl.ds(12 * ((k - 1) // 3), 12)
            first[at] = jnp.where(even, top, bottom)
            second[at] = jnp.where(even, bottom, top)


def sides(one, two, even, has_low, has_high):
    keep_low, keep_high = has_low.astype(f32), has_high.astype(f32)

    def low(*at):
        return jnp.where(even, two[at], one[at]) * keep_low

    def high(*at):
        return jnp.where(even, one[at], two[at]) * keep_high

    return low, high


def near(i, u, cx, cy, cz):
    here = u[i]
    cy_i, cz_i = cy[i], cz[i]
    total = cx[i] * u[i + 1] + cx[i - 1] * u[i - 1]
    total = total + (cy_i * ahead(here, 0) + back(cy_i * here, 0))
    return total + (cz_i * ahead(here, 1) + back(cz_i * here, 1))


def join(layers):
    total = layers[0]
    for k, v in enumerate(layers[1:], 1):
        v = pltpu.roll(v, 64, 1) if k >= 2 else v
        total = total + (pltpu.roll(v, 4, 0) if k % 2 else v)
    return total


class Layers:
    def __init__(self, inner, outer=None):
        self.inner, self.outer = inner, outer

    def __getitem__(self, i):
        if 4 <= i < 19:
            return self.inner[i - 4]
        return self.outer[i if i < 4 else i - 15]

    def __setitem__(self, i, value):
        self.inner[i - 4] = value


class Over(dict):
    def __init__(self, inner, rows=None):
        self.inner, self.rows = inner, rows

    def __missing__(self, i):
        return self.inner[i - 4 if self.rows is None else self.rows[i]]


def own_layer(x, inner, outer, first, last, skip):
    return inner[x - first] if first <= x <= last else outer[x if x < first else x - skip]


def ring_layer(fields, g, lo, hi, hit, face=None):
    src_i, cx_i, cy_i, cz_i = fields
    row, lane = iota((RING, LONG), 0), iota((RING, LONG), 1)
    none1, none4 = jnp.zeros((1, LONG), f32), jnp.zeros((4, LONG), f32)

    def ring(own, n):
        return jnp.concatenate([own, hi[2 * n : 2 * n + 2], none4, lo[2 * n : 2 * n + 2]], axis=0)

    src_r, cx_r, cz_r, g = ring(src_i, 0), ring(cx_i, 1), ring(cz_i, 3), ring(g, 4)
    cy_r = jnp.concatenate([cy_i, hi[4:6], none1, none1, none1, lo[11:12], lo[4:6]], axis=0)
    if face is not None:
        cy_r = jnp.where(row == 23, face, cy_r)
    g = g + jnp.where((row == 0) | (row == 16), back(cy_r, 0), 0.0)
    inv = jnp.where(hit, 1.0 / g, 0.0)
    u = src_r * inv * (1.0 / FINE[0])
    u = jnp.where(row == 18, hi[10:11], u)
    u = jnp.where(row == 21, lo[10:11], u)
    return cx_r, cy_r, jnp.where(lane == LONG - 1, 0.0, cz_r), g, inv, src_r, u


def inside_ring(flags):
    row = iota((RING, LONG), 0)
    return (row < 16) | ((row < 18) & (flags[3] > 0)) | ((row >= 22) & (flags[2] > 0))


EDGE_ROWS = ((4, 5, 6, 16, 17, 18), (4, 5, 17, 18), (5, 6, 16, 17), (6, 7, 15, 16))
EDGES = [{i: k + sum(map(len, EDGE_ROWS[:n])) for k, i in enumerate(v)} for n, v in enumerate(EDGE_ROWS)]


def smooth_inner(
    src, cx, cy, cz, diag, one, two,
    cx_o, cy_o, cz_o, g_o, inv_o, edge, iterate, resid, u0, u1, u2, r,
):
    flags = place()
    center, m1, q1, m2, q2 = FINE
    left, right = sides(one, two, flags[4] > 0, flags[2] > 0, flags[3] > 0)
    hit = inside_ring(flags)
    made = [Layers(ref) for ref in (cx_o, cy_o, cz_o, g_o, inv_o, r, u0)]
    u1, u2 = Layers(u1), Layers(u2)
    for i in range(4, 19):
        x, at = i - 3, ((i - 4) % 8, pl.ds(12 * ((i - 4) // 8), 12))
        fields = src[x], cx[x], cy[x], cz[x]
        for out, value in zip(made, ring_layer(fields, diag[x], left(*at), right(*at), hit)):
            out[i] = value
    cx, cy, cz, g, inv, r, u0 = made
    for i in range(5, 18):
        u = u0[i]
        v = r[i] - (g[i] * u - near(i, u0, cx, cy, cz))
        r[i] = v
        u1[i] = m1 * u + q1 * (inv[i] * v)
    for i in range(6, 17):
        u = u1[i]
        v = r[i] - (g[i] * u - near(i, u1, cx, cy, cz))
        r[i] = v
        v = m2 * u + q2 * (inv[i] * v)
        u2[i] = v
        iterate[i - 6] = (u0[i] + u + v)[:SIDE]
    for values, rows in zip((r, u0, u1, u2), EDGES):
        for i, at in rows.items():
            edge[at] = values[i]
    for i in range(7, 16):
        resid[i - 7] = (r[i] - (g[i] * u2[i] - near(i, u2, cx, cy, cz)))[:SIDE]


def smooth_outer(
    src, cx, cy, cz, one_x, two_x, diag, one, two, coarse, active,
    cx_i, cy_i, cz_i, g_i, inv_i, edge, resid_i,
    cx_o, cy_o, cz_o, g_o, inv_o, iterate, resid, packed, weight, first, second,
):
    flags = place()
    center, m1, q1, m2, q2 = FINE
    has_low, has_high = flags[0] > 0, flags[1] > 0
    low, high = sides(one_x, two_x, flags[5] > 0, has_low, has_high)
    left, right = sides(one, two, flags[4] > 0, flags[2] > 0, flags[3] > 0)
    hit = inside_ring(flags)
    own_row = iota((RING, LONG), 0) < SIDE
    none12 = jnp.zeros((12, LONG), f32)
    layers = [([low(UP_AT[n] + k) for n in range(4)], has_low) for k in range(3)]
    layers.append(([ref[0] for ref in (src, cx, cy, cz)], True))
    layers += [([high(3 * n + k) for n in range(4)], has_high) for k in range(3)]
    made = [Over(ref) for ref in (cx_i, cy_i, cz_i, g_i, inv_i)]
    made += [Over(edge, EDGES[0]), Over(edge, EDGES[1])]
    for k, (fields, inside) in enumerate(layers):
        lo, hi, face = none12, none12, None
        if 1 <= k < 6:
            at = (k - 1) % 3, pl.ds(12 * ((k - 1) // 3), 12)
            lo, hi, here = left(*at), right(*at), hit & inside
        else:
            dst, at = (0, 0) if k == 0 else (1, 12)
            face, here = left(dst, pl.ds(at, 12))[11:12], hit & inside & own_row
        values = ring_layer(fields, diag[k], lo, hi, here, face)
        for out, value in zip(made, values):
            out[k if k < 4 else k + 15] = value
        for out, value in zip((cx_o, cy_o, cz_o, g_o, inv_o), values):
            out[k] = value
    cx, cy, cz, g, inv, r, u0 = made
    u1, u2 = Over(edge, EDGES[2]), Over(edge, EDGES[3])

    lanes, rows = sum_lanes(False), sum_rows(False)
    crow, clane = iota((8, 128), 0), iota((8, 128), 1)
    own = (crow < 4) & (clane < 64)
    mask = active[...]
    tails = [sum(cy[4 * a + 3 + k][SIDE:] for k in range(4)) for a in range(4)]
    below = by_right(jnp.concatenate([cx[2][:SIDE]] + tails, axis=0), lanes)
    below_x = by_left(rows, below[:SIDE])
    inverse, uppers, tiles = [], [], []
    for a in range(4):
        below_y = back(below[SIDE + 8 * a : SIDE + 8 * a + 8], 0)
        cx_c, cy_c, cz_c, ab_c = (coarse[n, a] for n in range(4))
        total = cx_c + cy_c + cz_c + ab_c + back(cz_c, 1)
        total = total + (below_x if a == 0 else coarse[0, a - 1])
        total = total + jnp.where(crow == 0, below_y, back(cy_c, 0))
        weight[a] = jnp.where(own, total, 0.0)
        inverse.append(jnp.where(own, mask / jnp.where(own, total, 1.0), 0.0))
        lower = cx_c + pltpu.roll(cy_c, 64, 1)
        tiles.append(pltpu.roll(inverse[a], 64, 1) + pltpu.roll(lower, 4, 0))
        uppers.append(jnp.where(clane == 63, 0.0, cz_c))
    packed[4] = join(uppers)

    for i in (1, 2, 3, 4, 18, 19, 20):
        v = r[i] - (g[i] * u0[i] - near(i, u0, cx, cy, cz))
        r[i] = v
        u1[i] = m1 * u0[i] + q1 * (inv[i] * v)
    for i in (2, 3, 4, 5, 17, 18, 19):
        v = r[i] - (g[i] * u1[i] - near(i, u1, cx, cy, cz))
        r[i] = v
        u2[i] = m2 * u1[i] + q2 * (inv[i] * v)
    for k, i in enumerate((3, 4, 5, 17, 18)):
        iterate[k] = (u0[i] + u1[i] + u2[i])[:SIDE]
    edges = {}
    for k, i in enumerate((3, 4, 5, 6, 16, 17, 18)):
        edges[i - 3] = (r[i] - (g[i] * u2[i] - near(i, u2, cx, cy, cz)))[:SIDE]
        resid[k] = edges[i - 3]
    even = flags[5] > 0
    rest = [edges[x] if x in edges else resid_i[x - 4] for x in range(SIDE)]
    totals = [(rest[x] + rest[x + 1]) + (rest[x + 2] + rest[x + 3]) for x in range(0, SIDE, 4)]

    for k in range(2):
        up, down = edges[14 + k], edges[k]
        for n in range(4):
            ys, zs = 8 * (n // 2), 128 * (n % 2)
            p, q = up[ys : ys + 8, zs : zs + 128], down[ys : ys + 8, zs : zs + 128]
            first[4 * k + n] = jnp.where(even, p, q)
            second[4 * k + n] = jnp.where(even, q, p)
    rhs = by_right(jnp.concatenate(totals, axis=0), lanes)
    for a in range(4):
        tiles[a] = tiles[a] + inverse[a] * by_left(rows, rhs[SIDE * a : SIDE * a + SIDE])
        packed[a] = tiles[a]
    ups, downs = tiles[1:4] + [join(uppers[1:4])], tiles[0:3] + [join(uppers[0:3])]
    for k, (p, q) in enumerate(zip(ups, downs)):
        first[8 + k] = jnp.where(even, p, q)
        second[8 + k] = jnp.where(even, q, p)


def residual_strips(layers, even, first, second, at):
    for c in range(2):
        parts = [layer[c] for layer in layers]
        bottom = jnp.concatenate([head for head, _ in parts], axis=0)
        top = jnp.concatenate([tail for _, tail in parts], axis=0)
        first[at + c] = jnp.where(even, top, bottom)
        second[at + c] = jnp.where(even, bottom, top)


def pack_own(resid_i, resid_o, packed, first, second):
    flags = place()
    def halves(x):
        mine = own_layer(x, resid_i, resid_o, 4, 12, 9)
        return [(mine[0:2, at : at + 128], mine[14:16, at : at + 128]) for at in (0, 128)]

    for n in range(4):
        residual_strips([halves(4 * n + k) for k in range(4)], flags[4] > 0, first, second, 2 * n)
    for k in range(5):
        first[8 + k] = packed[k]
        second[8 + k] = packed[k]


def pack_halo(one_x, two_x, first, second):
    flags = place()
    low, high = sides(one_x, two_x, flags[5] > 0, flags[0] > 0, flags[1] > 0)

    def halves(get, k):
        return [(get(4 * k + c)[0:2], get(4 * k + 2 + c)[6:8]) for c in range(2)]

    layers = [halves(low, 0), halves(low, 1), halves(high, 0), halves(high, 1)]
    residual_strips(layers, flags[4] > 0, first, second, 0)
    for k, get in enumerate((low, high)):
        for a in range(4):
            at = 2 + 3 * k + a if a < 3 else 8 + k
            tile = get(8 + a)
            first[at] = tile
            second[at] = tile


def krylov(packed, weight, one_x, two_x, one, two, one_out, two_out, basis, message, ext, t1s):
    flags = place()
    low, high = sides(one_x, two_x, flags[5] > 0, flags[0] > 0, flags[1] > 0)
    left, right = sides(one, two, flags[4] > 0, flags[2] > 0, flags[3] > 0)
    left_out, right_out = sides(one_out, two_out, flags[4] > 0, flags[2] > 0, flags[3] > 0)
    crow, clane = iota((8, 128), 0), iota((8, 128), 1)
    top, thin = crow < 4, clane < 64

    def tiles(own, out):
        return [out(2 + a) for a in range(3)] + [own(8 + a) for a in range(4)] + [
            out(5 + a) for a in range(3)
        ] + [out(8), own(12), out(9)]

    mine = [low(8 + a) for a in range(3)] + [packed[a] for a in range(4)]
    mine += [high(8 + a) for a in range(3)] + [low(11), packed[4], high(11)]
    previous, following = tiles(left, left_out), tiles(right, right_out)

    def upper(field, a):
        group, k = (0, a) if a < 3 else (1, a - 3) if a < 7 else (2, a - 7)
        tile = field[10 + group]
        return (pltpu.roll(tile, 64, 1) if k >= 2 else tile), k % 2

    def turn(tile):
        return pltpu.roll(tile, 4, 0)

    for a in range(10):
        here, after, before = mine[a], following[a], previous[a]
        pairs = (
            (jnp.where(top, here, turn(after)), jnp.where(top, turn(here), after)),
            (jnp.where(top, 0.0, turn(before)), jnp.where(top, 0.0, before)),
        )
        (here, odd), (after, _), (before, _) = (upper(f, a) for f in (mine, following, previous))
        if odd:
            faces = jnp.where(top, turn(here), after), jnp.where(top, 0.0, before)
        else:
            faces = jnp.where(top, here, turn(after)), jnp.where(top, 0.0, turn(before))
        for n in range(2):
            at = pl.ds(8 * n, 8)
            for m in range(2):
                ext[2 * m, a, at] = jnp.where(thin, pairs[n][m], 0.0)
                ext[2 * m + 1, a, at] = jnp.where(thin, pltpu.roll(pairs[n][m], 64, 1), 0.0)
            ext[4, a, at] = jnp.where(thin, faces[n], 0.0)

    z, inv, cx, cy, cz = (ext.at[n] for n in range(5))
    for a in range(1, 9):
        t1s[a] = z[a] - inv[a] * near(a, z, cx, cy, cz)
    for a in range(2, 8):
        t1 = t1s[a]
        basis[0, a - 2] = z[a]
        basis[1, a - 2] = t1
        basis[2, a - 2] = t1 - inv[a] * near(a, t1s, cx, cy, cz)

    def total(parts):
        return jnp.sum(sum(parts), keepdims=True)

    g = [weight[a] for a in range(4)]
    v0, v1, v2 = ([basis[n, a + 1, 0:8] for a in range(4)] for n in range(3))
    s00 = total([w * p * p for w, p in zip(g, v0)])
    s01 = total([w * p * q for w, p, q in zip(g, v0, v1)])
    alpha = jnp.where(s00 > 0, s01 / jnp.where(s00 > 0, s00, 1.0), 0.0)
    e = [q - alpha * p for p, q in zip(v0, v1)]
    te = [q - alpha * p for p, q in zip(v1, v2)]
    terms = [
        total([w * p * p for w, p in zip(g, e)]),
        2.0 * total([w * p * q for w, p, q in zip(g, e, v0)]),
        s00,
        total([w * p * q for w, p, q in zip(g, e, te)]),
        total([w * (p * q + r * t) for w, p, q, r, t in zip(g, v0, te, e, v1)]),
        s01,
    ]
    lane = iota((8, 128), 1)
    line = jnp.where(lane < 64, 0.0, alpha)
    for n, term in enumerate(terms):
        line = jnp.where(lane == n, term, line)
    message[...] = jnp.broadcast_to(line[0:1], (256, 128))


def finish(
    gathered, basis, cx_i, cy_i, cz_i, g_i, inv_i, cx_o, cy_o, cz_o, g_o, inv_o,
    resid_i, resid_o, iterate_i, iterate_o, one_x, two_x, one, two, one_out, two_out,
    out, correction,
):
    flags = place()
    center, m1, q1, m2, q2 = FINE
    low, high = sides(one_x, two_x, flags[5] > 0, flags[0] > 0, flags[1] > 0)
    left, right = sides(one, two, flags[4] > 0, flags[2] > 0, flags[3] > 0)

    pairs = (cx_i, cx_o), (cy_i, cy_o), (cz_i, cz_o), (g_i, g_o), (inv_i, inv_o)
    cx, cy, cz, g, inv = (Layers(*pair) for pair in pairs)

    lines = gathered[...]
    lane1 = iota((1, 128), 1)
    sums = jnp.sum(lines, axis=0, keepdims=True)

    def pick(values, first, count):
        hit = (lane1 >= first) & (lane1 < first + count)
        return jnp.sum(jnp.where(hit, values, 0.0), axis=1, keepdims=True)

    norm = pick(sums, 2, 1)
    a1 = pick(sums, 5, 1) / norm
    shift = pltpu.roll(lines, 64, 1) - a1
    plain, linear, quadratic = (((lane1 == k) | (lane1 == k + 3)).astype(f32) for k in range(3))
    power = plain + shift * (linear + shift * quadratic)
    sums = jnp.sum(lines * power, axis=0, keepdims=True)
    square, energy = pick(sums, 0, 3), pick(sums, 3, 3)
    bound = jnp.maximum(a1, energy / square) + jnp.sqrt(square / norm)
    middle, k1, h1, k2, h2 = factors(coarse_share, 1.0)
    scale = 1.0 / bound
    v0, h1, h2 = scale * (1.0 / middle), scale * h1, scale * h2
    v1 = (k1 * v0 + h1, -h1 * v0)
    v2 = (k2 * v1[0] + h2, k2 * v1[1] - h2 * (v0 + v1[0]), -h2 * v1[1])
    weights = (v0 + v1[0] + v2[0], v1[1] + v2[1], v2[2])

    upper = iota((8, 128), 0) < 4
    tall = []
    for a in range(6):
        field = weights[0] * basis[0, a] + weights[1] * basis[1, a] + weights[2] * basis[2, a]
        if 1 <= a <= 4:
            correction[a - 1] = field[0:4, 0:64]
        for p, q in ((0, 1), (2, 3), (4, 15)):
            p, q = (jnp.broadcast_to(field[k : k + 1], (8, 128)) for k in (p, q))
            tall.append(jnp.where(upper, p, q))
    lanes = (iota((128, LONG), 1) // 4 == iota((128, LONG), 0)).astype(bf16)
    fine = by_right(jnp.concatenate(tall, axis=0), lanes)
    lifted = [fine[RING * a : RING * a + RING] for a in range(6)]
    lift = [lifted[(i + 1) // 4] for i in range(ROWS)]

    none4 = jnp.zeros((4, LONG), f32)

    left_out, right_out = sides(one_out, two_out, flags[4] > 0, flags[2] > 0, flags[3] > 0)

    def strip(own, outer, x):
        get, n, k = (own, (x - 2) // 4, (x - 2) % 4) if 2 <= x < 18 else (outer, 0, x if x < 2 else x - 16)
        return jnp.concatenate([get(2 * n + c, pl.ds(2 * k, 2)) for c in range(2)], axis=1)

    def ring_of(i):
        x = i - 1
        if x < 2 or x >= 18:
            get, k = (low, x) if x < 2 else (high, x - 18)
            halves = [
                jnp.concatenate([get(4 * k + 2 * h + c) for c in range(2)], axis=1) for h in range(2)
            ]
            mine = jnp.concatenate(halves, axis=0)
        else:
            mine = own_layer(x - 2, resid_i, resid_o, 4, 12, 9)
        after, before = strip(right, right_out, x), strip(left, left_out, x)
        return jnp.concatenate([mine, after, none4, before], axis=0)

    r, u0, u1 = {}, {}, {}
    for k in range(1, ROWS + 1):
        if k < ROWS - 1:
            r[k] = ring_of(k) - (g[k] * lift[k] - near(k, lift, cx, cy, cz))
            u0[k] = inv[k] * r[k] * (1.0 / center)
        i = k - 1
        if 2 <= i < ROWS - 2:
            r[i] = r[i] - (g[i] * u0[i] - near(i, u0, cx, cy, cz))
            u1[i] = m1 * u0[i] + q1 * (inv[i] * r[i])
        i = k - 2
        if 3 <= i < 19:
            last = r[i] - (g[i] * u1[i] - near(i, u1, cx, cy, cz))
            step = (u0[i] + u1[i]) + (m2 * u1[i] + q2 * (inv[i] * last)) + lift[i]
            out[i - 3] = own_layer(i - 3, iterate_i, iterate_o, 3, 13, 11) + step[:SIDE]


def swap(values, axis, odd):
    count = lax.axis_size(axis)
    other = [(i ^ 1) if not odd else (((i + 1) ^ 1) - 1) % count for i in range(count)]
    return lax.ppermute(values, axis, list(enumerate(other)))


def body(src, cx, cy, cz, ab, active):
    count = lax.axis_size("coarse") * lax.axis_size("fine")
    block = (SIDE, SIDE, LONG)

    first, second = pack_first_call((src, cx, cy, cz, ab))
    one_x, two_x = swap(first, "coarse", False), swap(second, "coarse", True)
    coarse, mask = call(coarsen, [(4, 4, 8, 128), (8, 128)], ins=[VMEM] * 5)(cx, cy, cz, ab, active)
    diag, first, second = call(
        pack_inner, [block, (8, 24, LONG), (8, 24, LONG)], ins=[VMEM] * 5
    )(src, cx, cy, cz, ab)
    one, two = swap(first, "fine", False), swap(second, "fine", True)
    diag_out, first, second = call(
        pack_outer, [(7, SIDE, LONG), (3, 24, LONG), (3, 24, LONG)], ins=[VMEM] * 7
    )(src, cx, cy, cz, ab, one_x, two_x)
    one_out, two_out = swap(first, "fine", False), swap(second, "fine", True)
    inner, outer = (15, RING, LONG), (7, RING, LONG)
    *fields_i, edge, iterate_i, resid_i = call(
        smooth_inner,
        [inner] * 5 + [(18, RING, LONG), (11, SIDE, LONG), (9, SIDE, LONG)],
        [pltpu.VMEM(inner, f32)] * 4,
        ins=[VMEM] * 7,
    )(src, cx, cy, cz, diag, one, two)
    *fields_o, iterate_o, resid_o, packed, weight, first, second = call(
        smooth_outer,
        [outer] * 5 + [(5, SIDE, LONG), (7, SIDE, LONG)]
        + [(5, 8, 128), (4, 8, 128), (12, 8, 128), (12, 8, 128)],
        ins=[VMEM] * 18,
    )(
        src, cx, cy, cz, one_x, two_x, diag_out, one_out, two_out, coarse, mask,
        *fields_i, edge, resid_i,
    )
    one_x, two_x = swap(first, "coarse", False), swap(second, "coarse", True)
    first, second = call(pack_own, [(13, 8, 128)] * 2, ins=[VMEM] * 3)(
        resid_i, resid_o, packed
    )
    one, two = swap(first, "fine", False), swap(second, "fine", True)
    first, second = call(pack_halo, [(10, 8, 128)] * 2, ins=[VMEM] * 2)(one_x, two_x)
    one_out, two_out = swap(first, "fine", False), swap(second, "fine", True)
    basis, message = call(
        krylov,
        [(3, 6, 16, 128), (256, 128)],
        [pltpu.VMEM((5, 10, 16, 128), f32), pltpu.VMEM((10, 16, 128), f32)],
        ins=[VMEM] * 8,
    )(packed, weight, one_x, two_x, one, two, one_out, two_out)
    gathered = lax.all_to_all(message[:count], ("fine", "coarse"), 0, 0, tiled=True)
    out, correction = call(
        finish,
        [block, (4, 4, 64)],
        ins=[VMEM] * 22,
    )(
        gathered, basis, *fields_i, *fields_o, resid_i, resid_o, iterate_i, iterate_o,
        one_x, two_x, one, two, one_out, two_out,
    )
    return (out, correction)


def solution(mesh):
    spec = P("coarse", "fine", None)
    return jax.shard_map(
        body, mesh=mesh, in_specs=(spec,) * 6, out_specs=(spec,) * 2, check_vma=False
    )
```

```python
import jax
import jax.numpy as jnp
from jax import lax
from jax.experimental import pallas as pl
from jax.experimental.pallas import tpu as pltpu
from jax.sharding import PartitionSpec as P

f32 = jnp.float32
bf16 = jnp.bfloat16
fine_low = 0.25
fine_high = 2.0
coarse_share = 0.125
SIDE = 16
LONG = 256
ROWS = SIDE + 6
RING = 24
VMEM = pl.BlockSpec(memory_space=pltpu.VMEM)
LIMIT = 24 * 1024 * 1024


def factors(lower, upper):
    center = 0.5 * (upper + lower)
    radius = 0.5 * (upper - lower)
    aspect = center / radius
    p0 = 1.0 / aspect
    p1 = 1.0 / (2.0 * aspect - p0)
    p2 = 1.0 / (2.0 * aspect - p1)
    return center, p1 * p0, 2.0 * p1 / radius, p2 * p1, 2.0 * p2 / radius


FINE = factors(fine_low, fine_high)


def iota(shape, axis):
    return lax.broadcasted_iota(jnp.int32, shape, axis)


def back(values, axis):
    return pltpu.roll(values, 1, axis)


def ahead(values, axis):
    return pltpu.roll(values, values.shape[axis] - 1, axis)


def call(kernel, outs, scratch=(), ins=None):
    return pl.pallas_call(
        kernel,
        out_shape=[jax.ShapeDtypeStruct(s, f32) for s in outs],
        in_specs=ins,
        out_specs=[VMEM] * len(outs),
        scratch_shapes=list(scratch),
        compiler_params=pltpu.CompilerParams(vmem_limit_bytes=LIMIT),
    )


def place():
    ix, iy = lax.axis_index("coarse"), lax.axis_index("fine")
    nx, ny = lax.axis_size("coarse"), lax.axis_size("fine")
    return ix, nx - 1 - ix, iy, ny - 1 - iy, 1 - iy % 2, 1 - ix % 2


def pack_first(*refs):
    fields, pair, sems = refs[:5], refs[5:7], refs[7]
    even = lax.axis_index("coarse") % 2 == 0

    def fill(up, down):
        copies = []
        for n, field in enumerate(fields):
            first = 12 if n == 1 else 13
            at = UP_AT[n] + first - 13
            copies.append((field.at[first:16], up.at[at : at + 16 - first]))
            copies.append((field.at[0:3], down.at[3 * n : 3 * n + 3]))
        copies = [pltpu.make_async_copy(a, b, sems.at[k]) for k, (a, b) in enumerate(copies)]
        for copy in copies:
            copy.start()
        for copy in copies:
            copy.wait()

    @pl.when(even)
    def _():
        fill(*pair)

    @pl.when(jnp.logical_not(even))
    def _():
        fill(*pair[::-1])


def pack_first_call(fields):
    return pl.pallas_call(
        pack_first,
        out_shape=[jax.ShapeDtypeStruct((16, SIDE, LONG), f32)] * 2,
        in_specs=[pl.BlockSpec(memory_space=pltpu.HBM)] * 5,
        out_specs=[VMEM] * 2,
        scratch_shapes=[pltpu.SemaphoreType.DMA((10,))],
    )(*fields)


UP_AT = (0, 4, 7, 10, 13)


def sum_lanes(last_only):
    cell, lane = iota((LONG, 128), 0), iota((LONG, 128), 1)
    hit = cell // 4 == lane
    if last_only:
        hit = hit & (cell % 4 == 3)
    return hit.astype(bf16)


def sum_rows(last_only):
    block, cell = iota((8, SIDE), 0), iota((8, SIDE), 1)
    hit = cell // 4 == block
    if last_only:
        hit = hit & (cell % 4 == 3)
    return hit.astype(bf16)


def parts_of(values):
    first = values.astype(bf16)
    rest = values - first.astype(f32)
    second = rest.astype(bf16)
    return first, second, (rest - second.astype(f32)).astype(bf16)


def by_right(values, choose):
    return sum(jnp.dot(p, choose, preferred_element_type=f32) for p in parts_of(values))


def by_left(choose, values):
    return sum(jnp.dot(choose, p, preferred_element_type=f32) for p in parts_of(values))


def coarsen(cx, cy, cz, ab, active, out, mask):
    lanes, last = sum_lanes(False), sum_lanes(True)
    rows, lastrow = sum_rows(False), sum_rows(True)

    def coarse(n, part, left, right):
        total = by_right(jnp.concatenate([part(4 * a) for a in range(4)], axis=0), right)
        for a in range(4):
            out[n, a] = by_left(left, total[SIDE * a : SIDE * a + SIDE])

    def layers(ref):
        return lambda x: (ref[x] + ref[x + 1]) + (ref[x + 2] + ref[x + 3])

    coarse(0, lambda x: cx[x + 3], rows, lanes)
    coarse(1, layers(cy), lastrow, lanes)
    coarse(2, layers(cz), rows, last)
    coarse(3, layers(ab), rows, lanes)
    spread = ((iota((16, 128), 1) // 4) == iota((16, 128), 0)).astype(bf16)
    line = jnp.broadcast_to(active[0].astype(f32), (8, 16)).astype(bf16)
    mask[...] = jnp.dot(line, spread, preferred_element_type=f32)


def diagonal(cx_i, cxl_i, cy_i, cz_i, ab_i):
    row, lane = iota((SIDE, LONG), 0), iota((SIDE, LONG), 1)
    g = cx_i + cxl_i + cy_i + cz_i + ab_i
    g = g + jnp.where(row == 0, 0.0, back(cy_i, 0))
    return g + jnp.where(lane == 0, 0.0, back(cz_i, 1))


def strips(src_i, cx_i, cy_i, cz_i, g, inside, beyond=None):
    start = jnp.where(inside, src_i / (FINE[0] * g), 0.0)
    pieces = (src_i, cx_i, cy_i, cz_i, g)
    third = cy_i[13:14] if beyond is None else beyond[15:16]
    top = jnp.concatenate([p[14:16] for p in pieces] + [start[13:14], third], axis=0)
    bottom = jnp.concatenate([p[0:2] for p in pieces] + [start[2:3], start[2:3]], axis=0)
    return top, bottom


def pack_inner(src, cx, cy, cz, ab, diag, first, second):
    flags = place()
    even = flags[4] > 0
    for x in range(1, SIDE):
        g = diagonal(cx[x], cx[x - 1], cy[x], cz[x], ab[x])
        diag[x] = g
        top, bottom = strips(src[x], cx[x], cy[x], cz[x], g, True)
        at = (x - 1) % 8, pl.ds(12 * ((x - 1) // 8), 12)
        first[at] = jnp.where(even, top, bottom)
        second[at] = jnp.where(even, bottom, top)


def pack_outer(src, cx, cy, cz, ab, one, two, diag, first, second):
    flags = place()
    even = flags[4] > 0
    has_low, has_high = flags[0] > 0, flags[1] > 0
    low, high = sides(one, two, flags[5] > 0, has_low, has_high)
    layers = []
    for k in range(3):
        f = [low(UP_AT[n] + k) for n in range(5)]
        layers.append((f, low(3 + k), has_low, low(UP_AT[2]) if k == 1 else None))
    layers.append(([ref[0] for ref in (src, cx, cy, cz, ab)], low(6), True, None))
    for k in range(3):
        f = [high(3 * n + k) for n in range(5)]
        before = cx[15] if k == 0 else high(3 + k - 1)
        layers.append((f, before, has_high, high(8) if k == 1 else None))
    for k, (f, before, inside, beyond) in enumerate(layers):
        g = diagonal(f[1], before, *f[2:])
        diag[k] = g
        if 1 <= k < 6:
            top, bottom = strips(*f[:4], g, inside, beyond)
            at = (k - 1) % 3, pl.ds(12 * ((k - 1) // 3), 12)
            first[at] = jnp.where(even, top, bottom)
            second[at] = jnp.where(even, bottom, top)


def sides(one, two, even, has_low, has_high):
    keep_low, keep_high = has_low.astype(f32), has_high.astype(f32)

    def low(*at):
        return jnp.where(even, two[at], one[at]) * keep_low

    def high(*at):
        return jnp.where(even, one[at], two[at]) * keep_high

    return low, high


def near(i, u, cx, cy, cz):
    here = u[i]
    cy_i, cz_i = cy[i], cz[i]
    total = cx[i] * u[i + 1] + cx[i - 1] * u[i - 1]
    total = total + (cy_i * ahead(here, 0) + back(cy_i * here, 0))
    return total + (cz_i * ahead(here, 1) + back(cz_i * here, 1))


def join(layers):
    total = layers[0]
    for k, v in enumerate(layers[1:], 1):
        v = pltpu.roll(v, 64, 1) if k >= 2 else v
        total = total + (pltpu.roll(v, 4, 0) if k % 2 else v)
    return total


class Layers:
    def __init__(self, inner, outer=None):
        self.inner, self.outer = inner, outer

    def __getitem__(self, i):
        if 4 <= i < 19:
            return self.inner[i - 4]
        return self.outer[i if i < 4 else i - 15]

    def __setitem__(self, i, value):
        self.inner[i - 4] = value


class Over(dict):
    def __init__(self, inner, rows=None):
        self.inner, self.rows = inner, rows

    def __missing__(self, i):
        return self.inner[i - 4 if self.rows is None else self.rows[i]]


def own_layer(x, inner, outer, first, last, skip):
    return inner[x - first] if first <= x <= last else outer[x if x < first else x - skip]


def ring_layer(fields, g, lo, hi, hit, face=None):
    src_i, cx_i, cy_i, cz_i = fields
    row, lane = iota((RING, LONG), 0), iota((RING, LONG), 1)
    none1, none4 = jnp.zeros((1, LONG), f32), jnp.zeros((4, LONG), f32)

    def ring(own, n):
        return jnp.concatenate([own, hi[2 * n : 2 * n + 2], none4, lo[2 * n : 2 * n + 2]], axis=0)

    src_r, cx_r, cz_r, g = ring(src_i, 0), ring(cx_i, 1), ring(cz_i, 3), ring(g, 4)
    cy_r = jnp.concatenate([cy_i, hi[4:6], none1, none1, none1, lo[11:12], lo[4:6]], axis=0)
    if face is not None:
        cy_r = jnp.where(row == 23, face, cy_r)
    g = g + jnp.where((row == 0) | (row == 16), back(cy_r, 0), 0.0)
    inv = jnp.where(hit, 1.0 / g, 0.0)
    u = src_r * inv * (1.0 / FINE[0])
    u = jnp.where(row == 18, hi[10:11], u)
    u = jnp.where(row == 21, lo[10:11], u)
    return cx_r, cy_r, jnp.where(lane == LONG - 1, 0.0, cz_r), g, inv, src_r, u


def inside_ring(flags):
    row = iota((RING, LONG), 0)
    return (row < 16) | ((row < 18) & (flags[3] > 0)) | ((row >= 22) & (flags[2] > 0))


EDGE_ROWS = ((4, 5, 6, 16, 17, 18), (4, 5, 17, 18), (5, 6, 16, 17), (6, 7, 15, 16))
EDGES = [{i: k + sum(map(len, EDGE_ROWS[:n])) for k, i in enumerate(v)} for n, v in enumerate(EDGE_ROWS)]


def smooth_inner(
    src, cx, cy, cz, diag, one, two,
    cx_o, cy_o, cz_o, g_o, inv_o, edge, iterate, resid, rhs, u0, u1, u2, r,
):
    flags = place()
    center, m1, q1, m2, q2 = FINE
    left, right = sides(one, two, flags[4] > 0, flags[2] > 0, flags[3] > 0)
    hit = inside_ring(flags)
    made = [Layers(ref) for ref in (cx_o, cy_o, cz_o, g_o, inv_o, r, u0)]
    u1, u2 = Layers(u1), Layers(u2)
    for i in range(4, 19):
        x, at = i - 3, ((i - 4) % 8, pl.ds(12 * ((i - 4) // 8), 12))
        fields = src[x], cx[x], cy[x], cz[x]
        for out, value in zip(made, ring_layer(fields, diag[x], left(*at), right(*at), hit)):
            out[i] = value
    cx, cy, cz, g, inv, r, u0 = made
    for i in range(5, 18):
        u = u0[i]
        v = r[i] - (g[i] * u - near(i, u0, cx, cy, cz))
        r[i] = v
        u1[i] = m1 * u + q1 * (inv[i] * v)
    for i in range(6, 17):
        u = u1[i]
        v = r[i] - (g[i] * u - near(i, u1, cx, cy, cz))
        r[i] = v
        v = m2 * u + q2 * (inv[i] * v)
        u2[i] = v
        iterate[i - 6] = (u0[i] + u + v)[:SIDE]
    for values, rows in zip((r, u0, u1, u2), EDGES):
        for i, at in rows.items():
            edge[at] = values[i]
    made = [(r[i] - (g[i] * u2[i] - near(i, u2, cx, cy, cz)))[:SIDE] for i in range(7, 16)]
    for k, value in enumerate(made):
        resid[k] = value
    totals = [(made[k] + made[k + 1]) + (made[k + 2] + made[k + 3]) for k in (0, 4)]
    total = by_right(jnp.concatenate(totals, axis=0), sum_lanes(False))
    for k in range(2):
        rhs[k] = by_left(sum_rows(False), total[SIDE * k : SIDE * k + SIDE])


def smooth_outer(
    src, cx, cy, cz, one_x, two_x, diag, one, two, coarse, active,
    cx_i, cy_i, cz_i, g_i, inv_i, edge, resid_i, rhs_i,
    cx_o, cy_o, cz_o, g_o, inv_o, iterate, resid, packed, weight, first, second,
):
    flags = place()
    center, m1, q1, m2, q2 = FINE
    has_low, has_high = flags[0] > 0, flags[1] > 0
    low, high = sides(one_x, two_x, flags[5] > 0, has_low, has_high)
    left, right = sides(one, two, flags[4] > 0, flags[2] > 0, flags[3] > 0)
    hit = inside_ring(flags)
    own_row = iota((RING, LONG), 0) < SIDE
    none12 = jnp.zeros((12, LONG), f32)
    layers = [([low(UP_AT[n] + k) for n in range(4)], has_low) for k in range(3)]
    layers.append(([ref[0] for ref in (src, cx, cy, cz)], True))
    layers += [([high(3 * n + k) for n in range(4)], has_high) for k in range(3)]
    made = [Over(ref) for ref in (cx_i, cy_i, cz_i, g_i, inv_i)]
    made += [Over(edge, EDGES[0]), Over(edge, EDGES[1])]
    for k, (fields, inside) in enumerate(layers):
        lo, hi, face = none12, none12, None
        if 1 <= k < 6:
            at = (k - 1) % 3, pl.ds(12 * ((k - 1) // 3), 12)
            lo, hi, here = left(*at), right(*at), hit & inside
        else:
            dst, at = (0, 0) if k == 0 else (1, 12)
            face, here = left(dst, pl.ds(at, 12))[11:12], hit & inside & own_row
        values = ring_layer(fields, diag[k], lo, hi, here, face)
        for out, value in zip(made, values):
            out[k if k < 4 else k + 15] = value
        for out, value in zip((cx_o, cy_o, cz_o, g_o, inv_o), values):
            out[k] = value
    cx, cy, cz, g, inv, r, u0 = made
    u1, u2 = Over(edge, EDGES[2]), Over(edge, EDGES[3])

    lanes, rows = sum_lanes(False), sum_rows(False)
    crow, clane = iota((8, 128), 0), iota((8, 128), 1)
    own = (crow < 4) & (clane < 64)
    mask = active[...]
    tails = [sum(cy[4 * a + 3 + k][SIDE:] for k in range(4)) for a in range(4)]
    below = by_right(jnp.concatenate([cx[2][:SIDE]] + tails, axis=0), lanes)
    below_x = by_left(rows, below[:SIDE])
    inverse, uppers, tiles = [], [], []
    for a in range(4):
        below_y = back(below[SIDE + 8 * a : SIDE + 8 * a + 8], 0)
        cx_c, cy_c, cz_c, ab_c = (coarse[n, a] for n in range(4))
        total = cx_c + cy_c + cz_c + ab_c + back(cz_c, 1)
        total = total + (below_x if a == 0 else coarse[0, a - 1])
        total = total + jnp.where(crow == 0, below_y, back(cy_c, 0))
        weight[a] = jnp.where(own, total, 0.0)
        inverse.append(jnp.where(own, mask / jnp.where(own, total, 1.0), 0.0))
        lower = cx_c + pltpu.roll(cy_c, 64, 1)
        tiles.append(pltpu.roll(inverse[a], 64, 1) + pltpu.roll(lower, 4, 0))
        uppers.append(jnp.where(clane == 63, 0.0, cz_c))
    packed[4] = join(uppers)

    for i in (1, 2, 3, 4, 18, 19, 20):
        v = r[i] - (g[i] * u0[i] - near(i, u0, cx, cy, cz))
        r[i] = v
        u1[i] = m1 * u0[i] + q1 * (inv[i] * v)
    for i in (2, 3, 4, 5, 17, 18, 19):
        v = r[i] - (g[i] * u1[i] - near(i, u1, cx, cy, cz))
        r[i] = v
        u2[i] = m2 * u1[i] + q2 * (inv[i] * v)
    for k, i in enumerate((3, 4, 5, 17, 18)):
        iterate[k] = (u0[i] + u1[i] + u2[i])[:SIDE]
    edges = {}
    for k, i in enumerate((3, 4, 5, 6, 16, 17, 18)):
        edges[i - 3] = (r[i] - (g[i] * u2[i] - near(i, u2, cx, cy, cz)))[:SIDE]
        resid[k] = edges[i - 3]
    even = flags[5] > 0
    rest = [edges[x] if x in edges else resid_i[x - 4] for x in range(SIDE)]
    totals = [(rest[x] + rest[x + 1]) + (rest[x + 2] + rest[x + 3]) for x in (0, 12)]

    for k in range(2):
        up, down = edges[14 + k], edges[k]
        for n in range(4):
            ys, zs = 8 * (n // 2), 128 * (n % 2)
            p, q = up[ys : ys + 8, zs : zs + 128], down[ys : ys + 8, zs : zs + 128]
            first[4 * k + n] = jnp.where(even, p, q)
            second[4 * k + n] = jnp.where(even, q, p)
    rhs = by_right(jnp.concatenate(totals, axis=0), lanes)
    for a in range(4):
        if a in (1, 2):
            here = rhs_i[a - 1]
        else:
            at = 0 if a == 0 else SIDE
            here = by_left(rows, rhs[at : at + SIDE])
        tiles[a] = tiles[a] + inverse[a] * here
        packed[a] = tiles[a]
    ups, downs = tiles[1:4] + [join(uppers[1:4])], tiles[0:3] + [join(uppers[0:3])]
    for k, (p, q) in enumerate(zip(ups, downs)):
        first[8 + k] = jnp.where(even, p, q)
        second[8 + k] = jnp.where(even, q, p)


def residual_strips(layers, even, first, second, at):
    for c in range(2):
        parts = [layer[c] for layer in layers]
        bottom = jnp.concatenate([head for head, _ in parts], axis=0)
        top = jnp.concatenate([tail for _, tail in parts], axis=0)
        first[at + c] = jnp.where(even, top, bottom)
        second[at + c] = jnp.where(even, bottom, top)


def pack_own(resid_i, resid_o, packed, first, second):
    flags = place()
    def halves(x):
        mine = own_layer(x, resid_i, resid_o, 4, 12, 9)
        return [(mine[0:2, at : at + 128], mine[14:16, at : at + 128]) for at in (0, 128)]

    for n in range(4):
        residual_strips([halves(4 * n + k) for k in range(4)], flags[4] > 0, first, second, 2 * n)
    for k in range(5):
        first[8 + k] = packed[k]
        second[8 + k] = packed[k]


def pack_halo(one_x, two_x, first, second):
    flags = place()
    low, high = sides(one_x, two_x, flags[5] > 0, flags[0] > 0, flags[1] > 0)

    def halves(get, k):
        return [(get(4 * k + c)[0:2], get(4 * k + 2 + c)[6:8]) for c in range(2)]

    layers = [halves(low, 0), halves(low, 1), halves(high, 0), halves(high, 1)]
    residual_strips(layers, flags[4] > 0, first, second, 0)
    for k, get in enumerate((low, high)):
        for a in range(4):
            at = 2 + 3 * k + a if a < 3 else 8 + k
            tile = get(8 + a)
            first[at] = tile
            second[at] = tile


def krylov(packed, weight, one_x, two_x, one, two, one_out, two_out, basis, message, ext, t1s):
    flags = place()
    low, high = sides(one_x, two_x, flags[5] > 0, flags[0] > 0, flags[1] > 0)
    left, right = sides(one, two, flags[4] > 0, flags[2] > 0, flags[3] > 0)
    left_out, right_out = sides(one_out, two_out, flags[4] > 0, flags[2] > 0, flags[3] > 0)
    crow, clane = iota((8, 128), 0), iota((8, 128), 1)
    top, thin = crow < 4, clane < 64

    def tiles(own, out):
        return [out(2 + a) for a in range(3)] + [own(8 + a) for a in range(4)] + [
            out(5 + a) for a in range(3)
        ] + [out(8), own(12), out(9)]

    mine = [low(8 + a) for a in range(3)] + [packed[a] for a in range(4)]
    mine += [high(8 + a) for a in range(3)] + [low(11), packed[4], high(11)]
    previous, following = tiles(left, left_out), tiles(right, right_out)

    def upper(field, a):
        group, k = (0, a) if a < 3 else (1, a - 3) if a < 7 else (2, a - 7)
        tile = field[10 + group]
        return (pltpu.roll(tile, 64, 1) if k >= 2 else tile), k % 2

    def turn(tile):
        return pltpu.roll(tile, 4, 0)

    for a in range(10):
        here, after, before = mine[a], following[a], previous[a]
        pairs = (
            (jnp.where(top, here, turn(after)), jnp.where(top, turn(here), after)),
            (jnp.where(top, 0.0, turn(before)), jnp.where(top, 0.0, before)),
        )
        (here, odd), (after, _), (before, _) = (upper(f, a) for f in (mine, following, previous))
        if odd:
            faces = jnp.where(top, turn(here), after), jnp.where(top, 0.0, before)
        else:
            faces = jnp.where(top, here, turn(after)), jnp.where(top, 0.0, turn(before))
        for n in range(2):
            at = pl.ds(8 * n, 8)
            for m in range(2):
                ext[2 * m, a, at] = jnp.where(thin, pairs[n][m], 0.0)
                ext[2 * m + 1, a, at] = jnp.where(thin, pltpu.roll(pairs[n][m], 64, 1), 0.0)
            ext[4, a, at] = jnp.where(thin, faces[n], 0.0)

    z, inv, cx, cy, cz = (ext.at[n] for n in range(5))
    for a in range(1, 9):
        t1s[a] = z[a] - inv[a] * near(a, z, cx, cy, cz)
    for a in range(2, 8):
        t1 = t1s[a]
        basis[0, a - 2] = z[a]
        basis[1, a - 2] = t1
        basis[2, a - 2] = t1 - inv[a] * near(a, t1s, cx, cy, cz)

    def total(parts):
        return jnp.sum(sum(parts), keepdims=True)

    g = [weight[a] for a in range(4)]
    v0, v1, v2 = ([basis[n, a + 1, 0:8] for a in range(4)] for n in range(3))
    s00 = total([w * p * p for w, p in zip(g, v0)])
    s01 = total([w * p * q for w, p, q in zip(g, v0, v1)])
    alpha = jnp.where(s00 > 0, s01 / jnp.where(s00 > 0, s00, 1.0), 0.0)
    e = [q - alpha * p for p, q in zip(v0, v1)]
    te = [q - alpha * p for p, q in zip(v1, v2)]
    terms = [
        total([w * p * p for w, p in zip(g, e)]),
        2.0 * total([w * p * q for w, p, q in zip(g, e, v0)]),
        s00,
        total([w * p * q for w, p, q in zip(g, e, te)]),
        total([w * (p * q + r * t) for w, p, q, r, t in zip(g, v0, te, e, v1)]),
        s01,
    ]
    lane = iota((8, 128), 1)
    line = jnp.where(lane < 64, 0.0, alpha)
    for n, term in enumerate(terms):
        line = jnp.where(lane == n, term, line)
    message[...] = jnp.broadcast_to(line[0:1], (256, 128))


def finish(
    gathered, basis, cx_i, cy_i, cz_i, g_i, inv_i, cx_o, cy_o, cz_o, g_o, inv_o,
    resid_i, resid_o, iterate_i, iterate_o, one_x, two_x, one, two, one_out, two_out,
    out, correction,
):
    flags = place()
    center, m1, q1, m2, q2 = FINE
    low, high = sides(one_x, two_x, flags[5] > 0, flags[0] > 0, flags[1] > 0)
    left, right = sides(one, two, flags[4] > 0, flags[2] > 0, flags[3] > 0)

    pairs = (cx_i, cx_o), (cy_i, cy_o), (cz_i, cz_o), (g_i, g_o), (inv_i, inv_o)
    cx, cy, cz, g, inv = (Layers(*pair) for pair in pairs)

    lines = gathered[...]
    lane1 = iota((1, 128), 1)
    sums = jnp.sum(lines, axis=0, keepdims=True)

    def pick(values, first, count):
        hit = (lane1 >= first) & (lane1 < first + count)
        return jnp.sum(jnp.where(hit, values, 0.0), axis=1, keepdims=True)

    norm = pick(sums, 2, 1)
    a1 = pick(sums, 5, 1) / norm
    shift = pltpu.roll(lines, 64, 1) - a1
    plain, linear, quadratic = (((lane1 == k) | (lane1 == k + 3)).astype(f32) for k in range(3))
    power = plain + shift * (linear + shift * quadratic)
    sums = jnp.sum(lines * power, axis=0, keepdims=True)
    square, energy = pick(sums, 0, 3), pick(sums, 3, 3)
    bound = jnp.maximum(a1, energy / square) + jnp.sqrt(square / norm)
    middle, k1, h1, k2, h2 = factors(coarse_share, 1.0)
    scale = 1.0 / bound
    v0, h1, h2 = scale * (1.0 / middle), scale * h1, scale * h2
    v1 = (k1 * v0 + h1, -h1 * v0)
    v2 = (k2 * v1[0] + h2, k2 * v1[1] - h2 * (v0 + v1[0]), -h2 * v1[1])
    weights = (v0 + v1[0] + v2[0], v1[1] + v2[1], v2[2])

    upper = iota((8, 128), 0) < 4
    tall = []
    for a in range(6):
        field = weights[0] * basis[0, a] + weights[1] * basis[1, a] + weights[2] * basis[2, a]
        if 1 <= a <= 4:
            correction[a - 1] = field[0:4, 0:64]
        for p, q in ((0, 1), (2, 3), (4, 15)):
            p, q = (jnp.broadcast_to(field[k : k + 1], (8, 128)) for k in (p, q))
            tall.append(jnp.where(upper, p, q))
    lanes = (iota((128, LONG), 1) // 4 == iota((128, LONG), 0)).astype(bf16)
    fine = by_right(jnp.concatenate(tall, axis=0), lanes)
    lifted = [fine[RING * a : RING * a + RING] for a in range(6)]
    lift = [lifted[(i + 1) // 4] for i in range(ROWS)]

    none4 = jnp.zeros((4, LONG), f32)

    left_out, right_out = sides(one_out, two_out, flags[4] > 0, flags[2] > 0, flags[3] > 0)

    def strip(own, outer, x):
        get, n, k = (own, (x - 2) // 4, (x - 2) % 4) if 2 <= x < 18 else (outer, 0, x if x < 2 else x - 16)
        return jnp.concatenate([get(2 * n + c, pl.ds(2 * k, 2)) for c in range(2)], axis=1)

    def ring_of(i):
        x = i - 1
        if x < 2 or x >= 18:
            get, k = (low, x) if x < 2 else (high, x - 18)
            halves = [
                jnp.concatenate([get(4 * k + 2 * h + c) for c in range(2)], axis=1) for h in range(2)
            ]
            mine = jnp.concatenate(halves, axis=0)
        else:
            mine = own_layer(x - 2, resid_i, resid_o, 4, 12, 9)
        after, before = strip(right, right_out, x), strip(left, left_out, x)
        return jnp.concatenate([mine, after, none4, before], axis=0)

    r, u0, u1 = {}, {}, {}
    for k in range(1, ROWS + 1):
        if k < ROWS - 1:
            r[k] = ring_of(k) - (g[k] * lift[k] - near(k, lift, cx, cy, cz))
            u0[k] = inv[k] * r[k] * (1.0 / center)
        i = k - 1
        if 2 <= i < ROWS - 2:
            r[i] = r[i] - (g[i] * u0[i] - near(i, u0, cx, cy, cz))
            u1[i] = m1 * u0[i] + q1 * (inv[i] * r[i])
        i = k - 2
        if 3 <= i < 19:
            last = r[i] - (g[i] * u1[i] - near(i, u1, cx, cy, cz))
            step = (u0[i] + u1[i]) + (m2 * u1[i] + q2 * (inv[i] * last)) + lift[i]
            out[i - 3] = own_layer(i - 3, iterate_i, iterate_o, 3, 13, 11) + step[:SIDE]


def swap(values, axis, odd):
    count = lax.axis_size(axis)
    other = [(i ^ 1) if not odd else (((i + 1) ^ 1) - 1) % count for i in range(count)]
    return lax.ppermute(values, axis, list(enumerate(other)))


def body(src, cx, cy, cz, ab, active):
    count = lax.axis_size("coarse") * lax.axis_size("fine")
    block = (SIDE, SIDE, LONG)

    first, second = pack_first_call((src, cx, cy, cz, ab))
    one_x, two_x = swap(first, "coarse", False), swap(second, "coarse", True)
    coarse, mask = call(coarsen, [(4, 4, 8, 128), (8, 128)], ins=[VMEM] * 5)(cx, cy, cz, ab, active)
    diag, first, second = call(
        pack_inner, [block, (8, 24, LONG), (8, 24, LONG)], ins=[VMEM] * 5
    )(src, cx, cy, cz, ab)
    one, two = swap(first, "fine", False), swap(second, "fine", True)
    diag_out, first, second = call(
        pack_outer, [(7, SIDE, LONG), (3, 24, LONG), (3, 24, LONG)], ins=[VMEM] * 7
    )(src, cx, cy, cz, ab, one_x, two_x)
    one_out, two_out = swap(first, "fine", False), swap(second, "fine", True)
    inner, outer = (15, RING, LONG), (7, RING, LONG)
    *fields_i, edge, iterate_i, resid_i, rhs_i = call(
        smooth_inner,
        [inner] * 5 + [(18, RING, LONG), (11, SIDE, LONG), (9, SIDE, LONG), (2, 8, 128)],
        [pltpu.VMEM(inner, f32)] * 4,
        ins=[VMEM] * 7,
    )(src, cx, cy, cz, diag, one, two)
    *fields_o, iterate_o, resid_o, packed, weight, first, second = call(
        smooth_outer,
        [outer] * 5 + [(5, SIDE, LONG), (7, SIDE, LONG)]
        + [(5, 8, 128), (4, 8, 128), (12, 8, 128), (12, 8, 128)],
        ins=[VMEM] * 19,
    )(
        src, cx, cy, cz, one_x, two_x, diag_out, one_out, two_out, coarse, mask,
        *fields_i, edge, resid_i, rhs_i,
    )
    one_x, two_x = swap(first, "coarse", False), swap(second, "coarse", True)
    first, second = call(pack_own, [(13, 8, 128)] * 2, ins=[VMEM] * 3)(
        resid_i, resid_o, packed
    )
    one, two = swap(first, "fine", False), swap(second, "fine", True)
    first, second = call(pack_halo, [(10, 8, 128)] * 2, ins=[VMEM] * 2)(one_x, two_x)
    one_out, two_out = swap(first, "fine", False), swap(second, "fine", True)
    basis, message = call(
        krylov,
        [(3, 6, 16, 128), (256, 128)],
        [pltpu.VMEM((5, 10, 16, 128), f32), pltpu.VMEM((10, 16, 128), f32)],
        ins=[VMEM] * 8,
    )(packed, weight, one_x, two_x, one, two, one_out, two_out)
    gathered = lax.all_to_all(message[:count], ("fine", "coarse"), 0, 0, tiled=True)
    out, correction = call(
        finish,
        [block, (4, 4, 64)],
        ins=[VMEM] * 22,
    )(
        gathered, basis, *fields_i, *fields_o, resid_i, resid_o, iterate_i, iterate_o,
        one_x, two_x, one, two, one_out, two_out,
    )
    return (out, correction)


def solution(mesh):
    spec = P("coarse", "fine", None)
    return jax.shard_map(
        body, mesh=mesh, in_specs=(spec,) * 6, out_specs=(spec,) * 2, check_vma=False
    )
```
